32 devices in a mesh: prow: 8 (over y, x, core), pcol: 4 (over z).
Axes of the slice: x: 2, y: 2, z: 4, core: 2. Of those that a mesh axis runs over, the one named last changes fastest.
Arguments:
- matrix: bfloat16 [16384, 6144], P('prow', 'pcol')
- pivots: int32 [512], replicated, may hold values from 512 to 16383, as said below
- unit_inverse: bfloat16 [512, 512], replicated, as said below
Outputs:
- factored: bfloat16 [16384, 6144], P('prow', 'pcol')
The draws below stay inside these ranges and needn't reach their ends.
Inputs may be any that keep to these rules, and one draw needn't show every extreme that they name: pivots are distinct rows, none among the first 512. unit_inverse is unit lower triangular.
All inputs are finite; a program needn't handle non-finite values.
Results may differ from the reference program's by a relative error of at most 0.0041.
Values may be sent and summed in bfloat16 or wider, within the bound.
No kernel may reach another device: no remote copies, remote signals or barrier semaphores. Data moves between devices by JAX's collectives and lax.ppermute only.
A program may use at most 64 MiB of HBM per device.

```python
import jax
import jax.numpy as jnp
from jax import lax

NB = 512
N = 6144
ROWS_DEV = 2048
M = 16384
N_PROW = 8


def draw_matrix(key, part):
    values = jax.random.normal(key, (M, N), jnp.float32)
    column_scale = jnp.where(jnp.arange(N) < NB, NB ** (-0.5), 1.0)
    return (values * column_scale[None, :]).astype(jnp.bfloat16)


def draw_unit_inverse(key, part):
    values = jax.random.normal(key, (NB, NB), jnp.float32)
    lower = jnp.tril(values * NB ** (-0.5), -1)
    return (lower + jnp.eye(NB, dtype=jnp.float32)).astype(jnp.bfloat16)


def draw_pivots(key, part):
    key_weight = jax.random.fold_in(key, 11)
    key_score = jax.random.fold_in(key, 12)
    key_forced = jax.random.fold_in(key, 13)
    row_ids = jnp.arange(M, dtype=jnp.int32)
    weights = jax.random.randint(key_weight, (M // ROWS_DEV,), 1, 4)
    row_weight = weights[row_ids // ROWS_DEV]
    scores = jax.random.randint(key_score, (M,), 0, 1024) * row_weight
    owners = jnp.array([1, N_PROW // 2, N_PROW - 1], dtype=jnp.int32)
    offsets = jax.random.randint(key_forced, (3,), 0, ROWS_DEV)
    forced_rows = owners * ROWS_DEV + offsets
    forced = jnp.any(row_ids[:, None] == forced_rows[None, :], axis=1)
    scores = jnp.where(forced, 4096, scores)
    keyed = jnp.where(row_ids >= NB, scores * M + row_ids, -1 - row_ids)
    chosen = lax.top_k(keyed, NB)[1]
    return chosen.astype(jnp.int32)


def setup_inputs(seed: int = 0) -> dict:
    key_list = jax.random.split(jax.random.key(seed), 4)
    return {
        "matrix": draw_matrix(jax.random.fold_in(key_list[3], 71), 0),
        "pivots": draw_pivots(jax.random.fold_in(key_list[3], 71), 0),
        "unit_inverse": draw_unit_inverse(jax.random.fold_in(key_list[3], 71), 0),
    }


def reference(matrix, pivots, unit_inverse):
    count = unit_inverse.shape[0]
    total_rows = matrix.shape[0]
    leading = jnp.arange(count, dtype=jnp.int32)
    swapped = matrix.at[leading].set(matrix[pivots]).at[pivots].set(matrix[:count])
    upper = jnp.dot(unit_inverse, swapped[:count], preferred_element_type=jnp.float32).astype(jnp.bfloat16)
    blocks = swapped.reshape(N_PROW, total_rows // N_PROW, swapped.shape[1])
    factors = matrix[:, :count].reshape(N_PROW, total_rows // N_PROW, count)

    def update_block(pair):
        block, factor = pair
        return (block.astype(jnp.float32) - jnp.dot(factor, upper, preferred_element_type=jnp.float32)).astype(jnp.bfloat16)

    updated = lax.map(update_block, (blocks, factors)).reshape(total_rows, swapped.shape[1])
    updated = updated.at[:count].set(upper)
    return updated.at[:, :count].set(matrix[:, :count])
```

```python
import functools

import jax
import jax.numpy as jnp
from jax import lax
from jax.experimental import pallas as pl
from jax.experimental.pallas import tpu as pltpu
from jax.sharding import PartitionSpec as P

GROUPS = 4
VMEM_BYTES = 48 * 2**20


def pick_kernel(place_ref, pivots_ref, matrix_ref, out_ref, onehot_ref):
    rows = matrix_ref.shape[0]
    width = pivots_ref.shape[0]

    @pl.when(pl.program_id(0) == 0)
    def _():
        row = lax.broadcasted_iota(jnp.int32, (width, rows), 1) + place_ref[0] * rows
        onehot_ref[...] = jnp.where(pivots_ref[...] == row, 1.0, 0.0).astype(jnp.bfloat16)

    out_ref[:width] = jnp.dot(
        onehot_ref[...], matrix_ref[...], preferred_element_type=jnp.float32
    ).astype(jnp.bfloat16)
    first = matrix_ref[:width]
    out_ref[width:] = jnp.where(place_ref[0] == 0, first, jnp.zeros_like(first))


def pick(place, pivots, matrix):
    rows, cols = matrix.shape
    width = pivots.shape[0]
    block = 256
    return pl.pallas_call(
        pick_kernel,
        grid_spec=pltpu.PrefetchScalarGridSpec(
            num_scalar_prefetch=1,
            grid=(cols // block,),
            in_specs=[
                pl.BlockSpec((width, 1), lambda i, s: (0, 0)),
                pl.BlockSpec((rows, block), lambda i, s: (0, i)),
            ],
            out_specs=pl.BlockSpec((2 * width, block), lambda i, s: (0, i)),
            scratch_shapes=[pltpu.VMEM((width, rows), jnp.bfloat16)],
        ),
        out_shape=jax.ShapeDtypeStruct((2 * width, cols), jnp.bfloat16),
        compiler_params=pltpu.CompilerParams(vmem_limit_bytes=VMEM_BYTES),
        cost_estimate=pl.CostEstimate(
            flops=2 * width * rows * cols, bytes_accessed=2 * rows * cols, transcendentals=0
        ),
        name="pick_rows",
    )(place, pivots[:, None], matrix)


def update_kernel(first_row, pick_source, n_sources, place_ref, pivots_ref, matrix_ref,
                  displaced_ref, upper_ref, *rest):
    sources = rest[:n_sources]
    out_ref, factors_ref, sem = rest[-3:]
    step = pl.program_id(0)
    block = matrix_ref.shape[0]
    width = upper_ref.shape[0]
    group_rows = factors_ref.shape[0]
    row_place, col_place, rows = place_ref[0], place_ref[1], place_ref[2]

    @pl.when(step == 0)
    def _():
        for number, source in enumerate(sources):
            @pl.when(pick_source(col_place) == number)
            def _():
                view = source
                if number == 0:
                    view = source.at[pl.ds(first_row, group_rows), pl.ds(0, width)]
                copy = pltpu.make_async_copy(view, factors_ref, sem)
                copy.start()
                copy.wait()

    local = first_row + step * block
    row = lax.broadcasted_iota(jnp.int32, (block, width), 0) + row_place * rows + local
    match = pivots_ref[...] == row
    onehot = jnp.where(match, 1.0, 0.0)
    has_pivot = jnp.max(onehot, axis=1, keepdims=True) > 0.0
    moved = jnp.dot(onehot.astype(jnp.bfloat16), displaced_ref[...],
                    preferred_element_type=jnp.float32)
    factors = factors_ref[pl.ds(pl.multiple_of(step * block, block), block), :]
    product = jnp.dot(factors, upper_ref[...], preferred_element_type=jnp.float32)
    swapped = jnp.where(has_pivot, moved, matrix_ref[...].astype(jnp.float32))
    out_ref[...] = (swapped - product).astype(jnp.bfloat16)

    if first_row < width:
        @pl.when((row_place == 0) & (local < width))
        def _():
            start = pl.multiple_of(jnp.minimum(local, width - block), block)
            out_ref[...] = upper_ref[pl.ds(start, block), :]

    @pl.when(col_place == 0)
    def _():
        out_ref[:, :width] = matrix_ref[:, :width]


def update(first_row, group_rows, pick_source, place, pivots, matrix, displaced, upper,
           received, out):
    rows, cols = matrix.shape
    width = upper.shape[0]
    block = 256
    offset = first_row // block
    sources = [matrix] + list(received)
    whole = lambda i, s: (0, 0)
    in_specs = [
        pl.BlockSpec((1, width), whole),
        pl.BlockSpec((block, cols), lambda i, s: (i + offset, 0)),
        pl.BlockSpec((width, cols), whole),
        pl.BlockSpec((width, cols), whole),
    ] + [pl.BlockSpec(memory_space=pl.ANY)] * len(sources)
    operands = [place, pivots[None, :], matrix, displaced, upper] + sources
    aliases = {}
    if out is not None:
        in_specs.append(pl.BlockSpec(memory_space=pl.ANY))
        aliases = {len(operands): 0}
        operands.append(out)
    return pl.pallas_call(
        functools.partial(update_kernel, first_row, pick_source, len(sources)),
        grid_spec=pltpu.PrefetchScalarGridSpec(
            num_scalar_prefetch=1,
            grid=(group_rows // block,),
            in_specs=in_specs,
            out_specs=pl.BlockSpec((block, cols), lambda i, s: (i + offset, 0)),
            scratch_shapes=[
                pltpu.VMEM((group_rows, width), jnp.bfloat16),
                pltpu.SemaphoreType.DMA,
            ],
        ),
        out_shape=jax.ShapeDtypeStruct((rows, cols), jnp.bfloat16),
        input_output_aliases=aliases,
        compiler_params=pltpu.CompilerParams(vmem_limit_bytes=VMEM_BYTES),
        cost_estimate=pl.CostEstimate(
            flops=4 * group_rows * width * cols,
            bytes_accessed=4 * group_rows * cols + 4 * width * cols,
            transcendentals=0,
        ),
        name="update_rows",
    )(*operands)


def reduce_scatter(value, axis, size, bits):
    place = lax.axis_index(axis)
    for bit in bits:
        pairs = [(i, i ^ (1 << bit)) for i in range(size)]
        half = value.shape[0] // 2
        mine = (place >> bit) & 1
        sent = lax.dynamic_slice_in_dim(value, (1 - mine) * half, half, 0)
        kept = lax.dynamic_slice_in_dim(value, mine * half, half, 0)
        value = kept + lax.ppermute(sent, axis, pairs)
    return value


def all_gather(value, axis, size, bits):
    place = lax.axis_index(axis)
    for bit in reversed(bits):
        pairs = [(i, i ^ (1 << bit)) for i in range(size)]
        other = lax.ppermute(value, axis, pairs)
        mine = (place >> bit) & 1
        both = jnp.concatenate([value, other, value], axis=0)
        value = lax.dynamic_slice_in_dim(both, mine * value.shape[0], 2 * value.shape[0], 0)
    return value


def sum_rows(value, axis, size):
    count = size.bit_length() - 1
    inner = list(range(1, count))
    part = reduce_scatter(value, axis, size, [0])
    half = part.shape[0] // 2
    parts = []
    for piece, bits in ((part[:half], inner), (part[half:], inner[::-1])):
        piece = reduce_scatter(piece, axis, size, bits)
        parts.append(all_gather(piece, axis, size, bits))
    return all_gather(jnp.concatenate(parts, axis=0), axis, size, [0])


def spread(panel, axis, size):
    middle = size // 2
    received = [lax.ppermute(panel, axis, [(0, middle)])]
    if middle > 1:
        received.append(lax.ppermute(received[0], axis, [(middle, middle - 1)]))
    if middle + 1 < size:
        received.append(lax.ppermute(received[0], axis, [(middle, middle + 1)]))
    distance = 1
    held = None
    while middle - distance > 1 or middle + distance + 1 < size:
        held = received[1] + received[2] if held is None else held
        pairs = []
        if middle - distance > 1:
            pairs.append((middle - distance, middle - distance - 1))
        if middle + distance + 1 < size:
            pairs.append((middle + distance, middle + distance + 1))
        held = lax.ppermute(held, axis, pairs)
        received.append(held)
        distance += 1
    return received


def source_of(size):
    middle = size // 2

    def pick_source(place):
        away = jnp.abs(place - middle)
        number = jnp.where(away >= 2, away + 1, jnp.where(place < middle, 1, 2) + 1)
        number = jnp.where(away == 0, 1, jnp.where(away == 1, number, away + 2))
        return jnp.where(place == 0, 0, number)

    return pick_source


def per_device(n_prow, n_pcol, matrix, pivots, unit_inverse):
    rows, cols = matrix.shape
    width = unit_inverse.shape[0]
    row_place = lax.axis_index("prow")
    col_place = lax.axis_index("pcol")
    place = jnp.stack([row_place, col_place, jnp.full_like(row_place, rows)]).astype(jnp.int32)
    group_rows = rows // GROUPS
    received = []
    for group in range(GROUPS):
        start = group * group_rows
        received.append(spread(matrix[start : start + group_rows, :width], "pcol", n_pcol))
    picked = pick(place, pivots, matrix)
    summed = sum_rows(picked, "prow", n_prow)
    full_rows, displaced = summed[:width], summed[width:]
    upper = jnp.dot(unit_inverse, full_rows, preferred_element_type=jnp.float32).astype(
        jnp.bfloat16
    )
    out = None
    for group in range(GROUPS):
        out = update(group * group_rows, group_rows, source_of(n_pcol), place, pivots, matrix,
                     displaced, upper, received[group], out)
    return out


def solution(mesh):
    return jax.shard_map(
        functools.partial(per_device, mesh.shape["prow"], mesh.shape["pcol"]),
        mesh=mesh,
        in_specs=(P("prow", "pcol"), P(), P()),
        out_specs=P("prow", "pcol"),
        check_vma=False,
    )
```

```python
import functools

import jax
import jax.numpy as jnp
from jax import lax
from jax.experimental import pallas as pl
from jax.experimental.pallas import tpu as pltpu
from jax.sharding import PartitionSpec as P

GROUPS = 4
BLOCK = 512
F32, BF16 = jnp.float32, jnp.bfloat16
VMEM = pl.BlockSpec(memory_space=pltpu.VMEM)
ANY = pl.BlockSpec(memory_space=pl.ANY)
SMALL = pltpu.CompilerParams(vmem_limit_bytes=8 * 2**20)
LARGE = pltpu.CompilerParams(vmem_limit_bytes=28 * 2**20)


def cost(flops, moved):
    return pl.CostEstimate(flops=flops, bytes_accessed=moved, transcendentals=0)


def chunk_kernel(first_row, matrix_ref, out_ref, sem):
    rows, width = out_ref.shape
    copy = pltpu.make_async_copy(
        matrix_ref.at[pl.ds(first_row, rows), pl.ds(0, width)], out_ref, sem
    )
    copy.start()
    copy.wait()


def chunk(matrix, first_row, rows, width):
    return pl.pallas_call(
        functools.partial(chunk_kernel, first_row),
        in_specs=[pl.BlockSpec(memory_space=pltpu.HBM)],
        out_specs=ANY,
        out_shape=jax.ShapeDtypeStruct((rows, width), BF16),
        scratch_shapes=[pltpu.SemaphoreType.DMA],
        compiler_params=SMALL,
        cost_estimate=cost(0, 4 * rows * width),
        name="chunk",
    )(matrix)


def pick_kernel(place_ref, pivots_ref, matrix_ref, keep_ref, send_ref, onehot_ref):
    rows = matrix_ref.shape[0]
    width = pivots_ref.shape[0]
    half = width // 2

    @pl.when(pl.program_id(0) == 0)
    def _():
        row = lax.broadcasted_iota(jnp.int32, (width, rows), 1) + place_ref[0] * rows
        onehot_ref[...] = jnp.where(pivots_ref[...] == row, 1.0, 0.0).astype(BF16)

    block = matrix_ref[...]
    send_ref[...] = jnp.dot(onehot_ref[half:], block, preferred_element_type=F32).astype(BF16)
    keep_ref[...] = jnp.dot(onehot_ref[:half], block, preferred_element_type=F32).astype(BF16)


def pick(place, pivots, matrix):
    rows, cols = matrix.shape
    width = pivots.shape[0]
    block = min(BLOCK, cols)
    half = jax.ShapeDtypeStruct((width // 2, cols), BF16)
    return pl.pallas_call(
        pick_kernel,
        grid_spec=pltpu.PrefetchScalarGridSpec(
            num_scalar_prefetch=1,
            grid=(cols // block,),
            in_specs=[
                pl.BlockSpec((width, 1), lambda i, s: (0, 0)),
                pl.BlockSpec((rows, block), lambda i, s: (0, i)),
            ],
            out_specs=[pl.BlockSpec((width // 2, block), lambda i, s: (0, i))] * 2,
            scratch_shapes=[pltpu.VMEM((width, rows), BF16)],
        ),
        out_shape=[half, half],
        compiler_params=LARGE,
        cost_estimate=cost(2 * width * rows * cols, 2 * rows * cols),
        name="pick_rows",
    )(place, pivots[:, None], matrix)


def split_sum_kernel(own_ref, got_ref, *rest):
    first_ref, second_ref = rest[-2:]
    half = first_ref.shape[0]
    first_ref[...] = own_ref[:half] + got_ref[:half]
    second_ref[...] = own_ref[half:] + got_ref[half:]


def split_sum(own, got, after):
    half = jax.ShapeDtypeStruct((own.shape[0] // 2, own.shape[1]), BF16)
    return pl.pallas_call(
        split_sum_kernel,
        in_specs=[VMEM, VMEM] + [ANY] * len(after),
        out_specs=[VMEM, VMEM],
        out_shape=[half, half],
        compiler_params=SMALL,
        cost_estimate=cost(own.size, 6 * own.size),
        name="split_sum",
    )(own, got, *after)


def stack_sum_kernel(count, *refs):
    out_ref = refs[-1]
    start = 0
    for own_ref, got_ref in zip(refs[:count], refs[count : 2 * count]):
        rows = own_ref.shape[0]
        out_ref[start : start + rows] = own_ref[...] + got_ref[...]
        start += rows


def stack_sum(own, got, after):
    rows = sum(x.shape[0] for x in own)
    cols = own[0].shape[1]
    return pl.pallas_call(
        functools.partial(stack_sum_kernel, len(own)),
        in_specs=[VMEM] * (2 * len(own)) + [ANY] * len(after),
        out_specs=VMEM,
        out_shape=jax.ShapeDtypeStruct((rows, cols), BF16),
        compiler_params=SMALL,
        cost_estimate=cost(rows * cols, 6 * rows * cols),
        name="stack_sum",
    )(*own, *got, *after)


def merge_kernel(first_ref, first_got_ref, second_ref, second_got_ref, *rest):
    out_ref = rest[-1]
    rows = first_ref.shape[0] // 2
    for number, (own_ref, got_ref) in enumerate(
        ((first_ref, first_got_ref), (second_ref, second_got_ref))
    ):
        for part in range(2):
            start = (2 * part + number) * rows
            piece = slice(part * rows, (part + 1) * rows)
            out_ref[start : start + rows] = own_ref[piece] + got_ref[piece]


def merge(first, first_got, second, second_got, after):
    rows, cols = 2 * first.shape[0], first.shape[1]
    return pl.pallas_call(
        merge_kernel,
        in_specs=[VMEM] * 4 + [ANY] * len(after),
        out_specs=VMEM,
        out_shape=jax.ShapeDtypeStruct((rows, cols), BF16),
        compiler_params=SMALL,
        cost_estimate=cost(rows * cols, 6 * rows * cols),
        name="merge",
    )(first, first_got, second, second_got, *after)


def update_kernel(groups, group_rows, per_group, pick_source, make_upper, *refs):
    place_ref, pivots_ref, matrix_ref, mine_ref, other_ref, factor_ref = refs[:6]
    sources = refs[6 : 6 + 1 + per_group * len(groups)]
    if make_upper:
        out_ref, upper_ref = refs[-6:-4]
    else:
        out_ref, upper_ref = refs[-5], factor_ref
    onehot_ref, keep_ref, panel_ref, sem = refs[-4:]
    step = pl.program_id(0)
    width = panel_ref.shape[1]
    half = width // 2
    block = out_ref.shape[1]
    row_place, col_place, rows, core = (place_ref[i] for i in range(4))
    first_row = groups[0] * group_rows

    def fetch(action):
        for number, group in enumerate(groups):
            here = panel_ref.at[pl.ds(number * group_rows, group_rows)]
            views = [sources[0].at[pl.ds(group * group_rows, group_rows), pl.ds(0, width)]]
            views += sources[1 + number * per_group : 1 + (number + 1) * per_group]
            for choice, view in enumerate(views):
                @pl.when(pick_source(col_place) == choice)
                def _():
                    action(pltpu.make_async_copy(view, here, sem.at[number]))

    @pl.when(step == 0)
    def _():
        fetch(lambda copy: copy.start())
        for number in range(len(groups)):
            here = slice(number * group_rows, (number + 1) * group_rows)
            row = lax.broadcasted_iota(jnp.int32, (group_rows, width), 0)
            row = row + (row_place * rows + first_row + number * group_rows)
            onehot = jnp.where(pivots_ref[...] == row, 1.0, 0.0)
            onehot_ref[here] = onehot.astype(BF16)
            has_pivot = jnp.max(onehot, axis=1, keepdims=True)
            keep_ref[here] = jnp.broadcast_to(1.0 - has_pivot, (group_rows, 128))

    def in_order(start):
        mine, other = mine_ref[start : start + half], other_ref[start : start + half]
        return jnp.where(core == 0, mine, other), jnp.where(core == 0, other, mine)

    if make_upper:
        top, bottom = in_order(0)
        upper_ref[...] = (
            jnp.dot(factor_ref[:, :half], top, preferred_element_type=F32)
            + jnp.dot(factor_ref[:, half:], bottom, preferred_element_type=F32)
        ).astype(BF16)

    @pl.when(step == 0)
    def _():
        fetch(lambda copy: copy.wait())

    in_panel = (col_place == 0) & (step * block < width)

    @pl.when(in_panel)
    def _():
        out_ref[...] = matrix_ref[...]

    @pl.when(jnp.logical_not(in_panel))
    def _():
        upper = upper_ref[...]
        top, bottom = in_order(half)
        for number, group in enumerate(groups):
            here = slice(number * group_rows, (number + 1) * group_rows)
            keep = jnp.concatenate([keep_ref[here]] * (block // 128), axis=1)
            moved = jnp.dot(onehot_ref[here, :half], top, preferred_element_type=F32)
            moved += jnp.dot(onehot_ref[here, half:], bottom, preferred_element_type=F32)
            product = jnp.dot(panel_ref[here], upper, preferred_element_type=F32)
            swapped = matrix_ref[here].astype(F32) * keep + moved
            out_ref[here] = (swapped - product).astype(BF16)
        if first_row < width:
            @pl.when(row_place == 0)
            def _():
                out_ref[: width - first_row] = upper[first_row:]


def update(groups, group_rows, pick_source, place, pivots, matrix, mine, other, received,
           unit_inverse=None, upper=None, out=None):
    rows, cols = matrix.shape
    width = mine.shape[0]
    block = min(BLOCK, cols)
    count = group_rows * len(groups)
    position = groups[0] // len(groups)
    make_upper = upper is None
    by_column = pl.BlockSpec((width, block), lambda i, s: (0, i))
    in_specs = [
        pl.BlockSpec((1, width), lambda i, s: (0, 0)),
        pl.BlockSpec((count, block), lambda i, s: (position, i)),
        by_column,
        by_column,
        pl.BlockSpec((width, width), lambda i, s: (0, 0)) if make_upper else by_column,
    ]
    sources = [matrix] + [x for group in groups for x in received[group]]
    in_specs += [ANY] * len(sources)
    operands = [place, pivots[None, :], matrix, mine, other]
    operands += [unit_inverse if make_upper else upper] + sources
    aliases = {}
    if out is not None:
        in_specs.append(ANY)
        aliases = {len(operands): 0}
        operands.append(out)
    out_specs = [pl.BlockSpec((count, block), lambda i, s: (position, i))]
    out_shape = [jax.ShapeDtypeStruct((rows, cols), BF16)]
    if make_upper:
        out_specs.append(by_column)
        out_shape.append(jax.ShapeDtypeStruct((width, cols), BF16))
    return pl.pallas_call(
        functools.partial(
            update_kernel, groups, group_rows, len(received[0]), pick_source, make_upper
        ),
        grid_spec=pltpu.PrefetchScalarGridSpec(
            num_scalar_prefetch=1,
            grid=(cols // block,),
            in_specs=in_specs,
            out_specs=out_specs,
            scratch_shapes=[
                pltpu.VMEM((count, width), BF16),
                pltpu.VMEM((count, 128), F32),
                pltpu.VMEM((count, width), BF16),
                pltpu.SemaphoreType.DMA((len(groups),)),
            ],
        ),
        out_shape=out_shape,
        input_output_aliases=aliases,
        compiler_params=LARGE,
        cost_estimate=cost(4 * count * width * cols, 4 * count * cols + 4 * width * cols),
        name="update_rows",
    )(*operands)


def swap_pairs(size, bit):
    return [(i, i ^ (1 << bit)) for i in range(size)]


def grow_pairs(bits_so_far, bit):
    places = [0]
    for b in bits_so_far:
        places += [i | (1 << b) for i in places]
    return [(i, i | (1 << bit)) for i in places]


def spread(panel, axis, size):
    middle = size // 2
    received = [lax.ppermute(panel, axis, [(0, middle)])]
    received.append(lax.ppermute(received[0], axis, [(middle, middle - 1)]))
    received.append(lax.ppermute(received[0], axis, [(middle, middle + 1)]))
    held = received[1] + received[2] if size > 4 else None
    distance = 1
    while middle - distance > 1 or middle + distance + 1 < size:
        pairs = []
        if middle - distance > 1:
            pairs.append((middle - distance, middle - distance - 1))
        if middle + distance + 1 < size:
            pairs.append((middle + distance, middle + distance + 1))
        held = lax.ppermute(held, axis, pairs)
        received.append(held)
        distance += 1
    return received


def source_of(size):
    middle = size // 2

    def pick_source(place):
        away = jnp.abs(place - middle)
        number = jnp.where(away == 0, 1, jnp.where(place < middle, 2, 3))
        number = jnp.where(away >= 2, away + 2, number)
        return jnp.where(place == 0, 0, number)

    return pick_source


def per_device(n_prow, n_pcol, matrix, pivots, unit_inverse):
    rows, cols = matrix.shape
    width = unit_inverse.shape[0]
    half, quarter = width // 2, width // 4
    row_place = lax.axis_index("prow")
    col_place = lax.axis_index("pcol")
    core = row_place & 1
    place = jnp.stack([row_place, col_place, jnp.full_like(row_place, rows), core])
    place = place.astype(jnp.int32)
    group_rows = rows // GROUPS
    bits = list(range(1, n_prow.bit_length() - 1))

    received = []
    for group in range(GROUPS):
        panel = chunk(matrix, group * group_rows, group_rows, width)
        received.append(spread(panel, "pcol", n_pcol))

    got = lax.ppermute(matrix[half:width], "prow", [(0, 1)])
    down = [
        jnp.where(row_place == 0, matrix[:quarter], got[:quarter]),
        jnp.where(row_place == 0, matrix[quarter:half], got[quarter:]),
    ]
    order = jnp.where(core == 0, pivots, jnp.roll(pivots, half))
    keep, send = pick(place, order, matrix)
    up = split_sum(keep, lax.ppermute(send, "prow", swap_pairs(n_prow, 0)), received[0][:1])

    orders = [bits, bits[::-1]]
    for number in range(len(bits) - 1):
        up_got = [
            lax.ppermute(x, "prow", swap_pairs(n_prow, b[number])) for x, b in zip(up, orders)
        ]
        down_got = [
            lax.ppermute(x, "prow", grow_pairs([0] + b[:number], b[number]))
            for x, b in zip(down, orders)
        ]
        if number < len(bits) - 2:
            up = [x + y for x, y in zip(up, up_got)]
            down = [x + y for x, y in zip(down, down_got)]
    after = received[0][1:3] + received[1][:1]
    both = [
        stack_sum([u, d], [ug, dg], after)
        for u, ug, d, dg in zip(up, up_got, down, down_got)
    ]
    both_got = [
        lax.ppermute(x, "prow", swap_pairs(n_prow, b[-1])) for x, b in zip(both, orders)
    ]
    after = received[1][1:3] + received[2][:1]
    mine = merge(both[0], both_got[0], both[1], both_got[1], after)
    other = lax.ppermute(mine, "prow", swap_pairs(n_prow, 0))

    common = (group_rows, source_of(n_pcol), place, pivots, matrix, mine, other, received)
    out, upper = update(list(range(GROUPS - 1)), *common, unit_inverse=unit_inverse)
    (out,) = update([GROUPS - 1], *common, upper=upper, out=out)
    return out


def solution(mesh):
    return jax.shard_map(
        functools.partial(per_device, mesh.shape["prow"], mesh.shape["pcol"]),
        mesh=mesh,
        in_specs=(P("prow", "pcol"), P(), P()),
        out_specs=P("prow", "pcol"),
        check_vma=False,
    )
```

```python
import functools

import jax
import jax.numpy as jnp
from jax import lax
from jax.experimental import pallas as pl
from jax.experimental.pallas import tpu as pltpu
from jax.sharding import PartitionSpec as P

GROUPS = 4
PARTS = 2
BLOCK = 512
F32, BF16 = jnp.float32, jnp.bfloat16
VMEM = pl.BlockSpec(memory_space=pltpu.VMEM)
ANY = pl.BlockSpec(memory_space=pl.ANY)
SMEM = pl.BlockSpec(memory_space=pltpu.SMEM)
SMALL = pltpu.CompilerParams(vmem_limit_bytes=8 * 2**20)
LARGE = pltpu.CompilerParams(vmem_limit_bytes=28 * 2**20)


def cost(flops, moved):
    return pl.CostEstimate(flops=flops, bytes_accessed=moved, transcendentals=0)


def chunk_kernel(first_row, axis, place_ref, matrix_ref, *refs):
    out_ref, sem = refs[-2:]
    rows, width = out_ref.shape

    @pl.when(place_ref[axis] == 0)
    def _():
        copy = pltpu.make_async_copy(
            matrix_ref.at[pl.ds(first_row, rows), pl.ds(0, width)], out_ref, sem
        )
        copy.start()
        copy.wait()


def chunk(place, axis, matrix, first_row, rows, width, held=None):
    in_specs, operands = [SMEM, ANY], [place, matrix]
    if held is not None:
        in_specs.append(ANY)
        operands.append(held)
    return pl.pallas_call(
        functools.partial(chunk_kernel, first_row, axis),
        in_specs=in_specs,
        out_specs=ANY,
        out_shape=jax.ShapeDtypeStruct((rows, width), BF16),
        scratch_shapes=[pltpu.SemaphoreType.DMA],
        input_output_aliases={} if held is None else {2: 0},
        compiler_params=SMALL,
        cost_estimate=cost(0, 4 * rows * width),
        name="chunk",
    )(*operands)


def pick_kernel(place_ref, pivots_ref, matrix_ref, *refs):
    onehot_ref = refs[PARTS * 2]
    rows = matrix_ref.shape[0]
    width = pivots_ref.shape[0]
    count = width // (2 * PARTS)

    @pl.when(pl.program_id(0) == 0)
    def _():
        row = lax.broadcasted_iota(jnp.int32, (width, rows), 1) + place_ref[0] * rows
        onehot_ref[...] = jnp.where(pivots_ref[...] == row, 1.0, 0.0).astype(BF16)

    picked = jnp.dot(onehot_ref[...], matrix_ref[...], preferred_element_type=F32).astype(BF16)
    for number, out_ref in enumerate(refs[: PARTS * 2]):
        out_ref[...] = picked[number * count : (number + 1) * count]


def pick(place, pivots, matrix):
    rows, cols = matrix.shape
    width = pivots.shape[0]
    block = min(BLOCK, cols)
    count = width // (2 * PARTS)
    return pl.pallas_call(
        pick_kernel,
        grid_spec=pltpu.PrefetchScalarGridSpec(
            num_scalar_prefetch=1,
            grid=(cols // block,),
            in_specs=[
                pl.BlockSpec((width, 1), lambda i, s: (0, 0)),
                pl.BlockSpec((rows, block), lambda i, s: (0, i)),
            ],
            out_specs=[pl.BlockSpec((count, block), lambda i, s: (0, i))] * (2 * PARTS),
            scratch_shapes=[pltpu.VMEM((width, rows), BF16)],
        ),
        out_shape=[jax.ShapeDtypeStruct((count, cols), BF16)] * (2 * PARTS),
        compiler_params=LARGE,
        cost_estimate=cost(2 * width * rows * cols, 2 * rows * cols),
        name="pick_rows",
    )(place, pivots[:, None], matrix)


def add_kernel(count, *refs):
    for own_ref, got_ref, out_ref in zip(refs[:count], refs[count:], refs[-count:]):
        out_ref[...] = own_ref[...] + got_ref[...]


def add(own, got, after=()):
    size = sum(x.size for x in own)
    return pl.pallas_call(
        functools.partial(add_kernel, len(own)),
        in_specs=[VMEM] * (2 * len(own)) + [ANY] * len(after),
        out_specs=[VMEM] * len(own),
        out_shape=[jax.ShapeDtypeStruct(x.shape, BF16) for x in own],
        compiler_params=SMALL,
        cost_estimate=cost(size, 6 * size),
        name="add",
    )(*own, *got, *after)


def exchange(parts, pairs):
    return [lax.ppermute(x, "prow", pairs) for x in parts]


def swap_kernel(place_ref, pivots_ref, matrix_ref, mine_ref, other_ref, *rest):
    out_ref, token_ref, onehot_ref, keep_ref = rest[-4:]
    token_ref[...] = jnp.zeros_like(token_ref)
    step = pl.program_id(0)
    rows, block = matrix_ref.shape
    width = pivots_ref.shape[1]
    half = width // 2
    row_place, col_place, core = (place_ref[i] for i in range(3))
    piece = min(rows, 512)

    @pl.when(step == 0)
    def _():
        for start in range(0, rows, piece):
            here = slice(start, start + piece)
            row = lax.broadcasted_iota(jnp.int32, (piece, width), 0) + row_place * rows + start
            onehot = jnp.where(pivots_ref[...] == row, 1.0, 0.0)
            onehot_ref[here] = onehot.astype(BF16)
            has_pivot = jnp.max(onehot, axis=1, keepdims=True)
            keep_ref[here] = jnp.broadcast_to(1.0 - has_pivot, (piece, 128))

    in_panel = (col_place == 0) & (step * block < width)

    @pl.when(in_panel)
    def _():
        out_ref[...] = matrix_ref[...]

    @pl.when(jnp.logical_not(in_panel))
    def _():
        mine, other = mine_ref[...], other_ref[...]
        top, bottom = jnp.where(core == 0, mine, other), jnp.where(core == 0, other, mine)
        for start in range(0, rows, piece):
            here = slice(start, start + piece)
            keep = jnp.concatenate([keep_ref[here]] * (block // 128), axis=1)
            moved = jnp.dot(onehot_ref[here, :half], top, preferred_element_type=F32)
            moved += jnp.dot(onehot_ref[here, half:], bottom, preferred_element_type=F32)
            out_ref[here] = (matrix_ref[here].astype(F32) * keep + moved).astype(BF16)


def swap(place, pivots, matrix, mine, other, after=()):
    rows, cols = matrix.shape
    width = pivots.shape[0]
    block = min(BLOCK, cols)
    by_column = pl.BlockSpec((rows, block), lambda i, s: (0, i))
    half_by_column = pl.BlockSpec((width // 2, block), lambda i, s: (0, i))
    return pl.pallas_call(
        swap_kernel,
        grid_spec=pltpu.PrefetchScalarGridSpec(
            num_scalar_prefetch=1,
            grid=(cols // block,),
            in_specs=[
                pl.BlockSpec((1, width), lambda i, s: (0, 0)),
                by_column,
                half_by_column,
                half_by_column,
            ]
            + [ANY] * len(after),
            out_specs=[by_column, pl.BlockSpec((8, 128), lambda i, s: (0, 0))],
            scratch_shapes=[pltpu.VMEM((rows, width), BF16), pltpu.VMEM((rows, 128), F32)],
        ),
        out_shape=[
            jax.ShapeDtypeStruct((rows, cols), BF16),
            jax.ShapeDtypeStruct((8, 128), F32),
        ],
        compiler_params=LARGE,
        cost_estimate=cost(2 * rows * width * cols, 4 * rows * cols),
        name="swap_rows",
    )(place, pivots[None, :], matrix, mine, other, *after)


def upper_kernel(place_ref, inverse_ref, *refs):
    mine_refs, other_refs, out_ref = refs[:PARTS], refs[PARTS : 2 * PARTS], refs[-1]
    width, cols = out_ref.shape
    count = width // (2 * PARTS)
    block = min(BLOCK, cols)
    for start in range(0, cols, block):
        here = slice(start, start + block)
        first = place_ref[2] == 0
        total = None
        for number in range(2 * PARTS):
            part = number % PARTS
            mine, other = mine_refs[part][:, here], other_refs[part][:, here]
            rows = jnp.where(first == (number < PARTS), mine, other)
            inverse = inverse_ref[:, number * count : (number + 1) * count]
            term = jnp.dot(inverse, rows, preferred_element_type=F32)
            total = term if total is None else total + term
        out_ref[:, here] = total.astype(BF16)


def upper_rows(place, unit_inverse, mine, other, after=()):
    width, cols = unit_inverse.shape[0], mine[0].shape[1]
    return pl.pallas_call(
        upper_kernel,
        in_specs=[SMEM] + [VMEM] * (1 + 2 * PARTS) + [ANY] * len(after),
        out_specs=VMEM,
        out_shape=jax.ShapeDtypeStruct((width, cols), BF16),
        compiler_params=pltpu.CompilerParams(vmem_limit_bytes=16 * 2**20),
        cost_estimate=cost(2 * width * width * cols, 4 * width * cols),
        name="upper",
    )(place, unit_inverse, *mine, *other, *after)


def update_kernel(groups, per_group, pick_source, place_ref, swapped_ref, upper_ref, *refs):
    sources = refs[: 1 + per_group * len(groups)]
    out_ref, panel_ref, sem = refs[-3:]
    step = pl.program_id(0)
    width = panel_ref.shape[1]
    block = out_ref.shape[1]
    row_place, col_place = place_ref[0], place_ref[1]
    first_row = groups[0][0]

    def fetch(number, action):
        start, count = groups[number]
        here = panel_ref.at[pl.ds(start - first_row, count)]
        views = [sources[0].at[pl.ds(start, count), pl.ds(0, width)]]
        views += sources[1 + number * per_group : 1 + (number + 1) * per_group]
        for choice, view in enumerate(views):
            @pl.when(pick_source(col_place) == choice)
            def _():
                action(pltpu.make_async_copy(view, here, sem.at[number]))

    @pl.when(step == 0)
    def _():
        for number in range(len(groups)):
            fetch(number, lambda copy: copy.start())
        for number in range(len(groups)):
            fetch(number, lambda copy: copy.wait())

    in_panel = (col_place == 0) & (step * block < width)

    @pl.when(in_panel)
    def _():
        out_ref[...] = swapped_ref[...]

    @pl.when(jnp.logical_not(in_panel))
    def _():
        upper = upper_ref[...]
        for start, count in groups:
            here = slice(start - first_row, start - first_row + count)
            product = jnp.dot(panel_ref[here], upper, preferred_element_type=F32)
            out_ref[here] = (swapped_ref[here].astype(F32) - product).astype(BF16)
        if first_row < width:
            @pl.when(row_place == 0)
            def _():
                out_ref[: width - first_row] = upper[first_row:]


def update(groups, pick_source, place, matrix, swapped, upper, received):
    rows, cols = matrix.shape
    width = upper.shape[0]
    block = min(BLOCK, cols)
    count = sum(size for _, size in groups)
    position = groups[0][0] // count
    by_column = pl.BlockSpec((count, block), lambda i, s: (position, i))
    sources = [matrix] + [x for group in received for x in group]
    return pl.pallas_call(
        functools.partial(update_kernel, groups, len(received[0]), pick_source),
        grid_spec=pltpu.PrefetchScalarGridSpec(
            num_scalar_prefetch=1,
            grid=(cols // block,),
            in_specs=[by_column, pl.BlockSpec((width, block), lambda i, s: (0, i))]
            + [ANY] * len(sources),
            out_specs=by_column,
            scratch_shapes=[
                pltpu.VMEM((count, width), BF16),
                pltpu.SemaphoreType.DMA((len(groups),)),
            ],
        ),
        out_shape=jax.ShapeDtypeStruct((rows, cols), BF16),
        input_output_aliases={1: 0},
        compiler_params=LARGE,
        cost_estimate=cost(2 * count * width * cols, 4 * count * cols),
        name="update_rows",
    )(place, swapped, upper, *sources)


def swap_pairs(size, orders, step):
    return [(i, i ^ (1 << orders[i & 1][step])) for i in range(size)]


def grow_pairs(orders, step):
    pairs = []
    for core, order in enumerate(orders):
        places = [core]
        for bit in order[:step]:
            places += [i | (1 << bit) for i in places]
        pairs += [(i, i | (1 << order[step])) for i in places]
    return pairs


def spread(place, matrix, width, groups, axis, size):
    middle = size // 2
    count = len(groups)
    held = []
    for number in range(count + 2):
        pairs = [(middle, middle - 1)]
        back = held[number - 2] if number >= 2 else None
        if number < count:
            pairs = [(0, middle)] + pairs * (number >= 2)
            sent = chunk(place, 1, matrix, *groups[number], width, back)
            if number >= 2:
                held[number - 2] = sent
        else:
            sent = back
        held.append(lax.ppermute(sent, axis, pairs))
    received = []
    for number in range(count):
        arrays = [held[number], held[number + 2]]
        arrays.append(lax.ppermute(held[number], axis, [(middle, middle + 1)]))
        distance = 1
        while middle - distance > 1 or middle + distance + 1 < size:
            if distance == 1:
                both = jnp.where(lax.axis_index(axis) < middle, arrays[1], arrays[2])
            pairs = []
            if middle - distance > 1:
                pairs.append((middle - distance, middle - distance - 1))
            if middle + distance + 1 < size:
                pairs.append((middle + distance, middle + distance + 1))
            both = lax.ppermute(both, axis, pairs)
            arrays.append(both)
            distance += 1
        received.append(arrays)
    return received


def source_of(size):
    middle = size // 2

    def pick_source(place):
        away = jnp.abs(place - middle)
        number = jnp.where(away == 0, 1, jnp.where(place < middle, 2, 3))
        number = jnp.where(away >= 2, away + 2, number)
        return jnp.where(place == 0, 0, number)

    return pick_source


def per_device(n_prow, n_pcol, matrix, pivots, unit_inverse):
    rows, cols = matrix.shape
    width = unit_inverse.shape[0]
    half = width // 2
    row_place = lax.axis_index("prow")
    col_place = lax.axis_index("pcol")
    core = row_place & 1
    place = jnp.stack([row_place, col_place, core]).astype(jnp.int32)
    matrix = pltpu.with_memory_space_constraint(matrix, pltpu.HBM)
    bits = list(range(1, n_prow.bit_length() - 1))
    orders = (bits, bits[::-1])
    cores = ([0], [0])
    last = len(bits) - 1

    size = rows // GROUPS
    groups = [(number * size, size) for number in range(GROUPS)]
    received = spread(place, matrix, width, groups, "pcol", n_pcol)
    arrived = [arrays[0] for arrays in received]
    arrived_left = [arrays[1] for arrays in received]
    arrived_right = [arrays[2] for arrays in received]

    order = jnp.where(core == 0, pivots, jnp.roll(pivots, half))
    down_got = lax.ppermute(chunk(place, 0, matrix, half, half, cols), "prow", [(0, 1)])
    picked = pick(place, order, matrix)
    up = picked[:PARTS]
    up_got = exchange(picked[PARTS:], swap_pairs(n_prow, cores, 0))
    down = chunk(place, 0, matrix, 0, half, cols, down_got)
    for step in range(last + 1):
        down_got = lax.ppermute(down, "prow", grow_pairs(orders, step))
        up = add(up, up_got, arrived[:1] if step == 0 else arrived[1:2] + arrived_right[:1])
        up_got = exchange(up, swap_pairs(n_prow, orders, step))
        (down,) = add([down], [down_got], up[-1:])
    down_got = lax.ppermute(down, "prow", swap_pairs(n_prow, cores, 0))
    swapped, token = swap(place, pivots, matrix, down, down_got, arrived[2:3])
    up = add(up, up_got, [token] + arrived_right[1:2])
    up_got = exchange(up, swap_pairs(n_prow, cores, 0))
    upper = upper_rows(place, unit_inverse, up, up_got, arrived[3:4])

    common = (source_of(n_pcol), place, matrix)
    out = update(groups[:-1], *common, swapped, upper, received[:-1])
    return update(groups[-1:], *common, out, upper, received[-1:])


def solution(mesh):
    return jax.shard_map(
        functools.partial(per_device, mesh.shape["prow"], mesh.shape["pcol"]),
        mesh=mesh,
        in_specs=(P("prow", "pcol"), P(), P()),
        out_specs=P("prow", "pcol"),
        check_vma=False,
    )
```

```python
import functools

import jax
import jax.numpy as jnp
from jax import lax
from jax.experimental import pallas as pl
from jax.experimental.pallas import tpu as pltpu
from jax.sharding import PartitionSpec as P

GROUPS = 2
CHUNK_WEIGHTS = (5, 5)
JOIN_WEIGHTS, JOIN_AFTER = (2, 2), ((0, 0), (3, 1))
DOWN_WEIGHTS, DOWN_AFTER = (0, 20), ((1, 0), (0, 0))
PIECES = 2
BLOCK = 512
F32, BF16 = jnp.float32, jnp.bfloat16
VMEM = pl.BlockSpec(memory_space=pltpu.VMEM)
ANY = pl.BlockSpec(memory_space=pl.ANY)
SMEM = pl.BlockSpec(memory_space=pltpu.SMEM)
SMALL = pltpu.CompilerParams(vmem_limit_bytes=8 * 2**20)
LARGE = pltpu.CompilerParams(vmem_limit_bytes=28 * 2**20)


FREE = pl.CostEstimate(flops=0, bytes_accessed=0, transcendentals=0)
def weight_of(x):
    x = float(x)
    return pl.CostEstimate(flops=int(x*1.15e9), bytes_accessed=int(x*3.69e6), transcendentals=0)


def chunk_kernel(first_row, axis, core, place_ref, matrix_ref, *refs):
    out_ref, sem = refs[-2:]
    rows, width = out_ref.shape

    @pl.when((place_ref[axis] == 0) & (place_ref[2] == core))
    def _():
        copy = pltpu.make_async_copy(
            matrix_ref.at[pl.ds(first_row, rows), pl.ds(0, width)], out_ref, sem
        )
        copy.start()
        copy.wait()


def chunk(place, axis, core, matrix, first_row, rows, width, held=None, weight=0, after=()):
    in_specs, operands = [SMEM, ANY], [place, matrix]
    if held is not None:
        in_specs.append(ANY)
        operands.append(held)
    in_specs += [ANY] * len(after)
    operands += after
    return pl.pallas_call(
        functools.partial(chunk_kernel, first_row, axis, core),
        in_specs=in_specs,
        out_specs=ANY,
        out_shape=jax.ShapeDtypeStruct((rows, width), BF16),
        scratch_shapes=[pltpu.SemaphoreType.DMA],
        input_output_aliases={} if held is None else {2: 0},
        compiler_params=SMALL,
        cost_estimate=weight_of(weight),
        name="chunk",
    )(*operands)


def pick_kernel(place_ref, pivots_ref, matrix_ref, *refs):
    onehot_ref = refs[-1]
    rows = matrix_ref.shape[0]
    width = pivots_ref.shape[0]
    count = width // PIECES

    @pl.when(pl.program_id(0) == 0)
    def _():
        row = lax.broadcasted_iota(jnp.int32, (width, rows), 1) + place_ref[0] * rows
        onehot_ref[...] = jnp.where(pivots_ref[...] == row, 1.0, 0.0).astype(BF16)

    picked = jnp.dot(onehot_ref[...], matrix_ref[...], preferred_element_type=F32).astype(BF16)
    for number, out_ref in enumerate(refs[:PIECES]):
        out_ref[...] = picked[number * count : (number + 1) * count]


def pick(place, pivots, matrix):
    rows, cols = matrix.shape
    width = pivots.shape[0]
    block = min(BLOCK, cols)
    count = width // PIECES
    return pl.pallas_call(
        pick_kernel,
        grid_spec=pltpu.PrefetchScalarGridSpec(
            num_scalar_prefetch=1,
            grid=(cols // block,),
            in_specs=[
                pl.BlockSpec((width, 1), lambda i, s: (0, 0)),
                pl.BlockSpec((rows, block), lambda i, s: (0, i)),
            ],
            out_specs=[pl.BlockSpec((count, block), lambda i, s: (0, i))] * PIECES,
            scratch_shapes=[pltpu.VMEM((width, rows), BF16)],
        ),
        out_shape=[jax.ShapeDtypeStruct((count, cols), BF16)] * PIECES,
        compiler_params=LARGE,
        cost_estimate=weight_of(0),
        name="pick_rows",
    )(place, pivots[:, None], matrix)


def add_kernel(count, *refs):
    start = 0
    out_ref = refs[-1]
    for own_ref, got_ref in zip(refs[:count], refs[count : 2 * count]):
        rows = own_ref.shape[0]
        out_ref[start : start + rows] = own_ref[...] + got_ref[...]
        start += rows


def add(own, got, after=(), weight=0):
    rows, cols = sum(x.shape[0] for x in own), own[0].shape[1]
    return pl.pallas_call(
        functools.partial(add_kernel, len(own)),
        in_specs=[VMEM] * (2 * len(own)) + [ANY] * len(after),
        out_specs=VMEM,
        out_shape=jax.ShapeDtypeStruct((rows, cols), BF16),
        compiler_params=SMALL,
        cost_estimate=weight_of(weight),
        name="add",
    )(*own, *got, *after)


def swap_kernel(place_ref, pivots_ref, matrix_ref, mine_ref, other_ref, *rest):
    out_ref, token_ref, onehot_ref, keep_ref = rest[-4:]
    token_ref[...] = jnp.zeros_like(token_ref)
    step = pl.program_id(0)
    rows, block = matrix_ref.shape
    width = pivots_ref.shape[1]
    half = width // 2
    row_place, col_place, core = (place_ref[i] for i in range(3))
    piece = min(rows, 512)

    @pl.when(step == 0)
    def _():
        for start in range(0, rows, piece):
            here = slice(start, start + piece)
            row = lax.broadcasted_iota(jnp.int32, (piece, width), 0) + row_place * rows + start
            onehot = jnp.where(pivots_ref[...] == row, 1.0, 0.0)
            onehot_ref[here] = onehot.astype(BF16)
            has_pivot = jnp.max(onehot, axis=1, keepdims=True)
            keep_ref[here] = jnp.broadcast_to(1.0 - has_pivot, (piece, 128))

    in_panel = (col_place == 0) & (step * block < width)

    @pl.when(in_panel)
    def _():
        out_ref[...] = matrix_ref[...]

    @pl.when(jnp.logical_not(in_panel))
    def _():
        mine, other = mine_ref[...], other_ref[...]
        top, bottom = jnp.where(core == 0, mine, other), jnp.where(core == 0, other, mine)
        for start in range(0, rows, piece):
            here = slice(start, start + piece)
            keep = jnp.concatenate([keep_ref[here]] * (block // 128), axis=1)
            moved = jnp.dot(onehot_ref[here, :half], top, preferred_element_type=F32)
            moved += jnp.dot(onehot_ref[here, half:], bottom, preferred_element_type=F32)
            out_ref[here] = (matrix_ref[here].astype(F32) * keep + moved).astype(BF16)


def swap(place, pivots, matrix, mine, other, after=()):
    rows, cols = matrix.shape
    width = pivots.shape[0]
    block = min(BLOCK, cols)
    by_column = pl.BlockSpec((rows, block), lambda i, s: (0, i))
    half_by_column = pl.BlockSpec((width // 2, block), lambda i, s: (0, i))
    return pl.pallas_call(
        swap_kernel,
        grid_spec=pltpu.PrefetchScalarGridSpec(
            num_scalar_prefetch=1,
            grid=(cols // block,),
            in_specs=[
                pl.BlockSpec((1, width), lambda i, s: (0, 0)),
                by_column,
                half_by_column,
                half_by_column,
            ]
            + [ANY] * len(after),
            out_specs=[by_column, pl.BlockSpec((8, 128), lambda i, s: (0, 0))],
            scratch_shapes=[pltpu.VMEM((rows, width), BF16), pltpu.VMEM((rows, 128), F32)],
        ),
        out_shape=[
            jax.ShapeDtypeStruct((rows, cols), BF16),
            jax.ShapeDtypeStruct((8, 128), F32),
        ],
        compiler_params=LARGE,
        cost_estimate=weight_of(0),
        name="swap_rows",
    )(place, pivots[None, :], matrix, mine, other, *after)


def upper_kernel(place_ref, inverse_ref, mine_ref, other_ref, *rest):
    out_ref = rest[-1]
    width, cols = out_ref.shape
    half = width // 2
    block = min(BLOCK, cols)
    for start in range(0, cols, block):
        here = slice(start, start + block)
        mine, other = mine_ref[:, here], other_ref[:, here]
        first = place_ref[2] == 0
        top, bottom = jnp.where(first, mine, other), jnp.where(first, other, mine)
        out_ref[:, here] = (
            jnp.dot(inverse_ref[:, :half], top, preferred_element_type=F32)
            + jnp.dot(inverse_ref[:, half:], bottom, preferred_element_type=F32)
        ).astype(BF16)


def upper_rows(place, unit_inverse, mine, other, after=()):
    width, cols = unit_inverse.shape[0], mine.shape[1]
    return pl.pallas_call(
        upper_kernel,
        in_specs=[SMEM, VMEM, VMEM, VMEM] + [ANY] * len(after),
        out_specs=VMEM,
        out_shape=jax.ShapeDtypeStruct((width, cols), BF16),
        compiler_params=pltpu.CompilerParams(vmem_limit_bytes=16 * 2**20),
        cost_estimate=weight_of(2),
        name="upper",
    )(place, unit_inverse, mine, other, *after)


def update_kernel(groups, per_group, pick_source, place_ref, swapped_ref, upper_ref, *refs):
    sources = refs[: 1 + per_group * len(groups)]
    out_ref, panel_ref, sem = refs[-3:]
    step = pl.program_id(0)
    width = panel_ref.shape[1]
    block = out_ref.shape[1]
    row_place, col_place = place_ref[0], place_ref[1]
    first_row = groups[0][0]

    def fetch(number, action):
        start, count = groups[number]
        here = panel_ref.at[pl.ds(start - first_row, count)]
        views = [sources[0].at[pl.ds(start, count), pl.ds(0, width)]]
        views += sources[1 + number * per_group : 1 + (number + 1) * per_group]
        for choice, view in enumerate(views):
            @pl.when(pick_source(col_place, place_ref[2]) == choice)
            def _():
                action(pltpu.make_async_copy(view, here, sem.at[number]))

    @pl.when(step == 0)
    def _():
        for number in range(len(groups)):
            fetch(number, lambda copy: copy.start())
        for number in range(len(groups)):
            fetch(number, lambda copy: copy.wait())

    in_panel = (col_place == 0) & (step * block < width)

    @pl.when(in_panel)
    def _():
        out_ref[...] = swapped_ref[...]

    @pl.when(jnp.logical_not(in_panel))
    def _():
        upper = upper_ref[...]
        for start, count in groups:
            here = slice(start - first_row, start - first_row + count)
            product = jnp.dot(panel_ref[here], upper, preferred_element_type=F32)
            out_ref[here] = (swapped_ref[here].astype(F32) - product).astype(BF16)
        if first_row < width:
            @pl.when(row_place == 0)
            def _():
                out_ref[: width - first_row] = upper[first_row:]


def update(groups, pick_source, place, matrix, swapped, upper, received):
    rows, cols = matrix.shape
    width = upper.shape[0]
    block = min(BLOCK, cols)
    count = sum(size for _, size in groups)
    first_row = groups[0][0]
    by_column = pl.BlockSpec(
        (pl.Element(count), pl.Element(block)), lambda i, s: (first_row, i * block)
    )
    sources = [matrix] + [x for group in received for x in group]
    return pl.pallas_call(
        functools.partial(update_kernel, groups, len(received[0]), pick_source),
        grid_spec=pltpu.PrefetchScalarGridSpec(
            num_scalar_prefetch=1,
            grid=(cols // block,),
            in_specs=[by_column, pl.BlockSpec((width, block), lambda i, s: (0, i))]
            + [ANY] * len(sources),
            out_specs=by_column,
            scratch_shapes=[
                pltpu.VMEM((count, width), BF16),
                pltpu.SemaphoreType.DMA((len(groups),)),
            ],
        ),
        out_shape=jax.ShapeDtypeStruct((rows, cols), BF16),
        input_output_aliases={1: 0},
        compiler_params=LARGE,
        cost_estimate=weight_of(0),
        name="update_rows",
    )(place, swapped, upper, *sources)


def swap_pairs(size, orders, step):
    return [(i, i ^ (1 << orders[i & 1][step])) for i in range(size)]


def grow_pairs(orders, step):
    pairs = []
    for core, order in enumerate(orders):
        places = [core]
        for bit in order[:step]:
            places += [i | (1 << bit) for i in places]
        pairs += [(i, i | (1 << order[step])) for i in places]
    return pairs


def spread(place, matrix, width, groups, core, n_prow, size):
    middle = size // 2
    count = len(groups)

    def move(value, pairs):
        pairs = [
            (row * size + a, row * size + b) for row in range(core, n_prow, 2) for a, b in pairs
        ]
        return lax.ppermute(value, ("prow", "pcol"), pairs)

    held = []
    for number in range(count + 1):
        pairs = [(middle, middle - 1)] * (number >= 1)
        sent = held[number - 1] if number >= 1 else None
        if number < count:
            pairs.append((0, middle))
            sent = chunk(place, 1, core, matrix, *groups[number], width, sent, CHUNK_WEIGHTS[number])
            if number >= 1:
                held[number - 1] = sent
        held.append(move(sent, pairs))
    received = []
    for number in range(count):
        arrays = [held[number], held[number + 1]]
        arrays.append(move(held[number], [(middle, middle + 1)]))
        distance = 1
        while middle - distance > 1 or middle + distance + 1 < size:
            if distance == 1:
                both = jnp.where(place[1] < middle, arrays[1], arrays[2])
            pairs = []
            if middle - distance > 1:
                pairs.append((middle - distance, middle - distance - 1))
            if middle + distance + 1 < size:
                pairs.append((middle + distance, middle + distance + 1))
            both = move(both, pairs)
            arrays.append(both)
            distance += 1
        received.append(arrays)
    return received


def source_of(size, per_core):
    middle = size // 2

    def pick_source(place, core):
        away = jnp.abs(place - middle)
        number = jnp.where(away == 0, 1, jnp.where(place < middle, 2, 3))
        number = jnp.where(away >= 2, away + 2, number)
        return jnp.where(place == 0, 0, number + core * per_core)

    return pick_source


def per_device(n_prow, n_pcol, matrix, pivots, unit_inverse):
    rows, cols = matrix.shape
    width = unit_inverse.shape[0]
    half = width // 2
    row_place = lax.axis_index("prow")
    col_place = lax.axis_index("pcol")
    core = row_place & 1
    place = jnp.stack([row_place, col_place, core]).astype(jnp.int32)
    matrix = pltpu.with_memory_space_constraint(matrix, pltpu.HBM)
    bits = list(range(1, n_prow.bit_length() - 1))
    orders = (bits, bits[::-1])
    cores = ([0], [0])
    last = len(bits) - 1

    size = rows // GROUPS
    groups = [(number * size, size) for number in range(GROUPS)]
    by_core = [spread(place, matrix, width, groups, c, n_prow, n_pcol) for c in range(2)]
    received = [first + second for first, second in zip(*by_core)]
    pick_source = source_of(n_pcol, len(by_core[0][0]))
    arrived = [x for pair in zip(*by_core) for x in (pair[0][0], pair[1][0])]
    arrived_right = [x for pair in zip(*by_core) for x in (pair[0][2], pair[1][2])]

    order = jnp.where(core == 0, pivots, jnp.roll(pivots, half))
    down_got = lax.ppermute(chunk(place, 0, 0, matrix, half, half, cols), "prow", [(0, 1)])
    pieces = pick(place, order, matrix)
    up, sent = pieces[: PIECES // 2], pieces[PIECES // 2 :]
    up_got = [lax.ppermute(x, "prow", swap_pairs(n_prow, cores, 0)) for x in sent]
    down = chunk(place, 0, 0, matrix, 0, half, cols, down_got)
    def pins(a, b):
        return arrived[max(a - 2, 0):a] + arrived_right[max(b - 2, 0):b]
    for step in range(last + 1):
        down_got = lax.ppermute(down, "prow", grow_pairs(orders, step))
        up = [add(up, up_got, pins(*JOIN_AFTER[min(step, 1)]), JOIN_WEIGHTS[min(step, 1)])]
        up_got = [lax.ppermute(up[0], "prow", swap_pairs(n_prow, orders, step))]
        down = add([down], [down_got], [] + pins(*DOWN_AFTER[min(step, 1)]), DOWN_WEIGHTS[min(step, 1)])
    down_got = lax.ppermute(down, "prow", swap_pairs(n_prow, cores, 0))
    swapped, token = swap(place, pivots, matrix, down, down_got, pins(0, 0))
    up = add(up, up_got, pins(2, 1), 0)
    up_got = lax.ppermute(up, "prow", swap_pairs(n_prow, cores, 0))
    upper = upper_rows(place, unit_inverse, up, up_got, pins(3, 2))

    common = (pick_source, place, matrix)
    out = update(groups[:-1], *common, swapped, upper, received[:-1])
    return update(groups[-1:], *common, out, upper, received[-1:])


def solution(mesh):
    return jax.shard_map(
        functools.partial(per_device, mesh.shape["prow"], mesh.shape["pcol"]),
        mesh=mesh,
        in_specs=(P("prow", "pcol"), P(), P()),
        out_specs=P("prow", "pcol"),
        check_vma=False,
    )
```

```python
import functools

import jax
import jax.numpy as jnp
from jax import lax
from jax.experimental import pallas as pl
from jax.experimental.pallas import tpu as pltpu
from jax.sharding import PartitionSpec as P

GROUPS = 2
CHUNK_WEIGHTS = (5, 5)
JOIN_WEIGHTS, JOIN_AFTER = (2, 2), ((0, 0), (3, 1))
DOWN_WEIGHTS, DOWN_AFTER = (0, 20), ((1, 0), (0, 0))
PIECES = 2
BLOCK = 512
F32, BF16 = jnp.float32, jnp.bfloat16
VMEM = pl.BlockSpec(memory_space=pltpu.VMEM)
ANY = pl.BlockSpec(memory_space=pl.ANY)
SMEM = pl.BlockSpec(memory_space=pltpu.SMEM)
SMALL = pltpu.CompilerParams(vmem_limit_bytes=8 * 2**20)
LARGE = pltpu.CompilerParams(vmem_limit_bytes=28 * 2**20)


FREE = pl.CostEstimate(flops=0, bytes_accessed=0, transcendentals=0)
def weight_of(x):
    x = float(x)
    return pl.CostEstimate(flops=int(x*1.15e9), bytes_accessed=int(x*3.69e6), transcendentals=0)


def chunk_kernel(first_row, axis, core, place_ref, matrix_ref, *refs):
    out_ref, sem = refs[-2:]
    rows, width = out_ref.shape

    @pl.when((place_ref[axis] == 0) & (place_ref[2] == core))
    def _():
        copy = pltpu.make_async_copy(
            matrix_ref.at[pl.ds(first_row, rows), pl.ds(0, width)], out_ref, sem
        )
        copy.start()
        copy.wait()


def chunk(place, axis, core, matrix, first_row, rows, width, held=None, weight=0, after=()):
    in_specs, operands = [SMEM, ANY], [place, matrix]
    if held is not None:
        in_specs.append(VMEM)
        operands.append(held)
    in_specs += [ANY] * len(after)
    operands += after
    return pl.pallas_call(
        functools.partial(chunk_kernel, first_row, axis, core),
        in_specs=in_specs,
        out_specs=VMEM,
        out_shape=jax.ShapeDtypeStruct((rows, width), BF16),
        scratch_shapes=[pltpu.SemaphoreType.DMA],
        input_output_aliases={} if held is None else {2: 0},
        compiler_params=SMALL,
        cost_estimate=weight_of(weight),
        name="chunk",
    )(*operands)


def pick_kernel(place_ref, pivots_ref, matrix_ref, *refs):
    onehot_ref = refs[-1]
    rows = matrix_ref.shape[0]
    width = pivots_ref.shape[0]
    count = width // PIECES

    @pl.when(pl.program_id(0) == 0)
    def _():
        row = lax.broadcasted_iota(jnp.int32, (width, rows), 1) + place_ref[0] * rows
        onehot_ref[...] = jnp.where(pivots_ref[...] == row, 1.0, 0.0).astype(BF16)

    picked = jnp.dot(onehot_ref[...], matrix_ref[...], preferred_element_type=F32).astype(BF16)
    for number, out_ref in enumerate(refs[:PIECES]):
        out_ref[...] = picked[number * count : (number + 1) * count]


def pick(place, pivots, matrix):
    rows, cols = matrix.shape
    width = pivots.shape[0]
    block = min(BLOCK, cols)
    count = width // PIECES
    return pl.pallas_call(
        pick_kernel,
        grid_spec=pltpu.PrefetchScalarGridSpec(
            num_scalar_prefetch=1,
            grid=(cols // block,),
            in_specs=[
                pl.BlockSpec((width, 1), lambda i, s: (0, 0)),
                pl.BlockSpec((rows, block), lambda i, s: (0, i)),
            ],
            out_specs=[pl.BlockSpec((count, block), lambda i, s: (0, i))] * PIECES,
            scratch_shapes=[pltpu.VMEM((width, rows), BF16)],
        ),
        out_shape=[jax.ShapeDtypeStruct((count, cols), BF16)] * PIECES,
        compiler_params=LARGE,
        cost_estimate=weight_of(0),
        name="pick_rows",
    )(place, pivots[:, None], matrix)


def add_kernel(count, *refs):
    start = 0
    out_ref = refs[-1]
    for own_ref, got_ref in zip(refs[:count], refs[count : 2 * count]):
        rows = own_ref.shape[0]
        out_ref[start : start + rows] = own_ref[...] + got_ref[...]
        start += rows


def add(own, got, after=(), weight=0):
    rows, cols = sum(x.shape[0] for x in own), own[0].shape[1]
    return pl.pallas_call(
        functools.partial(add_kernel, len(own)),
        in_specs=[VMEM] * (2 * len(own)) + [ANY] * len(after),
        out_specs=VMEM,
        out_shape=jax.ShapeDtypeStruct((rows, cols), BF16),
        compiler_params=SMALL,
        cost_estimate=weight_of(weight),
        name="add",
    )(*own, *got, *after)


def swap_kernel(place_ref, pivots_ref, matrix_ref, mine_ref, other_ref, *rest):
    out_ref, token_ref, onehot_ref, keep_ref = rest[-4:]
    token_ref[...] = jnp.zeros_like(token_ref)
    step = pl.program_id(0)
    rows, block = matrix_ref.shape
    width = pivots_ref.shape[1]
    half = width // 2
    row_place, col_place, core = (place_ref[i] for i in range(3))
    piece = min(rows, 512)

    @pl.when(step == 0)
    def _():
        for start in range(0, rows, piece):
            here = slice(start, start + piece)
            row = lax.broadcasted_iota(jnp.int32, (piece, width), 0) + row_place * rows + start
            onehot = jnp.where(pivots_ref[...] == row, 1.0, 0.0)
            onehot_ref[here] = onehot.astype(BF16)
            has_pivot = jnp.max(onehot, axis=1, keepdims=True)
            keep_ref[here] = jnp.broadcast_to(1.0 - has_pivot, (piece, 128))

    in_panel = (col_place == 0) & (step * block < width)

    @pl.when(in_panel)
    def _():
        out_ref[...] = matrix_ref[...]

    @pl.when(jnp.logical_not(in_panel))
    def _():
        mine, other = mine_ref[...], other_ref[...]
        top, bottom = jnp.where(core == 0, mine, other), jnp.where(core == 0, other, mine)
        for start in range(0, rows, piece):
            here = slice(start, start + piece)
            keep = jnp.concatenate([keep_ref[here]] * (block // 128), axis=1)
            moved = jnp.dot(onehot_ref[here, :half], top, preferred_element_type=F32)
            moved += jnp.dot(onehot_ref[here, half:], bottom, preferred_element_type=F32)
            out_ref[here] = (matrix_ref[here].astype(F32) * keep + moved).astype(BF16)


def swap(place, pivots, matrix, mine, other, after=()):
    rows, cols = matrix.shape
    width = pivots.shape[0]
    block = min(BLOCK, cols)
    by_column = pl.BlockSpec((rows, block), lambda i, s: (0, i))
    half_by_column = pl.BlockSpec((width // 2, block), lambda i, s: (0, i))
    return pl.pallas_call(
        swap_kernel,
        grid_spec=pltpu.PrefetchScalarGridSpec(
            num_scalar_prefetch=1,
            grid=(cols // block,),
            in_specs=[
                pl.BlockSpec((1, width), lambda i, s: (0, 0)),
                by_column,
                half_by_column,
                half_by_column,
            ]
            + [ANY] * len(after),
            out_specs=[by_column, pl.BlockSpec((8, 128), lambda i, s: (0, 0))],
            scratch_shapes=[pltpu.VMEM((rows, width), BF16), pltpu.VMEM((rows, 128), F32)],
        ),
        out_shape=[
            jax.ShapeDtypeStruct((rows, cols), BF16),
            jax.ShapeDtypeStruct((8, 128), F32),
        ],
        compiler_params=LARGE,
        cost_estimate=weight_of(0),
        name="swap_rows",
    )(place, pivots[None, :], matrix, mine, other, *after)


def upper_kernel(place_ref, inverse_ref, mine_ref, other_ref, *rest):
    out_ref = rest[-1]
    width, cols = out_ref.shape
    half = width // 2
    block = min(BLOCK, cols)
    for start in range(0, cols, block):
        here = slice(start, start + block)
        mine, other = mine_ref[:, here], other_ref[:, here]
        first = place_ref[2] == 0
        top, bottom = jnp.where(first, mine, other), jnp.where(first, other, mine)
        out_ref[:, here] = (
            jnp.dot(inverse_ref[:, :half], top, preferred_element_type=F32)
            + jnp.dot(inverse_ref[:, half:], bottom, preferred_element_type=F32)
        ).astype(BF16)


def upper_rows(place, unit_inverse, mine, other, after=()):
    width, cols = unit_inverse.shape[0], mine.shape[1]
    return pl.pallas_call(
        upper_kernel,
        in_specs=[SMEM, VMEM, VMEM, VMEM] + [ANY] * len(after),
        out_specs=VMEM,
        out_shape=jax.ShapeDtypeStruct((width, cols), BF16),
        compiler_params=pltpu.CompilerParams(vmem_limit_bytes=16 * 2**20),
        cost_estimate=weight_of(2),
        name="upper",
    )(place, unit_inverse, mine, other, *after)


def update_kernel(groups, per_group, pick_source, place_ref, swapped_ref, upper_ref, *refs):
    sources = refs[: 1 + per_group * len(groups)]
    out_ref, panel_ref, sem = refs[-3:]
    step = pl.program_id(0)
    width = panel_ref.shape[1]
    block = out_ref.shape[1]
    row_place, col_place = place_ref[0], place_ref[1]
    first_row = groups[0][0]

    def fetch(number, action):
        start, count = groups[number]
        here = panel_ref.at[pl.ds(start - first_row, count)]
        views = [sources[0].at[pl.ds(start, count), pl.ds(0, width)]]
        views += sources[1 + number * per_group : 1 + (number + 1) * per_group]
        for choice, view in enumerate(views):
            @pl.when(pick_source(col_place, place_ref[2]) == choice)
            def _():
                action(pltpu.make_async_copy(view, here, sem.at[number]))

    @pl.when(step == 0)
    def _():
        for number in range(len(groups)):
            fetch(number, lambda copy: copy.start())
        for number in range(len(groups)):
            fetch(number, lambda copy: copy.wait())

    in_panel = (col_place == 0) & (step * block < width)

    @pl.when(in_panel)
    def _():
        out_ref[...] = swapped_ref[...]

    @pl.when(jnp.logical_not(in_panel))
    def _():
        upper = upper_ref[...]
        for start, count in groups:
            here = slice(start - first_row, start - first_row + count)
            product = jnp.dot(panel_ref[here], upper, preferred_element_type=F32)
            out_ref[here] = (swapped_ref[here].astype(F32) - product).astype(BF16)
        if first_row < width:
            @pl.when(row_place == 0)
            def _():
                out_ref[: width - first_row] = upper[first_row:]


def update(groups, pick_source, place, matrix, swapped, upper, received):
    rows, cols = matrix.shape
    width = upper.shape[0]
    block = min(BLOCK, cols)
    count = sum(size for _, size in groups)
    first_row = groups[0][0]
    by_column = pl.BlockSpec(
        (pl.Element(count), pl.Element(block)), lambda i, s: (first_row, i * block)
    )
    sources = [matrix] + [x for group in received for x in group]
    return pl.pallas_call(
        functools.partial(update_kernel, groups, len(received[0]), pick_source),
        grid_spec=pltpu.PrefetchScalarGridSpec(
            num_scalar_prefetch=1,
            grid=(cols // block,),
            in_specs=[by_column, pl.BlockSpec((width, block), lambda i, s: (0, i))]
            + [ANY] * len(sources),
            out_specs=by_column,
            scratch_shapes=[
                pltpu.VMEM((count, width), BF16),
                pltpu.SemaphoreType.DMA((len(groups),)),
            ],
        ),
        out_shape=jax.ShapeDtypeStruct((rows, cols), BF16),
        input_output_aliases={1: 0},
        compiler_params=LARGE,
        cost_estimate=weight_of(0),
        name="update_rows",
    )(place, swapped, upper, *sources)


def swap_pairs(size, orders, step):
    return [(i, i ^ (1 << orders[i & 1][step])) for i in range(size)]


def grow_pairs(orders, step):
    pairs = []
    for core, order in enumerate(orders):
        places = [core]
        for bit in order[:step]:
            places += [i | (1 << bit) for i in places]
        pairs += [(i, i | (1 << order[step])) for i in places]
    return pairs


def spread(place, matrix, width, groups, core, n_prow, size):
    middle = size // 2
    count = len(groups)

    def move(value, pairs):
        pairs = [
            (row * size + a, row * size + b) for row in range(core, n_prow, 2) for a, b in pairs
        ]
        return lax.ppermute(value, ("prow", "pcol"), pairs)

    held = []
    for number in range(count + 1):
        pairs = [(middle, middle - 1)] * (number >= 1)
        sent = held[number - 1] if number >= 1 else None
        if number < count:
            pairs.append((0, middle))
            sent = chunk(place, 1, core, matrix, *groups[number], width, sent, CHUNK_WEIGHTS[number])
            if number >= 1:
                held[number - 1] = sent
        held.append(move(sent, pairs))
    received = []
    for number in range(count):
        arrays = [held[number], held[number + 1]]
        arrays.append(move(held[number], [(middle, middle + 1)]))
        distance = 1
        while middle - distance > 1 or middle + distance + 1 < size:
            if distance == 1:
                both = jnp.where(place[1] < middle, arrays[1], arrays[2])
            pairs = []
            if middle - distance > 1:
                pairs.append((middle - distance, middle - distance - 1))
            if middle + distance + 1 < size:
                pairs.append((middle + distance, middle + distance + 1))
            both = move(both, pairs)
            arrays.append(both)
            distance += 1
        received.append(arrays)
    return received


def source_of(size, per_core):
    middle = size // 2

    def pick_source(place, core):
        away = jnp.abs(place - middle)
        number = jnp.where(away == 0, 1, jnp.where(place < middle, 2, 3))
        number = jnp.where(away >= 2, away + 2, number)
        return jnp.where(place == 0, 0, number + core * per_core)

    return pick_source


def per_device(n_prow, n_pcol, matrix, pivots, unit_inverse):
    rows, cols = matrix.shape
    width = unit_inverse.shape[0]
    half = width // 2
    row_place = lax.axis_index("prow")
    col_place = lax.axis_index("pcol")
    core = row_place & 1
    place = jnp.stack([row_place, col_place, core]).astype(jnp.int32)
    matrix = pltpu.with_memory_space_constraint(matrix, pltpu.HBM)
    bits = list(range(1, n_prow.bit_length() - 1))
    orders = (bits, bits[::-1])
    cores = ([0], [0])
    last = len(bits) - 1

    size = rows // GROUPS
    groups = [(number * size, size) for number in range(GROUPS)]
    by_core = [spread(place, matrix, width, groups, c, n_prow, n_pcol) for c in range(2)]
    received = [first + second for first, second in zip(*by_core)]
    pick_source = source_of(n_pcol, len(by_core[0][0]))
    arrived = [x for pair in zip(*by_core) for x in (pair[0][0], pair[1][0])]
    arrived_right = [x for pair in zip(*by_core) for x in (pair[0][2], pair[1][2])]

    order = jnp.where(core == 0, pivots, jnp.roll(pivots, half))
    down_got = lax.ppermute(chunk(place, 0, 0, matrix, half, half, cols), "prow", [(0, 1)])
    pieces = pick(place, order, matrix)
    up, sent = pieces[: PIECES // 2], pieces[PIECES // 2 :]
    up_got = [lax.ppermute(x, "prow", swap_pairs(n_prow, cores, 0)) for x in sent]
    down = chunk(place, 0, 0, matrix, 0, half, cols, down_got)
    def pins(a, b):
        return arrived[max(a - 2, 0):a] + arrived_right[max(b - 2, 0):b]
    for step in range(last + 1):
        down_got = lax.ppermute(down, "prow", grow_pairs(orders, step))
        up = [add(up, up_got, pins(*JOIN_AFTER[min(step, 1)]), JOIN_WEIGHTS[min(step, 1)])]
        up_got = [lax.ppermute(up[0], "prow", swap_pairs(n_prow, orders, step))]
        down = add([down], [down_got], [] + pins(*DOWN_AFTER[min(step, 1)]), DOWN_WEIGHTS[min(step, 1)])
    down_got = lax.ppermute(down, "prow", swap_pairs(n_prow, cores, 0))
    swapped, token = swap(place, pivots, matrix, down, down_got, pins(0, 0))
    up = add(up, up_got, pins(2, 1), 0)
    up_got = lax.ppermute(up, "prow", swap_pairs(n_prow, cores, 0))
    upper = upper_rows(place, unit_inverse, up, up_got, pins(3, 2))

    common = (pick_source, place, matrix)
    out = update(groups[:-1], *common, swapped, upper, received[:-1])
    return update(groups[-1:], *common, out, upper, received[-1:])


def solution(mesh):
    return jax.shard_map(
        functools.partial(per_device, mesh.shape["prow"], mesh.shape["pcol"]),
        mesh=mesh,
        in_specs=(P("prow", "pcol"), P(), P()),
        out_specs=P("prow", "pcol"),
        check_vma=False,
    )
```

```python
import functools

import jax
import jax.numpy as jnp
from jax import lax
from jax.experimental import pallas as pl
from jax.experimental.pallas import tpu as pltpu
from jax.sharding import PartitionSpec as P

GROUPS = 2
CHUNK_WEIGHTS = (0, 5)
JOIN_WEIGHTS, JOIN_AFTER = (2, 2), ((1, 0), (3, 1))
DOWN_WEIGHTS, DOWN_AFTER = (0, 20), ((1, 0), (0, 0))
PIECES = 2
BLOCK = 256
F32, BF16 = jnp.float32, jnp.bfloat16
VMEM = pl.BlockSpec(memory_space=pltpu.VMEM)
ANY = pl.BlockSpec(memory_space=pl.ANY)
SMEM = pl.BlockSpec(memory_space=pltpu.SMEM)
SMALL = pltpu.CompilerParams(vmem_limit_bytes=8 * 2**20)
LARGE = pltpu.CompilerParams(vmem_limit_bytes=28 * 2**20)


FREE = pl.CostEstimate(flops=0, bytes_accessed=0, transcendentals=0)
def weight_of(x):
    x = float(x)
    return pl.CostEstimate(flops=int(x*1.15e9), bytes_accessed=int(x*3.69e6), transcendentals=0)


def chunk_kernel(first_row, axis, core, place_ref, matrix_ref, *refs):
    out_ref, sem = refs[-2:]
    rows, width = out_ref.shape

    @pl.when((place_ref[axis] == 0) & (place_ref[2] == core))
    def _():
        copy = pltpu.make_async_copy(
            matrix_ref.at[pl.ds(first_row, rows), pl.ds(0, width)], out_ref, sem
        )
        copy.start()
        copy.wait()


def chunk(place, axis, core, matrix, first_row, rows, width, held=None, weight=0, after=()):
    in_specs, operands = [SMEM, ANY], [place, matrix]
    if held is not None:
        in_specs.append(VMEM)
        operands.append(held)
    in_specs += [ANY] * len(after)
    operands += after
    return pl.pallas_call(
        functools.partial(chunk_kernel, first_row, axis, core),
        in_specs=in_specs,
        out_specs=VMEM,
        out_shape=jax.ShapeDtypeStruct((rows, width), BF16),
        scratch_shapes=[pltpu.SemaphoreType.DMA],
        input_output_aliases={} if held is None else {2: 0},
        compiler_params=SMALL,
        cost_estimate=weight_of(weight),
        name="chunk",
    )(*operands)


def columns(number, block):
    return pl.ds(pl.multiple_of(number * block, block), block)


def pick_kernel(place_ref, pivots_ref, matrix_ref, *refs):
    whole_ref, onehot_ref, sem = refs[-3:]
    outs = refs[-3 - PIECES : -3]
    rows, cols = whole_ref.shape
    width = pivots_ref.shape[0]
    block = min(BLOCK, cols)
    count = width // PIECES

    def fetch(number):
        here = columns(number, block)
        return pltpu.make_async_copy(
            matrix_ref.at[:, here], whole_ref.at[:, here], sem.at[number]
        )

    for number in range(cols // block):
        fetch(number).start()
    row = lax.broadcasted_iota(jnp.int32, (width, rows), 1) + place_ref[0] * rows
    onehot_ref[...] = jnp.where(pivots_ref[...] == row, 1.0, 0.0).astype(BF16)

    @pl.loop(0, cols // block)
    def _(number):
        fetch(number).wait()
        here = columns(number, block)
        picked = jnp.dot(onehot_ref[...], whole_ref[:, here], preferred_element_type=F32)
        picked = picked.astype(BF16)
        for piece, out_ref in enumerate(outs):
            out_ref[:, here] = picked[piece * count : (piece + 1) * count]


def pick(place, pivots, matrix, after=()):
    rows, cols = matrix.shape
    width = pivots.shape[0]
    block = min(BLOCK, cols)
    return pl.pallas_call(
        pick_kernel,
        in_specs=[SMEM, VMEM, ANY] + [ANY] * len(after),
        out_specs=[VMEM] * PIECES,
        out_shape=[jax.ShapeDtypeStruct((width // PIECES, cols), BF16)] * PIECES,
        scratch_shapes=[
            pltpu.VMEM((rows, cols), BF16),
            pltpu.VMEM((width, rows), BF16),
            pltpu.SemaphoreType.DMA((cols // block,)),
        ],
        compiler_params=LARGE,
        cost_estimate=weight_of(0),
        name="pick_rows",
    )(place, pivots[:, None], matrix, *after)


def add_kernel(count, *refs):
    start = 0
    out_ref = refs[-1]
    for own_ref, got_ref in zip(refs[:count], refs[count : 2 * count]):
        rows = own_ref.shape[0]
        out_ref[start : start + rows] = own_ref[...] + got_ref[...]
        start += rows


def add(own, got, after=(), weight=0):
    rows, cols = sum(x.shape[0] for x in own), own[0].shape[1]
    return pl.pallas_call(
        functools.partial(add_kernel, len(own)),
        in_specs=[VMEM] * (2 * len(own)) + [ANY] * len(after),
        out_specs=VMEM,
        out_shape=jax.ShapeDtypeStruct((rows, cols), BF16),
        compiler_params=SMALL,
        cost_estimate=weight_of(weight),
        name="add",
    )(*own, *got, *after)


def swap_kernel(place_ref, pivots_ref, matrix_ref, mine_ref, other_ref, *rest):
    out_ref, token_ref, whole_ref, onehot_ref, keep_ref, down_ref, in_sem, out_sem = rest[-8:]
    rows, cols = whole_ref.shape
    width = pivots_ref.shape[1]
    half = width // 2
    row_place, col_place, core = (place_ref[i] for i in range(3))
    block = min(BLOCK, cols)
    piece = min(rows, 512)

    def fetch(number):
        here = columns(number, block)
        return pltpu.make_async_copy(
            matrix_ref.at[:, here], whole_ref.at[:, here], in_sem.at[number]
        )

    def store(number):
        here = columns(number, block)
        return pltpu.make_async_copy(
            whole_ref.at[:, here], out_ref.at[:, here], out_sem.at[number]
        )

    for number in range(cols // block):
        fetch(number).start()
    token_ref[...] = jnp.zeros_like(token_ref)
    down_ref[pl.ds(pl.multiple_of(core * half, half), half)] = mine_ref[...]
    down_ref[pl.ds(pl.multiple_of((1 - core) * half, half), half)] = other_ref[...]
    for start in range(0, rows, piece):
        here = slice(start, start + piece)
        row = lax.broadcasted_iota(jnp.int32, (piece, width), 0) + row_place * rows + start
        onehot = jnp.where(pivots_ref[...] == row, 1.0, 0.0)
        onehot_ref[here] = onehot.astype(BF16)
        has_pivot = jnp.max(onehot, axis=1, keepdims=True)
        keep_ref[here] = jnp.broadcast_to(1.0 - has_pivot, (piece, 128))

    @pl.loop(0, cols // block)
    def _(number):
        fetch(number).wait()
        there = columns(number, block)

        @pl.when((col_place > 0) | (number * block >= width))
        def _():
            down = down_ref[:, there]
            for start in range(0, rows, piece):
                here = slice(start, start + piece)
                keep = jnp.concatenate([keep_ref[here]] * (block // 128), axis=1)
                moved = jnp.dot(onehot_ref[here], down, preferred_element_type=F32)
                kept = whole_ref[here, there].astype(F32) * keep
                whole_ref[here, there] = (kept + moved).astype(BF16)

        store(number).start()

    for number in range(cols // block):
        store(number).wait()


def swap(place, pivots, matrix, mine, other, after=()):
    rows, cols = matrix.shape
    width = pivots.shape[0]
    count = cols // min(BLOCK, cols)
    return pl.pallas_call(
        swap_kernel,
        in_specs=[SMEM, VMEM, ANY, VMEM, VMEM] + [ANY] * len(after),
        out_specs=[pl.BlockSpec(memory_space=pltpu.HBM), VMEM],
        out_shape=[
            jax.ShapeDtypeStruct((rows, cols), BF16),
            jax.ShapeDtypeStruct((8, 128), F32),
        ],
        scratch_shapes=[
            pltpu.VMEM((rows, cols), BF16),
            pltpu.VMEM((rows, width), BF16),
            pltpu.VMEM((rows, 128), F32),
            pltpu.VMEM((width, cols), BF16),
            pltpu.SemaphoreType.DMA((count,)),
            pltpu.SemaphoreType.DMA((count,)),
        ],
        compiler_params=LARGE,
        cost_estimate=weight_of(0),
        name="swap_rows",
    )(place, pivots[None, :], matrix, mine, other, *after)


def upper_kernel(place_ref, inverse_ref, mine_ref, other_ref, *rest):
    out_ref = rest[-1]
    width, cols = out_ref.shape
    half = width // 2
    block = min(BLOCK, cols)
    for start in range(0, cols, block):
        here = slice(start, start + block)
        mine, other = mine_ref[:, here], other_ref[:, here]
        first = place_ref[2] == 0
        top, bottom = jnp.where(first, mine, other), jnp.where(first, other, mine)
        out_ref[:, here] = (
            jnp.dot(inverse_ref[:, :half], top, preferred_element_type=F32)
            + jnp.dot(inverse_ref[:, half:], bottom, preferred_element_type=F32)
        ).astype(BF16)


def upper_rows(place, unit_inverse, mine, other, after=()):
    width, cols = unit_inverse.shape[0], mine.shape[1]
    return pl.pallas_call(
        upper_kernel,
        in_specs=[SMEM, VMEM, VMEM, VMEM] + [ANY] * len(after),
        out_specs=VMEM,
        out_shape=jax.ShapeDtypeStruct((width, cols), BF16),
        compiler_params=pltpu.CompilerParams(vmem_limit_bytes=16 * 2**20),
        cost_estimate=weight_of(2),
        name="upper",
    )(place, unit_inverse, mine, other, *after)


def update_kernel(first_row, per_group, pick_source, place_ref, swapped_ref, upper_ref, *refs):
    sources = refs[: 1 + per_group]
    out_ref, rows_ref, panel_ref, in_sem, out_sem, sem = refs[-6:]
    count, width = panel_ref.shape
    cols = rows_ref.shape[1]
    row_place, col_place, core = (place_ref[i] for i in range(3))
    block = min(BLOCK, cols)
    piece = min(count, 512)
    rows = pl.ds(first_row, count)

    def fetch_panel(action):
        views = [sources[0].at[rows, pl.ds(0, width)], *sources[1:]]
        for choice, view in enumerate(views):
            @pl.when(pick_source(col_place, core) == choice)
            def _():
                action(pltpu.make_async_copy(view, panel_ref, sem))

    def fetch(number):
        here = columns(number, block)
        return pltpu.make_async_copy(
            swapped_ref.at[rows, here], rows_ref.at[:, here], in_sem.at[number]
        )

    def store(number):
        here = columns(number, block)
        return pltpu.make_async_copy(
            rows_ref.at[:, here], out_ref.at[rows, here], out_sem.at[number]
        )

    fetch_panel(lambda copy: copy.start())
    for number in range(cols // block):
        fetch(number).start()
    fetch_panel(lambda copy: copy.wait())

    @pl.loop(0, cols // block)
    def _(number):
        fetch(number).wait()
        there = columns(number, block)

        @pl.when((col_place > 0) | (number * block >= width))
        def _():
            upper = upper_ref[:, there]
            for start in range(0, count, piece):
                here = slice(start, start + piece)
                product = jnp.dot(panel_ref[here], upper, preferred_element_type=F32)
                left = rows_ref[here, there].astype(F32) - product
                rows_ref[here, there] = left.astype(BF16)
            if first_row < width:
                @pl.when(row_place == 0)
                def _():
                    rows_ref[: width - first_row, there] = upper[first_row:]

        store(number).start()

    for number in range(cols // block):
        store(number).wait()


def update(group, pick_source, place, matrix, swapped, upper, received):
    first_row, count = group
    rows, cols = matrix.shape
    width = upper.shape[0]
    blocks = cols // min(BLOCK, cols)
    sources = [matrix] + received
    hbm = pl.BlockSpec(memory_space=pltpu.HBM)
    return pl.pallas_call(
        functools.partial(update_kernel, first_row, len(received), pick_source),
        in_specs=[SMEM, hbm, VMEM] + [ANY] * len(sources),
        out_specs=hbm,
        out_shape=jax.ShapeDtypeStruct((rows, cols), BF16),
        scratch_shapes=[
            pltpu.VMEM((count, cols), BF16),
            pltpu.VMEM((count, width), BF16),
            pltpu.SemaphoreType.DMA((blocks,)),
            pltpu.SemaphoreType.DMA((blocks,)),
            pltpu.SemaphoreType.DMA,
        ],
        input_output_aliases={1: 0},
        compiler_params=LARGE,
        cost_estimate=weight_of(0),
        name="update_rows",
    )(place, swapped, upper, *sources)


def swap_pairs(size, orders, step):
    return [(i, i ^ (1 << orders[i & 1][step])) for i in range(size)]


def grow_pairs(orders, step):
    pairs = []
    for core, order in enumerate(orders):
        places = [core]
        for bit in order[:step]:
            places += [i | (1 << bit) for i in places]
        pairs += [(i, i | (1 << order[step])) for i in places]
    return pairs


def spread(place, matrix, width, groups, core, n_prow, size):
    middle = size // 2
    count = len(groups)

    def move(value, pairs):
        pairs = [
            (row * size + a, row * size + b) for row in range(core, n_prow, 2) for a, b in pairs
        ]
        return lax.ppermute(value, ("prow", "pcol"), pairs)

    held = []
    for number in range(count + 1):
        pairs = [(middle, middle - 1)] * (number >= 1)
        sent = held[number - 1] if number >= 1 else None
        if number < count:
            pairs.append((0, middle))
            sent = chunk(place, 1, core, matrix, *groups[number], width, sent, CHUNK_WEIGHTS[number])
            if number >= 1:
                held[number - 1] = sent
        held.append(move(sent, pairs))
    received = []
    for number in range(count):
        arrays = [held[number], held[number + 1]]
        arrays.append(move(held[number], [(middle, middle + 1)]))
        distance = 1
        while middle - distance > 1 or middle + distance + 1 < size:
            if distance == 1:
                both = jnp.where(place[1] < middle, arrays[1], arrays[2])
            pairs = []
            if middle - distance > 1:
                pairs.append((middle - distance, middle - distance - 1))
            if middle + distance + 1 < size:
                pairs.append((middle + distance, middle + distance + 1))
            both = move(both, pairs)
            arrays.append(both)
            distance += 1
        received.append(arrays)
    return received


def source_of(size, per_core):
    middle = size // 2

    def pick_source(place, core):
        away = jnp.abs(place - middle)
        number = jnp.where(away == 0, 1, jnp.where(place < middle, 2, 3))
        number = jnp.where(away >= 2, away + 2, number)
        return jnp.where(place == 0, 0, number + core * per_core)

    return pick_source


def per_device(n_prow, n_pcol, matrix, pivots, unit_inverse):
    rows, cols = matrix.shape
    width = unit_inverse.shape[0]
    half = width // 2
    row_place = lax.axis_index("prow")
    col_place = lax.axis_index("pcol")
    core = row_place & 1
    place = jnp.stack([row_place, col_place, core]).astype(jnp.int32)
    matrix = pltpu.with_memory_space_constraint(matrix, pltpu.HBM)
    bits = list(range(1, n_prow.bit_length() - 1))
    orders = (bits, bits[::-1])
    cores = ([0], [0])
    last = len(bits) - 1

    size = rows // GROUPS
    groups = [(number * size, size) for number in range(GROUPS)]
    by_core = [spread(place, matrix, width, groups, c, n_prow, n_pcol) for c in range(2)]
    received = [first + second for first, second in zip(*by_core)]
    pick_source = source_of(n_pcol, len(by_core[0][0]))
    arrived = [x for pair in zip(*by_core) for x in (pair[0][0], pair[1][0])]
    arrived_right = [x for pair in zip(*by_core) for x in (pair[0][2], pair[1][2])]

    order = jnp.where(core == 0, pivots, jnp.roll(pivots, half))
    down_got = lax.ppermute(chunk(place, 0, 0, matrix, half, half, cols), "prow", [(0, 1)])
    if 0 < 2:
        down = chunk(place, 0, 0, matrix, 0, half, cols, down_got)
    pieces = pick(place, order, matrix, [down] if 0 == 1 else [])
    up, sent = pieces[: PIECES // 2], pieces[PIECES // 2 :]
    up_got = [lax.ppermute(x, "prow", swap_pairs(n_prow, cores, 0)) for x in sent]
    if 0 == 3:
        down = chunk(place, 0, 0, matrix, 0, half, cols, down_got, after=pieces[:1])
    def pins(a, b):
        return arrived[max(a - 2, 0):a] + arrived_right[max(b - 2, 0):b]
    for step in range(last + 1):
        up = [add(up, up_got, pins(*JOIN_AFTER[min(step, 1)]), JOIN_WEIGHTS[min(step, 1)])]
        if step == 0 and 0 == 2:
            down = chunk(place, 0, 0, matrix, 0, half, cols, down_got, after=up)
        down_got = lax.ppermute(down, "prow", grow_pairs(orders, step))
        up_got = [lax.ppermute(up[0], "prow", swap_pairs(n_prow, orders, step))]
        down = add([down], [down_got], [] + pins(*DOWN_AFTER[min(step, 1)]), DOWN_WEIGHTS[min(step, 1)])
    down_got = lax.ppermute(down, "prow", swap_pairs(n_prow, cores, 0))
    swapped, token = swap(place, pivots, matrix, down, down_got, pins(3, 1))
    up = add(up, up_got, pins(0, 0), 0)
    up_got = lax.ppermute(up, "prow", swap_pairs(n_prow, cores, 0))
    upper = upper_rows(place, unit_inverse, up, up_got, pins(3, 2))

    out = swapped
    for group, arrays in zip(groups, received):
        out = update(group, pick_source, place, matrix, out, upper, arrays)
    return out


def solution(mesh):
    return jax.shard_map(
        functools.partial(per_device, mesh.shape["prow"], mesh.shape["pcol"]),
        mesh=mesh,
        in_specs=(P("prow", "pcol"), P(), P()),
        out_specs=P("prow", "pcol"),
        check_vma=False,
    )
```

```python
import functools

import jax
import jax.numpy as jnp
from jax import lax
from jax.experimental import pallas as pl
from jax.experimental.pallas import tpu as pltpu
from jax.sharding import PartitionSpec as P

GROUPS = 2
CHUNK_WEIGHTS = (0, 5)
JOIN_WEIGHTS, JOIN_AFTER = (0, 5), ((1, 0), (2, 1))
DOWN_WEIGHTS, DOWN_AFTER = (0, 2), ((0, 0), (0, 0))
PIECES = 2
BLOCK = 256
F32, BF16 = jnp.float32, jnp.bfloat16
VMEM = pl.BlockSpec(memory_space=pltpu.VMEM)
ANY = pl.BlockSpec(memory_space=pl.ANY)
SMEM = pl.BlockSpec(memory_space=pltpu.SMEM)
SMALL = pltpu.CompilerParams(vmem_limit_bytes=8 * 2**20)
LARGE = pltpu.CompilerParams(vmem_limit_bytes=28 * 2**20)


FREE = pl.CostEstimate(flops=0, bytes_accessed=0, transcendentals=0)
def weight_of(x):
    x = float(x)
    return pl.CostEstimate(flops=int(x*1.15e9), bytes_accessed=int(x*3.69e6), transcendentals=0)


def chunk_kernel(first_row, axis, core, place_ref, matrix_ref, *refs):
    out_ref, sem = refs[-2:]
    rows, width = out_ref.shape

    @pl.when((place_ref[axis] == 0) & (place_ref[2] == core))
    def _():
        copy = pltpu.make_async_copy(
            matrix_ref.at[pl.ds(first_row, rows), pl.ds(0, width)], out_ref, sem
        )
        copy.start()
        copy.wait()


def chunk(place, axis, core, matrix, first_row, rows, width, held=None, weight=0, after=()):
    in_specs, operands = [SMEM, ANY], [place, matrix]
    if held is not None:
        in_specs.append(VMEM)
        operands.append(held)
    in_specs += [ANY] * len(after)
    operands += after
    return pl.pallas_call(
        functools.partial(chunk_kernel, first_row, axis, core),
        in_specs=in_specs,
        out_specs=VMEM,
        out_shape=jax.ShapeDtypeStruct((rows, width), BF16),
        scratch_shapes=[pltpu.SemaphoreType.DMA],
        input_output_aliases={} if held is None else {2: 0},
        compiler_params=SMALL,
        cost_estimate=weight_of(weight),
        name="chunk",
    )(*operands)


def columns(number, block):
    return pl.ds(pl.multiple_of(number * block, block), block)


def pick_kernel(place_ref, pivots_ref, matrix_ref, *refs):
    whole_ref, onehot_ref, sem = refs[-3:]
    outs = refs[-3 - PIECES : -3]
    rows, cols = whole_ref.shape
    width = pivots_ref.shape[0]
    block = min(BLOCK, cols)
    count = width // PIECES

    def fetch(number):
        here = columns(number, block)
        return pltpu.make_async_copy(
            matrix_ref.at[:, here], whole_ref.at[:, here], sem.at[number]
        )

    for number in range(cols // block):
        fetch(number).start()
    row = lax.broadcasted_iota(jnp.int32, (width, rows), 1) + place_ref[0] * rows
    onehot_ref[...] = jnp.where(pivots_ref[...] == row, 1.0, 0.0).astype(BF16)

    @pl.loop(0, cols // block)
    def _(number):
        fetch(number).wait()
        here = columns(number, block)
        picked = jnp.dot(onehot_ref[...], whole_ref[:, here], preferred_element_type=F32)
        picked = picked.astype(BF16)
        for piece, out_ref in enumerate(outs):
            out_ref[:, here] = picked[piece * count : (piece + 1) * count]


def pick(place, pivots, matrix, after=()):
    rows, cols = matrix.shape
    width = pivots.shape[0]
    block = min(BLOCK, cols)
    return pl.pallas_call(
        pick_kernel,
        in_specs=[SMEM, VMEM, ANY] + [ANY] * len(after),
        out_specs=[VMEM] * PIECES,
        out_shape=[jax.ShapeDtypeStruct((width // PIECES, cols), BF16)] * PIECES,
        scratch_shapes=[
            pltpu.VMEM((rows, cols), BF16),
            pltpu.VMEM((width, rows), BF16),
            pltpu.SemaphoreType.DMA((cols // block,)),
        ],
        compiler_params=LARGE,
        cost_estimate=weight_of(0),
        name="pick_rows",
    )(place, pivots[:, None], matrix, *after)


def add_kernel(count, *refs):
    start = 0
    out_ref = refs[-1]
    for own_ref, got_ref in zip(refs[:count], refs[count : 2 * count]):
        rows = own_ref.shape[0]
        out_ref[start : start + rows] = own_ref[...] + got_ref[...]
        start += rows


def add(own, got, after=(), weight=0):
    rows, cols = sum(x.shape[0] for x in own), own[0].shape[1]
    return pl.pallas_call(
        functools.partial(add_kernel, len(own)),
        in_specs=[VMEM] * (2 * len(own)) + [ANY] * len(after),
        out_specs=VMEM,
        out_shape=jax.ShapeDtypeStruct((rows, cols), BF16),
        compiler_params=SMALL,
        cost_estimate=weight_of(weight),
        name="add",
    )(*own, *got, *after)


def in_order(core, mine, other, out_ref):
    half = mine.shape[0]
    out_ref[pl.ds(pl.multiple_of(core * half, half), half)] = mine
    out_ref[pl.ds(pl.multiple_of((1 - core) * half, half), half)] = other


def update_kernel(first_row, per_group, pick_source, make_upper, place_ref, pivots_ref,
                  matrix_ref, down_ref, down_got_ref, *refs):
    if make_upper:
        inverse_ref, up_ref, up_got_ref = refs[:3]
        sources = refs[3 : 4 + per_group]
        out_ref, upper_ref = refs[-10:-8]
    else:
        upper_ref = refs[0]
        sources = refs[1 : 2 + per_group]
        out_ref = refs[-9]
    rows_ref, left_ref, right_ref, keep_ref, pivot_rows_ref, in_sem, out_sem, sem = refs[-8:]
    count, cols = rows_ref.shape
    width = left_ref.shape[1] // 2
    row_place, col_place, core, rows = (place_ref[i] for i in range(4))
    block = min(BLOCK, cols)
    piece = min(count, 512)
    here = pl.ds(first_row, count)

    def fetch_panel(action):
        views = [sources[0].at[here, pl.ds(0, width)], *sources[1:]]
        panel_ref = left_ref.at[pl.ds(0, count), pl.ds(width, width)]
        for choice, view in enumerate(views):
            @pl.when(pick_source(col_place, core) == choice)
            def _():
                action(pltpu.make_async_copy(view, panel_ref, sem))

    def fetch(number):
        there = columns(number, block)
        return pltpu.make_async_copy(
            matrix_ref.at[here, there], rows_ref.at[:, there], in_sem.at[number]
        )

    def store(number):
        there = columns(number, block)
        return pltpu.make_async_copy(
            rows_ref.at[:, there], out_ref.at[here, there], out_sem.at[number]
        )

    fetch_panel(lambda copy: copy.start())
    for number in range(cols // block):
        fetch(number).start()
    for start in range(0, count, piece):
        these = slice(start, start + piece)
        row = lax.broadcasted_iota(jnp.int32, (piece, width), 0)
        row = row + (row_place * rows + first_row + start)
        onehot = jnp.where(pivots_ref[...] == row, 1.0, 0.0)
        left_ref[these, :width] = onehot.astype(BF16)
        has_pivot = jnp.max(onehot, axis=1, keepdims=True)
        keep_ref[these] = jnp.broadcast_to(1.0 - has_pivot, (piece, 128))
    fetch_panel(lambda copy: copy.wait())

    @pl.loop(0, cols // block)
    def _(number):
        there = columns(number, block)
        if make_upper:
            in_order(core, up_ref[:, there], up_got_ref[:, there], pivot_rows_ref)
            upper_ref[:, there] = jnp.dot(
                inverse_ref[...], pivot_rows_ref[...], preferred_element_type=F32
            ).astype(BF16)
        fetch(number).wait()

        @pl.when((col_place > 0) | (number * block >= width))
        def _():
            in_order(core, down_ref[:, there], down_got_ref[:, there], right_ref)
            upper = upper_ref[:, there]
            right_ref[width:] = -upper
            right = right_ref[...]
            for start in range(0, count, piece):
                these = slice(start, start + piece)
                change = jnp.dot(left_ref[these], right, preferred_element_type=F32)
                keep = jnp.concatenate([keep_ref[these]] * (block // 128), axis=1)
                kept = rows_ref[these, there].astype(F32) * keep
                rows_ref[these, there] = (kept + change).astype(BF16)
            if first_row < width:
                @pl.when(row_place == 0)
                def _():
                    rows_ref[: width - first_row, there] = upper[first_row:]

        store(number).start()

    for number in range(cols // block):
        store(number).wait()


def update(group, pick_source, place, pivots, matrix, down, down_got, received,
           upper_terms=None, upper=None, out=None):
    first_row, count = group
    rows, cols = matrix.shape
    width = pivots.shape[0]
    make_upper = upper is None
    block = min(BLOCK, cols)
    operands = [place, pivots[None, :], matrix, down, down_got]
    in_specs = [SMEM, VMEM, ANY, VMEM, VMEM]
    terms = list(upper_terms) if make_upper else [upper]
    operands += terms + [matrix] + received
    in_specs += [VMEM] * len(terms) + [ANY] * (1 + len(received))
    hbm = pl.BlockSpec(memory_space=pltpu.HBM)
    aliases = {}
    if out is not None:
        aliases = {len(operands): 0}
        operands.append(out)
        in_specs.append(hbm)
    out_shape = [jax.ShapeDtypeStruct((rows, cols), BF16)]
    if make_upper:
        out_shape.append(jax.ShapeDtypeStruct((width, cols), BF16))
    return pl.pallas_call(
        functools.partial(update_kernel, first_row, len(received), pick_source, make_upper),
        in_specs=in_specs,
        out_specs=[hbm, VMEM][: len(out_shape)],
        out_shape=out_shape,
        scratch_shapes=[
            pltpu.VMEM((count, cols), BF16),
            pltpu.VMEM((count, 2 * width), BF16),
            pltpu.VMEM((2 * width, block), BF16),
            pltpu.VMEM((count, 128), F32),
            pltpu.VMEM((width, block), BF16),
            pltpu.SemaphoreType.DMA((cols // block,)),
            pltpu.SemaphoreType.DMA((cols // block,)),
            pltpu.SemaphoreType.DMA,
        ],
        input_output_aliases=aliases,
        compiler_params=LARGE,
        cost_estimate=weight_of(0),
        name="update_rows",
    )(*operands)


def swap_pairs(size, orders, step):
    return [(i, i ^ (1 << orders[i & 1][step])) for i in range(size)]


def grow_pairs(orders, step):
    pairs = []
    for core, order in enumerate(orders):
        places = [core]
        for bit in order[:step]:
            places += [i | (1 << bit) for i in places]
        pairs += [(i, i | (1 << order[step])) for i in places]
    return pairs


def move(value, pairs, core, n_prow, size):
    pairs = [(row * size + a, row * size + b) for row in range(core, n_prow, 2) for a, b in pairs]
    return lax.ppermute(value, ("prow", "pcol"), pairs)


def send(place, matrix, width, groups, core, n_prow, size):
    middle = size // 2
    held = []
    for number, group in enumerate(groups):
        last = held[-1] if held else None
        sent = chunk(place, 1, core, matrix, *group, width, last, CHUNK_WEIGHTS[number])
        if held:
            held[-1] = sent
        pairs = [(0, middle)] + [(middle, middle - 1)] * bool(held[:1])
        held.append(move(sent, pairs, core, n_prow, size))
    return held


def pass_on(place, held, rights, core, n_prow, size):
    middle = size // 2
    last = move(held[-1], [(middle, middle - 1)], core, n_prow, size)
    received = []
    for number, value in enumerate(held):
        left = held[number + 1] if number + 1 < len(held) else last
        right = rights[number] if number < len(rights) else None
        if right is None:
            right = move(value, [(middle, middle + 1)], core, n_prow, size)
        arrays = [value, left, right]
        both = jnp.where(place[1] < middle, left, right) if size > 4 else None
        distance = 1
        while middle - distance > 1 or middle + distance + 1 < size:
            pairs = []
            if middle - distance > 1:
                pairs.append((middle - distance, middle - distance - 1))
            if middle + distance + 1 < size:
                pairs.append((middle + distance, middle + distance + 1))
            both = move(both, pairs, core, n_prow, size)
            arrays.append(both)
            distance += 1
        received.append(arrays)
    return received


def source_of(size, per_core):
    middle = size // 2

    def pick_source(place, core):
        away = jnp.abs(place - middle)
        number = jnp.where(away == 0, 1, jnp.where(place < middle, 2, 3))
        number = jnp.where(away >= 2, away + 2, number)
        return jnp.where(place == 0, 0, number + core * per_core)

    return pick_source


def per_device(n_prow, n_pcol, matrix, pivots, unit_inverse):
    rows, cols = matrix.shape
    width = unit_inverse.shape[0]
    half = width // 2
    row_place = lax.axis_index("prow")
    col_place = lax.axis_index("pcol")
    core = row_place & 1
    place = jnp.stack([row_place, col_place, core, jnp.full_like(core, rows)]).astype(jnp.int32)
    matrix = pltpu.with_memory_space_constraint(matrix, pltpu.HBM)
    bits = list(range(1, n_prow.bit_length() - 1))
    orders = (bits, bits[::-1])
    cores = ([0], [0])
    last = len(bits) - 1

    size = rows // GROUPS
    groups = [(number * size, size) for number in range(GROUPS)]
    held = [send(place, matrix, width, groups, c, n_prow, n_pcol) for c in range(2)]
    arrived = [x for pair in zip(*held) for x in pair]
    middle = n_pcol // 2
    rights = [
        [move(x, [(middle, middle + 1)], c, n_prow, n_pcol) for x in held[c][: GROUPS - c]]
        for c in range(2)
    ]
    arrived_right = [rights[0][0], rights[1][0]] + rights[0][1:]

    order = jnp.where(core == 0, pivots, jnp.roll(pivots, half))
    down_got = lax.ppermute(chunk(place, 0, 0, matrix, half, half, cols), "prow", [(0, 1)])
    down = chunk(place, 0, 0, matrix, 0, half, cols, down_got)
    pieces = pick(place, order, matrix, [down])
    up, sent = pieces[: PIECES // 2], pieces[PIECES // 2 :]
    up_got = [lax.ppermute(x, "prow", swap_pairs(n_prow, cores, 0)) for x in sent]
    def pins(a, b):
        return arrived[max(a - 2, 0):a] + arrived_right[max(b - 2, 0):b]
    for step in range(last + 1):
        up = [add(up, up_got, pins(*JOIN_AFTER[min(step, 1)]), JOIN_WEIGHTS[min(step, 1)])]
        down_got = lax.ppermute(down, "prow", grow_pairs(orders, step))
        up_got = [lax.ppermute(up[0], "prow", swap_pairs(n_prow, orders, step))]
        down = add([down], [down_got], up + pins(*DOWN_AFTER[min(step, 1)]), DOWN_WEIGHTS[min(step, 1)])
    down_got = lax.ppermute(down, "prow", swap_pairs(n_prow, cores, 0))
    up = add(up, up_got, pins(0, 0), 0)
    up_got = lax.ppermute(up, "prow", swap_pairs(n_prow, cores, 0))

    by_core = [pass_on(place, held[c], rights[c], c, n_prow, n_pcol) for c in range(2)]
    received = [first + second for first, second in zip(*by_core)]
    common = (source_of(n_pcol, len(by_core[0][0])), place, pivots, matrix, down, down_got)
    out, upper = update(groups[0], *common, received[0], upper_terms=(unit_inverse, up, up_got))
    for group, arrays in zip(groups[1:], received[1:]):
        (out,) = update(group, *common, arrays, upper=upper, out=out)
    return out


def solution(mesh):
    return jax.shard_map(
        functools.partial(per_device, mesh.shape["prow"], mesh.shape["pcol"]),
        mesh=mesh,
        in_specs=(P("prow", "pcol"), P(), P()),
        out_specs=P("prow", "pcol"),
        check_vma=False,
    )
```

```python
import functools

import jax
import jax.numpy as jnp
from jax import lax
from jax.experimental import pallas as pl
from jax.experimental.pallas import tpu as pltpu
from jax.sharding import PartitionSpec as P

GROUPS = 2
CHUNK_WEIGHTS = (0, 5)
JOIN_WEIGHTS, JOIN_AFTER = (2, 2), ((1, 0), (3, 1))
DOWN_WEIGHTS, DOWN_AFTER = (0, 20), ((1, 0), (0, 0))
PIECES = 2
BLOCK = 256
F32, BF16 = jnp.float32, jnp.bfloat16
VMEM = pl.BlockSpec(memory_space=pltpu.VMEM)
ANY = pl.BlockSpec(memory_space=pl.ANY)
SMEM = pl.BlockSpec(memory_space=pltpu.SMEM)
SMALL = pltpu.CompilerParams(vmem_limit_bytes=8 * 2**20)
LARGE = pltpu.CompilerParams(vmem_limit_bytes=28 * 2**20)


FREE = pl.CostEstimate(flops=0, bytes_accessed=0, transcendentals=0)
def weight_of(x):
    x = float(x)
    return pl.CostEstimate(flops=int(x*1.15e9), bytes_accessed=int(x*3.69e6), transcendentals=0)


def chunk_kernel(first_row, axis, core, place_ref, matrix_ref, *refs):
    out_ref, sem = refs[-2:]
    rows, width = out_ref.shape

    @pl.when((place_ref[axis] == 0) & (place_ref[2] == core))
    def _():
        copy = pltpu.make_async_copy(
            matrix_ref.at[pl.ds(first_row, rows), pl.ds(0, width)], out_ref, sem
        )
        copy.start()
        copy.wait()


def chunk(place, axis, core, matrix, first_row, rows, width, held=None, weight=0, after=()):
    in_specs, operands = [SMEM, ANY], [place, matrix]
    if held is not None:
        in_specs.append(VMEM)
        operands.append(held)
    in_specs += [ANY] * len(after)
    operands += after
    return pl.pallas_call(
        functools.partial(chunk_kernel, first_row, axis, core),
        in_specs=in_specs,
        out_specs=VMEM,
        out_shape=jax.ShapeDtypeStruct((rows, width), BF16),
        scratch_shapes=[pltpu.SemaphoreType.DMA],
        input_output_aliases={} if held is None else {2: 0},
        compiler_params=SMALL,
        cost_estimate=weight_of(weight),
        name="chunk",
    )(*operands)


def columns(number, block):
    return pl.ds(pl.multiple_of(number * block, block), block)


def pick_kernel(place_ref, pivots_ref, matrix_ref, *refs):
    whole_ref, onehot_ref, sem = refs[-3:]
    outs = refs[-3 - PIECES : -3]
    rows, cols = whole_ref.shape
    width = pivots_ref.shape[0]
    block = min(BLOCK, cols)
    count = width // PIECES

    def fetch(number):
        here = columns(number, block)
        return pltpu.make_async_copy(
            matrix_ref.at[:, here], whole_ref.at[:, here], sem.at[number]
        )

    for number in range(cols // block):
        fetch(number).start()
    row = lax.broadcasted_iota(jnp.int32, (width, rows), 1) + place_ref[0] * rows
    onehot_ref[...] = jnp.where(pivots_ref[...] == row, 1.0, 0.0).astype(BF16)

    @pl.loop(0, cols // block)
    def _(number):
        fetch(number).wait()
        here = columns(number, block)
        picked = jnp.dot(onehot_ref[...], whole_ref[:, here], preferred_element_type=F32)
        picked = picked.astype(BF16)
        for piece, out_ref in enumerate(outs):
            out_ref[:, here] = picked[piece * count : (piece + 1) * count]


def pick(place, pivots, matrix, after=()):
    rows, cols = matrix.shape
    width = pivots.shape[0]
    block = min(BLOCK, cols)
    return pl.pallas_call(
        pick_kernel,
        in_specs=[SMEM, VMEM, ANY] + [ANY] * len(after),
        out_specs=[VMEM] * PIECES,
        out_shape=[jax.ShapeDtypeStruct((width // PIECES, cols), BF16)] * PIECES,
        scratch_shapes=[
            pltpu.VMEM((rows, cols), BF16),
            pltpu.VMEM((width, rows), BF16),
            pltpu.SemaphoreType.DMA((cols // block,)),
        ],
        compiler_params=LARGE,
        cost_estimate=weight_of(0),
        name="pick_rows",
    )(place, pivots[:, None], matrix, *after)


def add_kernel(count, *refs):
    start = 0
    out_ref = refs[-1]
    for own_ref, got_ref in zip(refs[:count], refs[count : 2 * count]):
        rows = own_ref.shape[0]
        out_ref[start : start + rows] = own_ref[...] + got_ref[...]
        start += rows


def add(own, got, after=(), weight=0):
    rows, cols = sum(x.shape[0] for x in own), own[0].shape[1]
    return pl.pallas_call(
        functools.partial(add_kernel, len(own)),
        in_specs=[VMEM] * (2 * len(own)) + [ANY] * len(after),
        out_specs=VMEM,
        out_shape=jax.ShapeDtypeStruct((rows, cols), BF16),
        compiler_params=SMALL,
        cost_estimate=weight_of(weight),
        name="add",
    )(*own, *got, *after)


def in_order(core, mine, other, out_ref):
    half = mine.shape[0]
    out_ref[pl.ds(pl.multiple_of(core * half, half), half)] = mine
    out_ref[pl.ds(pl.multiple_of((1 - core) * half, half), half)] = other


def update_kernel(first_row, per_group, pick_source, make_upper, place_ref, pivots_ref,
                  matrix_ref, down_ref, down_got_ref, *refs):
    if make_upper:
        inverse_ref, up_ref, up_got_ref = refs[:3]
        sources = refs[3 : 4 + per_group]
        out_ref, upper_ref = refs[-10:-8]
    else:
        upper_ref = refs[0]
        sources = refs[1 : 2 + per_group]
        out_ref = refs[-9]
    rows_ref, left_ref, right_ref, keep_ref, pivot_rows_ref, in_sem, out_sem, sem = refs[-8:]
    count, cols = rows_ref.shape
    width = left_ref.shape[1] // 2
    row_place, col_place, core, rows = (place_ref[i] for i in range(4))
    block = min(BLOCK, cols)
    piece = min(count, 512)
    here = pl.ds(first_row, count)

    def fetch_panel(action):
        views = [sources[0].at[here, pl.ds(0, width)], *sources[1:]]
        panel_ref = left_ref.at[pl.ds(0, count), pl.ds(width, width)]
        for choice, view in enumerate(views):
            @pl.when(pick_source(col_place, core) == choice)
            def _():
                action(pltpu.make_async_copy(view, panel_ref, sem))

    def fetch(number):
        there = columns(number, block)
        return pltpu.make_async_copy(
            matrix_ref.at[here, there], rows_ref.at[:, there], in_sem.at[number]
        )

    def store(number):
        there = columns(number, block)
        return pltpu.make_async_copy(
            rows_ref.at[:, there], out_ref.at[here, there], out_sem.at[number]
        )

    fetch_panel(lambda copy: copy.start())
    for number in range(cols // block):
        fetch(number).start()
    for start in range(0, count, piece):
        these = slice(start, start + piece)
        row = lax.broadcasted_iota(jnp.int32, (piece, width), 0)
        row = row + (row_place * rows + first_row + start)
        onehot = jnp.where(pivots_ref[...] == row, 1.0, 0.0)
        left_ref[these, :width] = onehot.astype(BF16)
        has_pivot = jnp.max(onehot, axis=1, keepdims=True)
        keep_ref[these] = jnp.broadcast_to(1.0 - has_pivot, (piece, 128))
    fetch_panel(lambda copy: copy.wait())

    @pl.loop(0, cols // block)
    def _(number):
        there = columns(number, block)
        if make_upper:
            in_order(core, up_ref[:, there], up_got_ref[:, there], pivot_rows_ref)
            upper_ref[:, there] = jnp.dot(
                inverse_ref[...], pivot_rows_ref[...], preferred_element_type=F32
            ).astype(BF16)
        fetch(number).wait()

        @pl.when((col_place > 0) | (number * block >= width))
        def _():
            in_order(core, down_ref[:, there], down_got_ref[:, there], right_ref)
            upper = upper_ref[:, there]
            right_ref[width:] = -upper
            right = right_ref[...]
            for start in range(0, count, piece):
                these = slice(start, start + piece)
                change = jnp.dot(left_ref[these], right, preferred_element_type=F32)
                keep = jnp.concatenate([keep_ref[these]] * (block // 128), axis=1)
                kept = rows_ref[these, there].astype(F32) * keep
                rows_ref[these, there] = (kept + change).astype(BF16)
            if first_row < width:
                @pl.when(row_place == 0)
                def _():
                    rows_ref[: width - first_row, there] = upper[first_row:]

        store(number).start()

    for number in range(cols // block):
        store(number).wait()


def update(group, pick_source, place, pivots, matrix, down, down_got, received,
           upper_terms=None, upper=None, out=None):
    first_row, count = group
    rows, cols = matrix.shape
    width = pivots.shape[0]
    make_upper = upper is None
    block = min(BLOCK, cols)
    operands = [place, pivots[None, :], matrix, down, down_got]
    in_specs = [SMEM, VMEM, ANY, VMEM, VMEM]
    terms = list(upper_terms) if make_upper else [upper]
    operands += terms + [matrix] + received
    in_specs += [VMEM] * len(terms) + [ANY] * (1 + len(received))
    hbm = pl.BlockSpec(memory_space=pltpu.HBM)
    aliases = {}
    if out is not None:
        aliases = {len(operands): 0}
        operands.append(out)
        in_specs.append(hbm)
    out_shape = [jax.ShapeDtypeStruct((rows, cols), BF16)]
    if make_upper:
        out_shape.append(jax.ShapeDtypeStruct((width, cols), BF16))
    return pl.pallas_call(
        functools.partial(update_kernel, first_row, len(received), pick_source, make_upper),
        in_specs=in_specs,
        out_specs=[hbm, VMEM][: len(out_shape)],
        out_shape=out_shape,
        scratch_shapes=[
            pltpu.VMEM((count, cols), BF16),
            pltpu.VMEM((count, 2 * width), BF16),
            pltpu.VMEM((2 * width, block), BF16),
            pltpu.VMEM((count, 128), F32),
            pltpu.VMEM((width, block), BF16),
            pltpu.SemaphoreType.DMA((cols // block,)),
            pltpu.SemaphoreType.DMA((cols // block,)),
            pltpu.SemaphoreType.DMA,
        ],
        input_output_aliases=aliases,
        compiler_params=LARGE,
        cost_estimate=weight_of(0),
        name="update_rows",
    )(*operands)


def swap_pairs(size, orders, step):
    return [(i, i ^ (1 << orders[i & 1][step])) for i in range(size)]


def grow_pairs(orders, step):
    pairs = []
    for core, order in enumerate(orders):
        places = [core]
        for bit in order[:step]:
            places += [i | (1 << bit) for i in places]
        pairs += [(i, i | (1 << order[step])) for i in places]
    return pairs


def move(value, pairs, core, n_prow, size):
    pairs = [(row * size + a, row * size + b) for row in range(core, n_prow, 2) for a, b in pairs]
    return lax.ppermute(value, ("prow", "pcol"), pairs)


def send(place, matrix, width, groups, core, n_prow, size):
    middle = size // 2
    held = []
    for number, group in enumerate(groups):
        last = held[-1] if held else None
        sent = chunk(place, 1, core, matrix, *group, width, last, CHUNK_WEIGHTS[number])
        if held:
            held[-1] = sent
        pairs = [(0, middle)] + [(middle, middle - 1)] * bool(held[:1])
        held.append(move(sent, pairs, core, n_prow, size))
    return held


def pass_on(place, held, rights, core, n_prow, size):
    middle = size // 2
    last = move(held[-1], [(middle, middle - 1)], core, n_prow, size)
    received = []
    for number, value in enumerate(held):
        left = held[number + 1] if number + 1 < len(held) else last
        right = rights[number] if number < len(rights) else None
        if right is None:
            right = move(value, [(middle, middle + 1)], core, n_prow, size)
        arrays = [value, left, right]
        both = jnp.where(place[1] < middle, left, right) if size > 4 else None
        distance = 1
        while middle - distance > 1 or middle + distance + 1 < size:
            pairs = []
            if middle - distance > 1:
                pairs.append((middle - distance, middle - distance - 1))
            if middle + distance + 1 < size:
                pairs.append((middle + distance, middle + distance + 1))
            both = move(both, pairs, core, n_prow, size)
            arrays.append(both)
            distance += 1
        received.append(arrays)
    return received


def source_of(size, per_core):
    middle = size // 2

    def pick_source(place, core):
        away = jnp.abs(place - middle)
        number = jnp.where(away == 0, 1, jnp.where(place < middle, 2, 3))
        number = jnp.where(away >= 2, away + 2, number)
        return jnp.where(place == 0, 0, number + core * per_core)

    return pick_source


def per_device(n_prow, n_pcol, matrix, pivots, unit_inverse):
    rows, cols = matrix.shape
    width = unit_inverse.shape[0]
    half = width // 2
    row_place = lax.axis_index("prow")
    col_place = lax.axis_index("pcol")
    core = row_place & 1
    place = jnp.stack([row_place, col_place, core, jnp.full_like(core, rows)]).astype(jnp.int32)
    matrix = pltpu.with_memory_space_constraint(matrix, pltpu.HBM)
    bits = list(range(1, n_prow.bit_length() - 1))
    orders = (bits, bits[::-1])
    cores = ([0], [0])
    last = len(bits) - 1

    size = rows // GROUPS
    groups = [(number * size, size) for number in range(GROUPS)]
    held = [send(place, matrix, width, groups, c, n_prow, n_pcol) for c in range(2)]
    arrived = [x for pair in zip(*held) for x in pair]
    middle = n_pcol // 2
    rights = [
        [move(x, [(middle, middle + 1)], c, n_prow, n_pcol) for x in held[c][: GROUPS - c]]
        for c in range(2)
    ]
    arrived_right = [rights[0][0], rights[1][0]] + rights[0][1:]

    order = jnp.where(core == 0, pivots, jnp.roll(pivots, half))
    down_got = lax.ppermute(chunk(place, 0, 0, matrix, half, half, cols), "prow", [(0, 1)])
    down = chunk(place, 0, 0, matrix, 0, half, cols, down_got)
    pieces = pick(place, order, matrix, [])
    up, sent = pieces[: PIECES // 2], pieces[PIECES // 2 :]
    up_got = [lax.ppermute(x, "prow", swap_pairs(n_prow, cores, 0)) for x in sent]
    def pins(a, b):
        return arrived[max(a - 2, 0):a] + arrived_right[max(b - 2, 0):b]
    for step in range(last + 1):
        up = [add(up, up_got, pins(*JOIN_AFTER[min(step, 1)]), JOIN_WEIGHTS[min(step, 1)])]
        down_got = lax.ppermute(down, "prow", grow_pairs(orders, step))
        up_got = [lax.ppermute(up[0], "prow", swap_pairs(n_prow, orders, step))]
        down = add([down], [down_got], [] + pins(*DOWN_AFTER[min(step, 1)]), DOWN_WEIGHTS[min(step, 1)])
    down_got = lax.ppermute(down, "prow", swap_pairs(n_prow, cores, 0))
    up = add(up, up_got, pins(0, 0), 0)
    up_got = lax.ppermute(up, "prow", swap_pairs(n_prow, cores, 0))

    by_core = [pass_on(place, held[c], rights[c], c, n_prow, n_pcol) for c in range(2)]
    received = [first + second for first, second in zip(*by_core)]
    common = (source_of(n_pcol, len(by_core[0][0])), place, pivots, matrix, down, down_got)
    out, upper = update(groups[0], *common, received[0], upper_terms=(unit_inverse, up, up_got))
    for group, arrays in zip(groups[1:], received[1:]):
        (out,) = update(group, *common, arrays, upper=upper, out=out)
    return out


def solution(mesh):
    return jax.shard_map(
        functools.partial(per_device, mesh.shape["prow"], mesh.shape["pcol"]),
        mesh=mesh,
        in_specs=(P("prow", "pcol"), P(), P()),
        out_specs=P("prow", "pcol"),
        check_vma=False,
    )
```

```python
import functools

import jax
import jax.numpy as jnp
from jax import lax
from jax.experimental import pallas as pl
from jax.experimental.pallas import tpu as pltpu
from jax.sharding import PartitionSpec as P

GROUPS = 2
CHUNK_WEIGHTS = (0, 5)
JOIN_WEIGHTS, JOIN_AFTER = (2, 2), ((1, 0), (3, 1))
DOWN_WEIGHTS, DOWN_AFTER = (0, 20), ((1, 0), (0, 0))
PIECES = 2
PICK_BLOCK, UPDATE_BLOCK = 256, 512
F32, BF16 = jnp.float32, jnp.bfloat16
VMEM = pl.BlockSpec(memory_space=pltpu.VMEM)
ANY = pl.BlockSpec(memory_space=pl.ANY)
SMEM = pl.BlockSpec(memory_space=pltpu.SMEM)
SMALL = pltpu.CompilerParams(vmem_limit_bytes=8 * 2**20)
LARGE = pltpu.CompilerParams(vmem_limit_bytes=28 * 2**20)


FREE = pl.CostEstimate(flops=0, bytes_accessed=0, transcendentals=0)
def weight_of(x):
    x = float(x)
    return pl.CostEstimate(flops=int(x*1.15e9), bytes_accessed=int(x*3.69e6), transcendentals=0)


def chunk_kernel(first_row, axis, core, place_ref, matrix_ref, *refs):
    out_ref, sem = refs[-2:]
    rows, width = out_ref.shape

    @pl.when((place_ref[axis] == 0) & (place_ref[2] == core))
    def _():
        copy = pltpu.make_async_copy(
            matrix_ref.at[pl.ds(first_row, rows), pl.ds(0, width)], out_ref, sem
        )
        copy.start()
        copy.wait()


def chunk(place, axis, core, matrix, first_row, rows, width, held=None, weight=0, after=()):
    in_specs, operands = [SMEM, ANY], [place, matrix]
    if held is not None:
        in_specs.append(VMEM)
        operands.append(held)
    in_specs += [ANY] * len(after)
    operands += after
    return pl.pallas_call(
        functools.partial(chunk_kernel, first_row, axis, core),
        in_specs=in_specs,
        out_specs=VMEM,
        out_shape=jax.ShapeDtypeStruct((rows, width), BF16),
        scratch_shapes=[pltpu.SemaphoreType.DMA],
        input_output_aliases={} if held is None else {2: 0},
        compiler_params=SMALL,
        cost_estimate=weight_of(weight),
        name="chunk",
    )(*operands)


def columns(number, block):
    return pl.ds(number * block, block)


def pick_kernel(place_ref, pivots_ref, matrix_ref, *refs):
    whole_ref, onehot_ref, sem = refs[-3:]
    outs = refs[-3 - PIECES : -3]
    rows, cols = whole_ref.shape
    width = pivots_ref.shape[0]
    block = min(PICK_BLOCK, cols)
    count = width // PIECES

    def fetch(number):
        here = columns(number, block)
        return pltpu.make_async_copy(
            matrix_ref.at[:, here], whole_ref.at[:, here], sem.at[number]
        )

    for number in range(cols // block):
        fetch(number).start()
    row = lax.broadcasted_iota(jnp.int32, (width, rows), 1) + place_ref[0] * rows
    onehot_ref[...] = jnp.where(pivots_ref[...] == row, 1.0, 0.0).astype(BF16)

    for number in range(cols // block):
        fetch(number).wait()
        here = columns(number, block)
        picked = jnp.dot(onehot_ref[...], whole_ref[:, here], preferred_element_type=F32)
        picked = picked.astype(BF16)
        for piece, out_ref in enumerate(outs):
            out_ref[:, here] = picked[piece * count : (piece + 1) * count]


def pick(place, pivots, matrix, after=()):
    rows, cols = matrix.shape
    width = pivots.shape[0]
    block = min(PICK_BLOCK, cols)
    return pl.pallas_call(
        pick_kernel,
        in_specs=[SMEM, VMEM, ANY] + [ANY] * len(after),
        out_specs=[VMEM] * PIECES,
        out_shape=[jax.ShapeDtypeStruct((width // PIECES, cols), BF16)] * PIECES,
        scratch_shapes=[
            pltpu.VMEM((rows, cols), BF16),
            pltpu.VMEM((width, rows), BF16),
            pltpu.SemaphoreType.DMA((cols // block,)),
        ],
        compiler_params=LARGE,
        cost_estimate=weight_of(0),
        name="pick_rows",
    )(place, pivots[:, None], matrix, *after)


def add_kernel(count, *refs):
    start = 0
    out_ref = refs[-1]
    for own_ref, got_ref in zip(refs[:count], refs[count : 2 * count]):
        rows = own_ref.shape[0]
        out_ref[start : start + rows] = own_ref[...] + got_ref[...]
        start += rows


def add(own, got, after=(), weight=0):
    rows, cols = sum(x.shape[0] for x in own), own[0].shape[1]
    return pl.pallas_call(
        functools.partial(add_kernel, len(own)),
        in_specs=[VMEM] * (2 * len(own)) + [ANY] * len(after),
        out_specs=VMEM,
        out_shape=jax.ShapeDtypeStruct((rows, cols), BF16),
        compiler_params=SMALL,
        cost_estimate=weight_of(weight),
        name="add",
    )(*own, *got, *after)


def in_order(core, mine, other, out_ref):
    half = mine.shape[0]
    out_ref[pl.ds(pl.multiple_of(core * half, half), half)] = mine
    out_ref[pl.ds(pl.multiple_of((1 - core) * half, half), half)] = other


def update_kernel(first_row, per_group, pick_source, make_upper, place_ref, pivots_ref,
                  matrix_ref, down_ref, down_got_ref, *refs):
    if make_upper:
        inverse_ref, up_ref, up_got_ref = refs[:3]
        sources = refs[3 : 4 + per_group]
        out_ref, upper_ref = refs[-10:-8]
    else:
        upper_ref = refs[0]
        sources = refs[1 : 2 + per_group]
        out_ref = refs[-9]
    rows_ref, left_ref, right_ref, keep_ref, pivot_rows_ref, in_sem, out_sem, sem = refs[-8:]
    count, cols = rows_ref.shape
    width = left_ref.shape[1] // 2
    row_place, col_place, core, rows = (place_ref[i] for i in range(4))
    block = min(UPDATE_BLOCK, cols)
    piece = min(count, 512)
    here = pl.ds(first_row, count)

    def fetch_panel(action):
        views = [sources[0].at[here, pl.ds(0, width)], *sources[1:]]
        panel_ref = left_ref.at[pl.ds(0, count), pl.ds(width, width)]
        for choice, view in enumerate(views):
            @pl.when(pick_source(col_place, core) == choice)
            def _():
                action(pltpu.make_async_copy(view, panel_ref, sem))

    def fetch(number):
        there = columns(number, block)
        return pltpu.make_async_copy(
            matrix_ref.at[here, there], rows_ref.at[:, there], in_sem.at[number]
        )

    def store(number):
        there = columns(number, block)
        return pltpu.make_async_copy(
            rows_ref.at[:, there], out_ref.at[here, there], out_sem.at[number]
        )

    fetch_panel(lambda copy: copy.start())
    for number in range(cols // block):
        fetch(number).start()
    for start in range(0, count, piece):
        these = slice(start, start + piece)
        row = lax.broadcasted_iota(jnp.int32, (piece, width), 0)
        row = row + (row_place * rows + first_row + start)
        onehot = jnp.where(pivots_ref[...] == row, 1.0, 0.0)
        left_ref[these, :width] = onehot.astype(BF16)
        has_pivot = jnp.max(onehot, axis=1, keepdims=True)
        keep_ref[these] = jnp.broadcast_to(1.0 - has_pivot, (piece, 128))
    fetch_panel(lambda copy: copy.wait())

    for number in range(cols // block):
        there = columns(number, block)
        if make_upper:
            in_order(core, up_ref[:, there], up_got_ref[:, there], pivot_rows_ref)
            upper_ref[:, there] = jnp.dot(
                inverse_ref[...], pivot_rows_ref[...], preferred_element_type=F32
            ).astype(BF16)
        fetch(number).wait()

        @pl.when((col_place > 0) | (number * block >= width))
        def _():
            in_order(core, down_ref[:, there], down_got_ref[:, there], right_ref)
            upper = upper_ref[:, there]
            right_ref[width:] = -upper
            right = right_ref[...]
            for start in range(0, count, piece):
                these = slice(start, start + piece)
                change = jnp.dot(left_ref[these], right, preferred_element_type=F32)
                keep = jnp.concatenate([keep_ref[these]] * (block // 128), axis=1)
                kept = rows_ref[these, there].astype(F32) * keep
                rows_ref[these, there] = (kept + change).astype(BF16)
            if first_row < width:
                @pl.when(row_place == 0)
                def _():
                    rows_ref[: width - first_row, there] = upper[first_row:]

        store(number).start()

    for number in range(cols // block):
        store(number).wait()


def update(group, pick_source, place, pivots, matrix, down, down_got, received,
           upper_terms=None, upper=None, out=None):
    first_row, count = group
    rows, cols = matrix.shape
    width = pivots.shape[0]
    make_upper = upper is None
    block = min(UPDATE_BLOCK, cols)
    operands = [place, pivots[None, :], matrix, down, down_got]
    in_specs = [SMEM, VMEM, ANY, VMEM, VMEM]
    terms = list(upper_terms) if make_upper else [upper]
    operands += terms + [matrix] + received
    in_specs += [VMEM] * len(terms) + [ANY] * (1 + len(received))
    hbm = pl.BlockSpec(memory_space=pltpu.HBM)
    aliases = {}
    if out is not None:
        aliases = {len(operands): 0}
        operands.append(out)
        in_specs.append(hbm)
    out_shape = [jax.ShapeDtypeStruct((rows, cols), BF16)]
    if make_upper:
        out_shape.append(jax.ShapeDtypeStruct((width, cols), BF16))
    return pl.pallas_call(
        functools.partial(update_kernel, first_row, len(received), pick_source, make_upper),
        in_specs=in_specs,
        out_specs=[hbm, VMEM][: len(out_shape)],
        out_shape=out_shape,
        scratch_shapes=[
            pltpu.VMEM((count, cols), BF16),
            pltpu.VMEM((count, 2 * width), BF16),
            pltpu.VMEM((2 * width, block), BF16),
            pltpu.VMEM((count, 128), F32),
            pltpu.VMEM((width, block), BF16),
            pltpu.SemaphoreType.DMA((cols // block,)),
            pltpu.SemaphoreType.DMA((cols // block,)),
            pltpu.SemaphoreType.DMA,
        ],
        input_output_aliases=aliases,
        compiler_params=LARGE,
        cost_estimate=weight_of(0),
        name="update_rows",
    )(*operands)


def swap_pairs(size, orders, step):
    return [(i, i ^ (1 << orders[i & 1][step])) for i in range(size)]


def grow_pairs(orders, step):
    pairs = []
    for core, order in enumerate(orders):
        places = [core]
        for bit in order[:step]:
            places += [i | (1 << bit) for i in places]
        pairs += [(i, i | (1 << order[step])) for i in places]
    return pairs


def move(value, pairs, core, n_prow, size):
    pairs = [(row * size + a, row * size + b) for row in range(core, n_prow, 2) for a, b in pairs]
    return lax.ppermute(value, ("prow", "pcol"), pairs)


def send(place, matrix, width, groups, core, n_prow, size):
    middle = size // 2
    held = []
    for number, group in enumerate(groups):
        last = held[-1] if held else None
        sent = chunk(place, 1, core, matrix, *group, width, last, CHUNK_WEIGHTS[number])
        if held:
            held[-1] = sent
        pairs = [(0, middle)] + [(middle, middle - 1)] * bool(held[:1])
        held.append(move(sent, pairs, core, n_prow, size))
    return held


def pass_on(place, held, rights, core, n_prow, size):
    middle = size // 2
    last = move(held[-1], [(middle, middle - 1)], core, n_prow, size)
    received = []
    for number, value in enumerate(held):
        left = held[number + 1] if number + 1 < len(held) else last
        right = rights[number] if number < len(rights) else None
        if right is None:
            right = move(value, [(middle, middle + 1)], core, n_prow, size)
        arrays = [value, left, right]
        both = jnp.where(place[1] < middle, left, right) if size > 4 else None
        distance = 1
        while middle - distance > 1 or middle + distance + 1 < size:
            pairs = []
            if middle - distance > 1:
                pairs.append((middle - distance, middle - distance - 1))
            if middle + distance + 1 < size:
                pairs.append((middle + distance, middle + distance + 1))
            both = move(both, pairs, core, n_prow, size)
            arrays.append(both)
            distance += 1
        received.append(arrays)
    return received


def source_of(size, per_core):
    middle = size // 2

    def pick_source(place, core):
        away = jnp.abs(place - middle)
        number = jnp.where(away == 0, 1, jnp.where(place < middle, 2, 3))
        number = jnp.where(away >= 2, away + 2, number)
        return jnp.where(place == 0, 0, number + core * per_core)

    return pick_source


def per_device(n_prow, n_pcol, matrix, pivots, unit_inverse):
    rows, cols = matrix.shape
    width = unit_inverse.shape[0]
    half = width // 2
    row_place = lax.axis_index("prow")
    col_place = lax.axis_index("pcol")
    core = row_place & 1
    place = jnp.stack([row_place, col_place, core, jnp.full_like(core, rows)]).astype(jnp.int32)
    matrix = pltpu.with_memory_space_constraint(matrix, pltpu.HBM)
    bits = list(range(1, n_prow.bit_length() - 1))
    orders = (bits, bits[::-1])
    cores = ([0], [0])
    last = len(bits) - 1

    size = rows // GROUPS
    groups = [(number * size, size) for number in range(GROUPS)]
    held = [send(place, matrix, width, groups, c, n_prow, n_pcol) for c in range(2)]
    arrived = [x for pair in zip(*held) for x in pair]
    middle = n_pcol // 2
    rights = [
        [move(x, [(middle, middle + 1)], c, n_prow, n_pcol) for x in held[c][: GROUPS - c]]
        for c in range(2)
    ]
    arrived_right = [rights[0][0], rights[1][0]] + rights[0][1:]

    order = jnp.where(core == 0, pivots, jnp.roll(pivots, half))
    down_got = lax.ppermute(chunk(place, 0, 0, matrix, half, half, cols), "prow", [(0, 1)])
    down = chunk(place, 0, 0, matrix, 0, half, cols, down_got)
    pieces = pick(place, order, matrix, [])
    up, sent = pieces[: PIECES // 2], pieces[PIECES // 2 :]
    up_got = [lax.ppermute(x, "prow", swap_pairs(n_prow, cores, 0)) for x in sent]
    def pins(a, b):
        return arrived[max(a - 2, 0):a] + arrived_right[max(b - 2, 0):b]
    for step in range(last + 1):
        up = [add(up, up_got, pins(*JOIN_AFTER[min(step, 1)]), JOIN_WEIGHTS[min(step, 1)])]
        down_got = lax.ppermute(down, "prow", grow_pairs(orders, step))
        up_got = [lax.ppermute(up[0], "prow", swap_pairs(n_prow, orders, step))]
        down = add([down], [down_got], [] + pins(*DOWN_AFTER[min(step, 1)]), DOWN_WEIGHTS[min(step, 1)])
    down_got = lax.ppermute(down, "prow", swap_pairs(n_prow, cores, 0))
    up = add(up, up_got, pins(0, 0), 0)
    up_got = lax.ppermute(up, "prow", swap_pairs(n_prow, cores, 0))

    by_core = [pass_on(place, held[c], rights[c], c, n_prow, n_pcol) for c in range(2)]
    received = [first + second for first, second in zip(*by_core)]
    common = (source_of(n_pcol, len(by_core[0][0])), place, pivots, matrix, down, down_got)
    out, upper = update(groups[0], *common, received[0], upper_terms=(unit_inverse, up, up_got))
    for group, arrays in zip(groups[1:], received[1:]):
        (out,) = update(group, *common, arrays, upper=upper, out=out)
    return out


def solution(mesh):
    return jax.shard_map(
        functools.partial(per_device, mesh.shape["prow"], mesh.shape["pcol"]),
        mesh=mesh,
        in_specs=(P("prow", "pcol"), P(), P()),
        out_specs=P("prow", "pcol"),
        check_vma=False,
    )
```

```python
import functools

import jax
import jax.numpy as jnp
from jax import lax
from jax.experimental import pallas as pl
from jax.experimental.pallas import tpu as pltpu
from jax.sharding import PartitionSpec as P

GROUPS = 2
CHUNK_WEIGHTS = (0, 5)
JOIN_WEIGHTS, JOIN_AFTER = (2, 2), ((1, 0), (3, 1))
DOWN_WEIGHTS, DOWN_AFTER = (0, 20), ((1, 0), (0, 0))
PIECES = 2
PICK_BLOCK, UPDATE_BLOCK = 256, 512
F32, BF16 = jnp.float32, jnp.bfloat16
VMEM = pl.BlockSpec(memory_space=pltpu.VMEM)
ANY = pl.BlockSpec(memory_space=pl.ANY)
SMEM = pl.BlockSpec(memory_space=pltpu.SMEM)
SMALL = pltpu.CompilerParams(vmem_limit_bytes=8 * 2**20)
LARGE = pltpu.CompilerParams(vmem_limit_bytes=28 * 2**20)


FREE = pl.CostEstimate(flops=0, bytes_accessed=0, transcendentals=0)
def weight_of(x):
    x = float(x)
    return pl.CostEstimate(flops=int(x*1.15e9), bytes_accessed=int(x*3.69e6), transcendentals=0)


def chunk_kernel(first_row, axis, core, place_ref, matrix_ref, *refs):
    out_ref, sem = refs[-2:]
    rows, width = out_ref.shape

    @pl.when((place_ref[axis] == 0) & (place_ref[2] == core))
    def _():
        copy = pltpu.make_async_copy(
            matrix_ref.at[pl.ds(first_row, rows), pl.ds(0, width)], out_ref, sem
        )
        copy.start()
        copy.wait()


def chunk(place, axis, core, matrix, first_row, rows, width, held=None, weight=0, after=()):
    in_specs, operands = [SMEM, ANY], [place, matrix]
    if held is not None:
        in_specs.append(VMEM)
        operands.append(held)
    in_specs += [ANY] * len(after)
    operands += after
    return pl.pallas_call(
        functools.partial(chunk_kernel, first_row, axis, core),
        in_specs=in_specs,
        out_specs=VMEM,
        out_shape=jax.ShapeDtypeStruct((rows, width), BF16),
        scratch_shapes=[pltpu.SemaphoreType.DMA],
        input_output_aliases={} if held is None else {2: 0},
        compiler_params=SMALL,
        cost_estimate=weight_of(weight),
        name="chunk",
    )(*operands)


def columns(number, block):
    return pl.ds(pl.multiple_of(number * block, block), block)


def pick_kernel(place_ref, pivots_ref, matrix_ref, *refs):
    whole_ref, onehot_ref, sem = refs[-3:]
    outs = refs[-3 - PIECES : -3]
    rows, cols = whole_ref.shape
    width = pivots_ref.shape[0]
    block = min(PICK_BLOCK, cols)
    count = width // PIECES

    def fetch(number):
        here = columns(number, block)
        return pltpu.make_async_copy(
            matrix_ref.at[:, here], whole_ref.at[:, here], sem.at[number]
        )

    for number in range(cols // block):
        fetch(number).start()
    row = lax.broadcasted_iota(jnp.int32, (width, rows), 1) + place_ref[0] * rows
    onehot_ref[...] = jnp.where(pivots_ref[...] == row, 1.0, 0.0).astype(BF16)

    @pl.loop(0, cols // block)
    def _(number):
        fetch(number).wait()
        here = columns(number, block)
        picked = jnp.dot(onehot_ref[...], whole_ref[:, here], preferred_element_type=F32)
        picked = picked.astype(BF16)
        for piece, out_ref in enumerate(outs):
            out_ref[:, here] = picked[piece * count : (piece + 1) * count]


def pick(place, pivots, matrix, after=()):
    rows, cols = matrix.shape
    width = pivots.shape[0]
    block = min(PICK_BLOCK, cols)
    return pl.pallas_call(
        pick_kernel,
        in_specs=[SMEM, VMEM, ANY] + [ANY] * len(after),
        out_specs=[VMEM] * PIECES,
        out_shape=[jax.ShapeDtypeStruct((width // PIECES, cols), BF16)] * PIECES,
        scratch_shapes=[
            pltpu.VMEM((rows, cols), BF16),
            pltpu.VMEM((width, rows), BF16),
            pltpu.SemaphoreType.DMA((cols // block,)),
        ],
        compiler_params=LARGE,
        cost_estimate=weight_of(0),
        name="pick_rows",
    )(place, pivots[:, None], matrix, *after)


def add_kernel(count, *refs):
    start = 0
    out_ref = refs[-1]
    for own_ref, got_ref in zip(refs[:count], refs[count : 2 * count]):
        rows = own_ref.shape[0]
        out_ref[start : start + rows] = own_ref[...] + got_ref[...]
        start += rows


def add(own, got, after=(), weight=0):
    rows, cols = sum(x.shape[0] for x in own), own[0].shape[1]
    return pl.pallas_call(
        functools.partial(add_kernel, len(own)),
        in_specs=[VMEM] * (2 * len(own)) + [ANY] * len(after),
        out_specs=VMEM,
        out_shape=jax.ShapeDtypeStruct((rows, cols), BF16),
        compiler_params=SMALL,
        cost_estimate=weight_of(weight),
        name="add",
    )(*own, *got, *after)


def in_order(core, mine, other, out_ref):
    half = mine.shape[0]
    out_ref[pl.ds(pl.multiple_of(core * half, half), half)] = mine
    out_ref[pl.ds(pl.multiple_of((1 - core) * half, half), half)] = other


def update_kernel(first_row, per_group, pick_source, make_upper, place_ref, pivots_ref,
                  matrix_ref, down_ref, down_got_ref, *refs):
    if make_upper:
        inverse_ref, up_ref, up_got_ref = refs[:3]
        sources = refs[3 : 4 + per_group]
        out_ref, upper_ref = refs[-10:-8]
    else:
        upper_ref = refs[0]
        sources = refs[1 : 2 + per_group]
        out_ref = refs[-9]
    rows_ref, left_ref, right_ref, keep_ref, pivot_rows_ref, in_sem, out_sem, sem = refs[-8:]
    count, cols = rows_ref.shape
    width = left_ref.shape[1] // 2
    row_place, col_place, core, rows = (place_ref[i] for i in range(4))
    block = min(UPDATE_BLOCK, cols)
    piece = min(count, 512)
    here = pl.ds(first_row, count)

    def fetch_panel(action):
        views = [sources[0].at[here, pl.ds(0, width)], *sources[1:]]
        panel_ref = left_ref.at[pl.ds(0, count), pl.ds(width, width)]
        for choice, view in enumerate(views):
            @pl.when(pick_source(col_place, core) == choice)
            def _():
                action(pltpu.make_async_copy(view, panel_ref, sem))

    def fetch(number):
        there = columns(number, block)
        return pltpu.make_async_copy(
            matrix_ref.at[here, there], rows_ref.at[:, there], in_sem.at[number]
        )

    def store(number):
        there = columns(number, block)
        return pltpu.make_async_copy(
            rows_ref.at[:, there], out_ref.at[here, there], out_sem.at[number]
        )

    fetch_panel(lambda copy: copy.start())
    for number in range(cols // block):
        fetch(number).start()
    for start in range(0, count, piece):
        these = slice(start, start + piece)
        row = lax.broadcasted_iota(jnp.int32, (piece, width), 0)
        row = row + (row_place * rows + first_row + start)
        onehot = jnp.where(pivots_ref[...] == row, 1.0, 0.0)
        left_ref[these, :width] = onehot.astype(BF16)
        has_pivot = jnp.max(onehot, axis=1, keepdims=True)
        keep_ref[these] = jnp.broadcast_to(1.0 - has_pivot, (piece, 128))
    fetch_panel(lambda copy: copy.wait())

    @pl.loop(0, cols // block)
    def _(number):
        there = columns(number, block)
        if make_upper:
            in_order(core, up_ref[:, there], up_got_ref[:, there], pivot_rows_ref)
            upper_ref[:, there] = jnp.dot(
                inverse_ref[...], pivot_rows_ref[...], preferred_element_type=F32
            ).astype(BF16)
        fetch(number).wait()

        @pl.when((col_place > 0) | (number * block >= width))
        def _():
            in_order(core, down_ref[:, there], down_got_ref[:, there], right_ref)
            upper = upper_ref[:, there]
            right_ref[width:] = -upper
            right = right_ref[...]
            for start in range(0, count, piece):
                these = slice(start, start + piece)
                change = jnp.dot(left_ref[these], right, preferred_element_type=F32)
                keep = jnp.concatenate([keep_ref[these]] * (block // 128), axis=1)
                kept = rows_ref[these, there].astype(F32) * keep
                rows_ref[these, there] = (kept + change).astype(BF16)
            if first_row < width:
                @pl.when(row_place == 0)
                def _():
                    rows_ref[: width - first_row, there] = upper[first_row:]

        store(number).start()

    for number in range(cols // block):
        store(number).wait()


def update(group, pick_source, place, pivots, matrix, down, down_got, received,
           upper_terms=None, upper=None, out=None):
    first_row, count = group
    rows, cols = matrix.shape
    width = pivots.shape[0]
    make_upper = upper is None
    block = min(UPDATE_BLOCK, cols)
    operands = [place, pivots[None, :], matrix, down, down_got]
    in_specs = [SMEM, VMEM, ANY, VMEM, VMEM]
    terms = list(upper_terms) if make_upper else [upper]
    operands += terms + [matrix] + received
    in_specs += [VMEM] * len(terms) + [ANY] * (1 + len(received))
    hbm = pl.BlockSpec(memory_space=pltpu.HBM)
    aliases = {}
    if out is not None:
        aliases = {len(operands): 0}
        operands.append(out)
        in_specs.append(hbm)
    out_shape = [jax.ShapeDtypeStruct((rows, cols), BF16)]
    if make_upper:
        out_shape.append(jax.ShapeDtypeStruct((width, cols), BF16))
    return pl.pallas_call(
        functools.partial(update_kernel, first_row, len(received), pick_source, make_upper),
        in_specs=in_specs,
        out_specs=[hbm, VMEM][: len(out_shape)],
        out_shape=out_shape,
        scratch_shapes=[
            pltpu.VMEM((count, cols), BF16),
            pltpu.VMEM((count, 2 * width), BF16),
            pltpu.VMEM((2 * width, block), BF16),
            pltpu.VMEM((count, 128), F32),
            pltpu.VMEM((width, block), BF16),
            pltpu.SemaphoreType.DMA((cols // block,)),
            pltpu.SemaphoreType.DMA((cols // block,)),
            pltpu.SemaphoreType.DMA,
        ],
        input_output_aliases=aliases,
        compiler_params=LARGE,
        cost_estimate=weight_of(0),
        name="update_rows",
    )(*operands)


def swap_pairs(size, orders, step):
    return [(i, i ^ (1 << orders[i & 1][step])) for i in range(size)]


def grow_pairs(orders, step):
    pairs = []
    for core, order in enumerate(orders):
        places = [core]
        for bit in order[:step]:
            places += [i | (1 << bit) for i in places]
        pairs += [(i, i | (1 << order[step])) for i in places]
    return pairs


def move(value, pairs, core, n_prow, size):
    pairs = [(row * size + a, row * size + b) for row in range(core, n_prow, 2) for a, b in pairs]
    return lax.ppermute(value, ("prow", "pcol"), pairs)


def send(place, matrix, width, groups, core, n_prow, size):
    middle = size // 2
    held = []
    for number, group in enumerate(groups):
        last = held[-1] if held else None
        sent = chunk(place, 1, core, matrix, *group, width, last, CHUNK_WEIGHTS[number])
        if held:
            held[-1] = sent
        pairs = [(0, middle)] + [(middle, middle - 1)] * bool(held[:1])
        held.append(move(sent, pairs, core, n_prow, size))
    return held


def pass_on(place, held, rights, core, n_prow, size):
    middle = size // 2
    last = move(held[-1], [(middle, middle - 1)], core, n_prow, size)
    received = []
    for number, value in enumerate(held):
        left = held[number + 1] if number + 1 < len(held) else last
        right = rights[number] if number < len(rights) else None
        if right is None:
            right = move(value, [(middle, middle + 1)], core, n_prow, size)
        arrays = [value, left, right]
        both = jnp.where(place[1] < middle, left, right) if size > 4 else None
        distance = 1
        while middle - distance > 1 or middle + distance + 1 < size:
            pairs = []
            if middle - distance > 1:
                pairs.append((middle - distance, middle - distance - 1))
            if middle + distance + 1 < size:
                pairs.append((middle + distance, middle + distance + 1))
            both = move(both, pairs, core, n_prow, size)
            arrays.append(both)
            distance += 1
        received.append(arrays)
    return received


def source_of(size, per_core):
    middle = size // 2

    def pick_source(place, core):
        away = jnp.abs(place - middle)
        number = jnp.where(away == 0, 1, jnp.where(place < middle, 2, 3))
        number = jnp.where(away >= 2, away + 2, number)
        return jnp.where(place == 0, 0, number + core * per_core)

    return pick_source


def per_device(n_prow, n_pcol, matrix, pivots, unit_inverse):
    rows, cols = matrix.shape
    width = unit_inverse.shape[0]
    half = width // 2
    row_place = lax.axis_index("prow")
    col_place = lax.axis_index("pcol")
    core = row_place & 1
    place = jnp.stack([row_place, col_place, core, jnp.full_like(core, rows)]).astype(jnp.int32)
    matrix = pltpu.with_memory_space_constraint(matrix, pltpu.HBM)
    bits = list(range(1, n_prow.bit_length() - 1))
    orders = (bits, bits[::-1])
    cores = ([0], [0])
    last = len(bits) - 1

    size = rows // GROUPS
    groups = [(number * size, size) for number in range(GROUPS)]
    held = [send(place, matrix, width, groups, c, n_prow, n_pcol) for c in range(2)]
    arrived = [x for pair in zip(*held) for x in pair]
    middle = n_pcol // 2
    rights = [
        [move(x, [(middle, middle + 1)], c, n_prow, n_pcol) for x in held[c][: GROUPS - c]]
        for c in range(2)
    ]
    arrived_right = [rights[0][0], rights[1][0]] + rights[0][1:]

    order = jnp.where(core == 0, pivots, jnp.roll(pivots, half))
    down_got = lax.ppermute(chunk(place, 0, 0, matrix, half, half, cols), "prow", [(0, 1)])
    down = chunk(place, 0, 0, matrix, 0, half, cols, down_got)
    pieces = pick(place, order, matrix, [])
    up, sent = pieces[: PIECES // 2], pieces[PIECES // 2 :]
    up_got = [lax.ppermute(x, "prow", swap_pairs(n_prow, cores, 0)) for x in sent]
    def pins(a, b):
        return arrived[max(a - 2, 0):a] + arrived_right[max(b - 2, 0):b]
    for step in range(last + 1):
        up = [add(up, up_got, pins(*JOIN_AFTER[min(step, 1)]), JOIN_WEIGHTS[min(step, 1)])]
        down_got = lax.ppermute(down, "prow", grow_pairs(orders, step))
        up_got = [lax.ppermute(up[0], "prow", swap_pairs(n_prow, orders, step))]
        down = add([down], [down_got], [] + pins(*DOWN_AFTER[min(step, 1)]), DOWN_WEIGHTS[min(step, 1)])
    down_got = lax.ppermute(down, "prow", swap_pairs(n_prow, cores, 0))
    up = add(up, up_got, pins(0, 0), 0)
    up_got = lax.ppermute(up, "prow", swap_pairs(n_prow, cores, 0))

    by_core = [pass_on(place, held[c], rights[c], c, n_prow, n_pcol) for c in range(2)]
    received = [first + second for first, second in zip(*by_core)]
    common = (source_of(n_pcol, len(by_core[0][0])), place, pivots, matrix, down, down_got)
    out, upper = update(groups[0], *common, received[0], upper_terms=(unit_inverse, up, up_got))
    for group, arrays in zip(groups[1:], received[1:]):
        (out,) = update(group, *common, arrays, upper=upper, out=out)
    return out


def solution(mesh):
    return jax.shard_map(
        functools.partial(per_device, mesh.shape["prow"], mesh.shape["pcol"]),
        mesh=mesh,
        in_specs=(P("prow", "pcol"), P(), P()),
        out_specs=P("prow", "pcol"),
        check_vma=False,
    )
```

```python
import functools

import jax
import jax.numpy as jnp
from jax import lax
from jax.experimental import pallas as pl
from jax.experimental.pallas import tpu as pltpu
from jax.sharding import PartitionSpec as P

GROUPS = 2
CHUNK_WEIGHTS = (0, 5)
JOIN_WEIGHTS, JOIN_AFTER = (2, 2), ((1, 0), (3, 1))
DOWN_WEIGHTS, DOWN_AFTER = (0, 20), ((1, 0), (0, 0))
PIECES = 2
PICK_BLOCK, UPDATE_BLOCK = 256, 512
COPIES = 4
F32, BF16 = jnp.float32, jnp.bfloat16
VMEM = pl.BlockSpec(memory_space=pltpu.VMEM)
ANY = pl.BlockSpec(memory_space=pl.ANY)
SMEM = pl.BlockSpec(memory_space=pltpu.SMEM)
SMALL = pltpu.CompilerParams(vmem_limit_bytes=8 * 2**20)
LARGE = pltpu.CompilerParams(vmem_limit_bytes=28 * 2**20)


FREE = pl.CostEstimate(flops=0, bytes_accessed=0, transcendentals=0)
def weight_of(x):
    x = float(x)
    return pl.CostEstimate(flops=int(x*1.15e9), bytes_accessed=int(x*3.69e6), transcendentals=0)


def row_copies(source, target, sem):
    rows = target.shape[0] // COPIES
    return [
        pltpu.make_async_copy(
            source.at[pl.ds(part * rows, rows)], target.at[pl.ds(part * rows, rows)], sem.at[part]
        )
        for part in range(COPIES)
    ]


def chunk_kernel(first_row, axis, core, place_ref, matrix_ref, *refs):
    out_ref, sem = refs[-2:]
    rows, width = out_ref.shape

    @pl.when((place_ref[axis] == 0) & (place_ref[2] == core))
    def _():
        view = matrix_ref.at[pl.ds(first_row, rows), pl.ds(0, width)]
        copies = row_copies(view, out_ref, sem)
        for copy in copies:
            copy.start()
        for copy in copies:
            copy.wait()


def chunk(place, axis, core, matrix, first_row, rows, width, held=None, weight=0, after=()):
    in_specs, operands = [SMEM, ANY], [place, matrix]
    if held is not None:
        in_specs.append(VMEM)
        operands.append(held)
    in_specs += [ANY] * len(after)
    operands += after
    return pl.pallas_call(
        functools.partial(chunk_kernel, first_row, axis, core),
        in_specs=in_specs,
        out_specs=VMEM,
        out_shape=jax.ShapeDtypeStruct((rows, width), BF16),
        scratch_shapes=[pltpu.SemaphoreType.DMA((COPIES,))],
        input_output_aliases={} if held is None else {2: 0},
        compiler_params=SMALL,
        cost_estimate=weight_of(weight),
        name="chunk",
    )(*operands)


def columns(number, block):
    return pl.ds(pl.multiple_of(number * block, block), block)


def pick_kernel(place_ref, pivots_ref, matrix_ref, *refs):
    whole_ref, onehot_ref, sem = refs[-3:]
    outs = refs[-3 - PIECES : -3]
    rows, cols = whole_ref.shape
    width = pivots_ref.shape[0]
    block = min(PICK_BLOCK, cols)
    count = width // PIECES

    def fetch(number):
        here = columns(number, block)
        return pltpu.make_async_copy(
            matrix_ref.at[:, here], whole_ref.at[:, here], sem.at[number]
        )

    for number in range(cols // block):
        fetch(number).start()
    row = lax.broadcasted_iota(jnp.int32, (width, rows), 1) + place_ref[0] * rows
    onehot_ref[...] = jnp.where(pivots_ref[...] == row, 1.0, 0.0).astype(BF16)

    @pl.loop(0, cols // block)
    def _(number):
        fetch(number).wait()
        here = columns(number, block)
        picked = jnp.dot(onehot_ref[...], whole_ref[:, here], preferred_element_type=F32)
        picked = picked.astype(BF16)
        for piece, out_ref in enumerate(outs):
            out_ref[:, here] = picked[piece * count : (piece + 1) * count]


def pick(place, pivots, matrix, after=()):
    rows, cols = matrix.shape
    width = pivots.shape[0]
    block = min(PICK_BLOCK, cols)
    return pl.pallas_call(
        pick_kernel,
        in_specs=[SMEM, VMEM, ANY] + [ANY] * len(after),
        out_specs=[VMEM] * PIECES,
        out_shape=[jax.ShapeDtypeStruct((width // PIECES, cols), BF16)] * PIECES,
        scratch_shapes=[
            pltpu.VMEM((rows, cols), BF16),
            pltpu.VMEM((width, rows), BF16),
            pltpu.SemaphoreType.DMA((cols // block,)),
        ],
        compiler_params=LARGE,
        cost_estimate=weight_of(0),
        name="pick_rows",
    )(place, pivots[:, None], matrix, *after)


def add_kernel(count, *refs):
    start = 0
    out_ref = refs[-1]
    for own_ref, got_ref in zip(refs[:count], refs[count : 2 * count]):
        rows = own_ref.shape[0]
        out_ref[start : start + rows] = own_ref[...] + got_ref[...]
        start += rows


def add(own, got, after=(), weight=0):
    rows, cols = sum(x.shape[0] for x in own), own[0].shape[1]
    return pl.pallas_call(
        functools.partial(add_kernel, len(own)),
        in_specs=[VMEM] * (2 * len(own)) + [ANY] * len(after),
        out_specs=VMEM,
        out_shape=jax.ShapeDtypeStruct((rows, cols), BF16),
        compiler_params=SMALL,
        cost_estimate=weight_of(weight),
        name="add",
    )(*own, *got, *after)


def in_order(core, mine, other, out_ref):
    half = mine.shape[0]
    out_ref[pl.ds(pl.multiple_of(core * half, half), half)] = mine
    out_ref[pl.ds(pl.multiple_of((1 - core) * half, half), half)] = other


def update_kernel(first_row, per_group, pick_source, make_upper, place_ref, pivots_ref,
                  matrix_ref, down_ref, down_got_ref, *refs):
    if make_upper:
        inverse_ref, up_ref, up_got_ref = refs[:3]
        sources = refs[3 : 4 + per_group]
        out_ref, upper_ref = refs[-10:-8]
    else:
        upper_ref = refs[0]
        sources = refs[1 : 2 + per_group]
        out_ref = refs[-9]
    rows_ref, left_ref, right_ref, keep_ref, pivot_rows_ref, in_sem, out_sem, sem = refs[-8:]
    count, cols = rows_ref.shape
    width = left_ref.shape[1] // 2
    row_place, col_place, core, rows = (place_ref[i] for i in range(4))
    block = min(UPDATE_BLOCK, cols)
    piece = min(count, 512)
    here = pl.ds(first_row, count)

    def fetch_panel(action):
        views = [sources[0].at[here, pl.ds(0, width)], *sources[1:]]
        panel_ref = left_ref.at[pl.ds(0, count), pl.ds(width, width)]
        for choice, view in enumerate(views):
            @pl.when(pick_source(col_place, core) == choice)
            def _():
                for copy in row_copies(view, panel_ref, sem):
                    action(copy)

    def fetch(number):
        there = columns(number, block)
        return pltpu.make_async_copy(
            matrix_ref.at[here, there], rows_ref.at[:, there], in_sem.at[number]
        )

    def store(number):
        there = columns(number, block)
        return pltpu.make_async_copy(
            rows_ref.at[:, there], out_ref.at[here, there], out_sem.at[number]
        )

    fetch_panel(lambda copy: copy.start())
    for number in range(cols // block):
        fetch(number).start()
    for start in range(0, count, piece):
        these = slice(start, start + piece)
        row = lax.broadcasted_iota(jnp.int32, (piece, width), 0)
        row = row + (row_place * rows + first_row + start)
        onehot = jnp.where(pivots_ref[...] == row, 1.0, 0.0)
        left_ref[these, :width] = onehot.astype(BF16)
        has_pivot = jnp.max(onehot, axis=1, keepdims=True)
        keep_ref[these] = jnp.broadcast_to(1.0 - has_pivot, (piece, 128))
    fetch_panel(lambda copy: copy.wait())

    @pl.loop(0, cols // block)
    def _(number):
        there = columns(number, block)
        if make_upper:
            in_order(core, up_ref[:, there], up_got_ref[:, there], pivot_rows_ref)
            upper_ref[:, there] = jnp.dot(
                inverse_ref[...], pivot_rows_ref[...], preferred_element_type=F32
            ).astype(BF16)
        fetch(number).wait()

        @pl.when((col_place > 0) | (number * block >= width))
        def _():
            in_order(core, down_ref[:, there], down_got_ref[:, there], right_ref)
            upper = upper_ref[:, there]
            right_ref[width:] = -upper
            right = right_ref[...]
            for start in range(0, count, piece):
                these = slice(start, start + piece)
                change = jnp.dot(left_ref[these], right, preferred_element_type=F32)
                keep = jnp.concatenate([keep_ref[these]] * (block // 128), axis=1)
                kept = rows_ref[these, there].astype(F32) * keep
                rows_ref[these, there] = (kept + change).astype(BF16)
            if first_row < width:
                @pl.when(row_place == 0)
                def _():
                    rows_ref[: width - first_row, there] = upper[first_row:]

        store(number).start()

    for number in range(cols // block):
        store(number).wait()


def update(group, pick_source, place, pivots, matrix, down, down_got, received,
           upper_terms=None, upper=None, out=None):
    first_row, count = group
    rows, cols = matrix.shape
    width = pivots.shape[0]
    make_upper = upper is None
    block = min(UPDATE_BLOCK, cols)
    operands = [place, pivots[None, :], matrix, down, down_got]
    in_specs = [SMEM, VMEM, ANY, VMEM, VMEM]
    terms = list(upper_terms) if make_upper else [upper]
    operands += terms + [matrix] + received
    in_specs += [VMEM] * len(terms) + [ANY] * (1 + len(received))
    hbm = pl.BlockSpec(memory_space=pltpu.HBM)
    aliases = {}
    if out is not None:
        aliases = {len(operands): 0}
        operands.append(out)
        in_specs.append(hbm)
    out_shape = [jax.ShapeDtypeStruct((rows, cols), BF16)]
    if make_upper:
        out_shape.append(jax.ShapeDtypeStruct((width, cols), BF16))
    return pl.pallas_call(
        functools.partial(update_kernel, first_row, len(received), pick_source, make_upper),
        in_specs=in_specs,
        out_specs=[hbm, VMEM][: len(out_shape)],
        out_shape=out_shape,
        scratch_shapes=[
            pltpu.VMEM((count, cols), BF16),
            pltpu.VMEM((count, 2 * width), BF16),
            pltpu.VMEM((2 * width, block), BF16),
            pltpu.VMEM((count, 128), F32),
            pltpu.VMEM((width, block), BF16),
            pltpu.SemaphoreType.DMA((cols // block,)),
            pltpu.SemaphoreType.DMA((cols // block,)),
            pltpu.SemaphoreType.DMA((COPIES,)),
        ],
        input_output_aliases=aliases,
        compiler_params=LARGE,
        cost_estimate=weight_of(0),
        name="update_rows",
    )(*operands)


def swap_pairs(size, orders, step):
    return [(i, i ^ (1 << orders[i & 1][step])) for i in range(size)]


def grow_pairs(orders, step):
    pairs = []
    for core, order in enumerate(orders):
        places = [core]
        for bit in order[:step]:
            places += [i | (1 << bit) for i in places]
        pairs += [(i, i | (1 << order[step])) for i in places]
    return pairs


def move(value, pairs, core, n_prow, size):
    pairs = [(row * size + a, row * size + b) for row in range(core, n_prow, 2) for a, b in pairs]
    return lax.ppermute(value, ("prow", "pcol"), pairs)


def send(place, matrix, width, groups, core, n_prow, size):
    middle = size // 2
    held = []
    for number, group in enumerate(groups):
        last = held[-1] if held else None
        sent = chunk(place, 1, core, matrix, *group, width, last, CHUNK_WEIGHTS[number])
        if held:
            held[-1] = sent
        pairs = [(0, middle)] + [(middle, middle - 1)] * bool(held[:1])
        held.append(move(sent, pairs, core, n_prow, size))
    return held


def pass_on(place, held, rights, core, n_prow, size):
    middle = size // 2
    last = move(held[-1], [(middle, middle - 1)], core, n_prow, size)
    received = []
    for number, value in enumerate(held):
        left = held[number + 1] if number + 1 < len(held) else last
        right = rights[number] if number < len(rights) else None
        if right is None:
            right = move(value, [(middle, middle + 1)], core, n_prow, size)
        arrays = [value, left, right]
        both = jnp.where(place[1] < middle, left, right) if size > 4 else None
        distance = 1
        while middle - distance > 1 or middle + distance + 1 < size:
            pairs = []
            if middle - distance > 1:
                pairs.append((middle - distance, middle - distance - 1))
            if middle + distance + 1 < size:
                pairs.append((middle + distance, middle + distance + 1))
            both = move(both, pairs, core, n_prow, size)
            arrays.append(both)
            distance += 1
        received.append(arrays)
    return received


def source_of(size, per_core):
    middle = size // 2

    def pick_source(place, core):
        away = jnp.abs(place - middle)
        number = jnp.where(away == 0, 1, jnp.where(place < middle, 2, 3))
        number = jnp.where(away >= 2, away + 2, number)
        return jnp.where(place == 0, 0, number + core * per_core)

    return pick_source


def per_device(n_prow, n_pcol, matrix, pivots, unit_inverse):
    rows, cols = matrix.shape
    width = unit_inverse.shape[0]
    half = width // 2
    row_place = lax.axis_index("prow")
    col_place = lax.axis_index("pcol")
    core = row_place & 1
    place = jnp.stack([row_place, col_place, core, jnp.full_like(core, rows)]).astype(jnp.int32)
    matrix = pltpu.with_memory_space_constraint(matrix, pltpu.HBM)
    bits = list(range(1, n_prow.bit_length() - 1))
    orders = (bits, bits[::-1])
    cores = ([0], [0])
    last = len(bits) - 1

    size = rows // GROUPS
    groups = [(number * size, size) for number in range(GROUPS)]
    held = [send(place, matrix, width, groups, c, n_prow, n_pcol) for c in range(2)]
    arrived = [x for pair in zip(*held) for x in pair]
    middle = n_pcol // 2
    rights = [
        [move(x, [(middle, middle + 1)], c, n_prow, n_pcol) for x in held[c][: GROUPS - c]]
        for c in range(2)
    ]
    arrived_right = [rights[0][0], rights[1][0]] + rights[0][1:]

    order = jnp.where(core == 0, pivots, jnp.roll(pivots, half))
    down_got = lax.ppermute(chunk(place, 0, 0, matrix, half, half, cols), "prow", [(0, 1)])
    down = chunk(place, 0, 0, matrix, 0, half, cols, down_got)
    pieces = pick(place, order, matrix, [])
    up, sent = pieces[: PIECES // 2], pieces[PIECES // 2 :]
    up_got = [lax.ppermute(x, "prow", swap_pairs(n_prow, cores, 0)) for x in sent]
    def pins(a, b):
        return arrived[max(a - 2, 0):a] + arrived_right[max(b - 2, 0):b]
    for step in range(last + 1):
        up = [add(up, up_got, pins(*JOIN_AFTER[min(step, 1)]), JOIN_WEIGHTS[min(step, 1)])]
        down_got = lax.ppermute(down, "prow", grow_pairs(orders, step))
        up_got = [lax.ppermute(up[0], "prow", swap_pairs(n_prow, orders, step))]
        down = add([down], [down_got], [] + pins(*DOWN_AFTER[min(step, 1)]), DOWN_WEIGHTS[min(step, 1)])
    down_got = lax.ppermute(down, "prow", swap_pairs(n_prow, cores, 0))
    up = add(up, up_got, pins(0, 0), 0)
    up_got = lax.ppermute(up, "prow", swap_pairs(n_prow, cores, 0))

    by_core = [pass_on(place, held[c], rights[c], c, n_prow, n_pcol) for c in range(2)]
    received = [first + second for first, second in zip(*by_core)]
    common = (source_of(n_pcol, len(by_core[0][0])), place, pivots, matrix, down, down_got)
    out, upper = update(groups[0], *common, received[0], upper_terms=(unit_inverse, up, up_got))
    for group, arrays in zip(groups[1:], received[1:]):
        (out,) = update(group, *common, arrays, upper=upper, out=out)
    return out


def solution(mesh):
    return jax.shard_map(
        functools.partial(per_device, mesh.shape["prow"], mesh.shape["pcol"]),
        mesh=mesh,
        in_specs=(P("prow", "pcol"), P(), P()),
        out_specs=P("prow", "pcol"),
        check_vma=False,
    )
```

```python
import functools

import jax
import jax.numpy as jnp
from jax import lax
from jax.experimental import pallas as pl
from jax.experimental.pallas import tpu as pltpu
from jax.sharding import PartitionSpec as P

GROUPS = 2
CHUNK_WEIGHTS = (0, 5)
JOIN_WEIGHTS, JOIN_AFTER = (2, 2), ((1, 0), (3, 1))
DOWN_WEIGHTS, DOWN_AFTER = (0, 20), ((1, 0), (0, 0))
PIECES = 2
PICK_BLOCK, UPDATE_BLOCK = 256, 512
COPIES = 4
F32, BF16 = jnp.float32, jnp.bfloat16
VMEM = pl.BlockSpec(memory_space=pltpu.VMEM)
ANY = pl.BlockSpec(memory_space=pl.ANY)
SMEM = pl.BlockSpec(memory_space=pltpu.SMEM)
SMALL = pltpu.CompilerParams(vmem_limit_bytes=8 * 2**20)
LARGE = pltpu.CompilerParams(vmem_limit_bytes=28 * 2**20)


FREE = pl.CostEstimate(flops=0, bytes_accessed=0, transcendentals=0)
def weight_of(x):
    x = float(x)
    return pl.CostEstimate(flops=int(x*1.15e9), bytes_accessed=int(x*3.69e6), transcendentals=0)


def row_copies(source, target, sem):
    rows = target.shape[0] // COPIES
    return [
        pltpu.make_async_copy(
            source.at[pl.ds(part * rows, rows)], target.at[pl.ds(part * rows, rows)], sem.at[part]
        )
        for part in range(COPIES)
    ]


def chunk_kernel(first_row, axis, core, place_ref, matrix_ref, *refs):
    out_ref, sem = refs[-2:]
    rows, width = out_ref.shape

    @pl.when((place_ref[axis] == 0) & (place_ref[2] == core))
    def _():
        view = matrix_ref.at[pl.ds(first_row, rows), pl.ds(0, width)]
        copies = row_copies(view, out_ref, sem)
        for copy in copies:
            copy.start()
        for copy in copies:
            copy.wait()


def chunk(place, axis, core, matrix, first_row, rows, width, held=None, weight=0, after=()):
    in_specs, operands = [SMEM, ANY], [place, matrix]
    if held is not None:
        in_specs.append(VMEM)
        operands.append(held)
    in_specs += [ANY] * len(after)
    operands += after
    return pl.pallas_call(
        functools.partial(chunk_kernel, first_row, axis, core),
        in_specs=in_specs,
        out_specs=VMEM,
        out_shape=jax.ShapeDtypeStruct((rows, width), BF16),
        scratch_shapes=[pltpu.SemaphoreType.DMA((COPIES,))],
        input_output_aliases={} if held is None else {2: 0},
        compiler_params=SMALL,
        cost_estimate=weight_of(weight),
        name="chunk",
    )(*operands)


def columns(number, block):
    return pl.ds(pl.multiple_of(number * block, block), block)


def pick_kernel(place_ref, pivots_ref, matrix_ref, *refs):
    whole_ref, onehot_ref, sem = refs[-3:]
    outs = refs[-3 - PIECES : -3]
    rows, cols = whole_ref.shape
    width = pivots_ref.shape[0]
    block = min(PICK_BLOCK, cols)
    count = width // PIECES

    def fetch(number):
        here = columns(number, block)
        return pltpu.make_async_copy(
            matrix_ref.at[:, here], whole_ref.at[:, here], sem.at[number]
        )

    for number in range(cols // block):
        fetch(number).start()
    row = lax.broadcasted_iota(jnp.int32, (width, rows), 1) + place_ref[0] * rows
    onehot_ref[...] = jnp.where(pivots_ref[...] == row, 1.0, 0.0).astype(BF16)

    @pl.loop(0, cols // block)
    def _(number):
        fetch(number).wait()
        here = columns(number, block)
        picked = jnp.dot(onehot_ref[...], whole_ref[:, here], preferred_element_type=F32)
        picked = picked.astype(BF16)
        for piece, out_ref in enumerate(outs):
            out_ref[:, here] = picked[piece * count : (piece + 1) * count]


def pick(place, pivots, matrix, after=()):
    rows, cols = matrix.shape
    width = pivots.shape[0]
    block = min(PICK_BLOCK, cols)
    return pl.pallas_call(
        pick_kernel,
        in_specs=[SMEM, VMEM, ANY] + [ANY] * len(after),
        out_specs=[VMEM] * PIECES,
        out_shape=[jax.ShapeDtypeStruct((width // PIECES, cols), BF16)] * PIECES,
        scratch_shapes=[
            pltpu.VMEM((rows, cols), BF16),
            pltpu.VMEM((width, rows), BF16),
            pltpu.SemaphoreType.DMA((cols // block,)),
        ],
        compiler_params=LARGE,
        cost_estimate=weight_of(0),
        name="pick_rows",
    )(place, pivots[:, None], matrix, *after)


def add_kernel(count, *refs):
    start = 0
    out_ref = refs[-1]
    for own_ref, got_ref in zip(refs[:count], refs[count : 2 * count]):
        rows = own_ref.shape[0]
        out_ref[start : start + rows] = own_ref[...] + got_ref[...]
        start += rows


def add(own, got, after=(), weight=0):
    rows, cols = sum(x.shape[0] for x in own), own[0].shape[1]
    return pl.pallas_call(
        functools.partial(add_kernel, len(own)),
        in_specs=[VMEM] * (2 * len(own)) + [ANY] * len(after),
        out_specs=VMEM,
        out_shape=jax.ShapeDtypeStruct((rows, cols), BF16),
        compiler_params=SMALL,
        cost_estimate=weight_of(weight),
        name="add",
    )(*own, *got, *after)


def in_order(core, mine, other, out_ref):
    half = mine.shape[0]
    out_ref[pl.ds(pl.multiple_of(core * half, half), half)] = mine
    out_ref[pl.ds(pl.multiple_of((1 - core) * half, half), half)] = other


def update_kernel(first_row, per_group, pick_source, make_upper, place_ref, pivots_ref,
                  matrix_ref, down_ref, down_got_ref, *refs):
    if make_upper:
        inverse_ref, up_ref, up_got_ref = refs[:3]
        sources = refs[3 : 4 + per_group]
        out_ref, upper_ref = refs[-10:-8]
    else:
        upper_ref = refs[0]
        sources = refs[1 : 2 + per_group]
        out_ref = refs[-9]
    rows_ref, left_ref, right_ref, keep_ref, pivot_rows_ref, in_sem, out_sem, sem = refs[-8:]
    count, cols = rows_ref.shape
    width = left_ref.shape[1] // 2
    row_place, col_place, core, rows = (place_ref[i] for i in range(4))
    block = min(UPDATE_BLOCK, cols)
    piece = min(count, 512)
    here = pl.ds(first_row, count)

    def fetch_panel(action):
        views = [sources[0].at[here, pl.ds(0, width)], *sources[1:]]
        panel_ref = left_ref.at[pl.ds(0, count), pl.ds(width, width)]
        for choice, view in enumerate(views):
            @pl.when(pick_source(col_place, core) == choice)
            def _():
                for copy in row_copies(view, panel_ref, sem):
                    action(copy)

    def fetch(number):
        there = columns(number, block)
        return pltpu.make_async_copy(
            matrix_ref.at[here, there], rows_ref.at[:, there], in_sem.at[number]
        )

    def store(number):
        there = columns(number, block)
        return pltpu.make_async_copy(
            rows_ref.at[:, there], out_ref.at[here, there], out_sem.at[number]
        )

    fetch_panel(lambda copy: copy.start())
    for number in range(cols // block):
        fetch(number).start()
    for start in range(0, count, piece):
        these = slice(start, start + piece)
        row = lax.broadcasted_iota(jnp.int32, (piece, width), 0)
        row = row + (row_place * rows + first_row + start)
        onehot = jnp.where(pivots_ref[...] == row, 1.0, 0.0)
        left_ref[these, :width] = onehot.astype(BF16)
        has_pivot = jnp.max(onehot, axis=1, keepdims=True)
        keep_ref[these] = jnp.broadcast_to(1.0 - has_pivot, (piece, 128))
    fetch_panel(lambda copy: copy.wait())

    @pl.loop(0, cols // block)
    def _(number):
        there = columns(number, block)
        if make_upper:
            in_order(core, up_ref[:, there], up_got_ref[:, there], pivot_rows_ref)
            upper_ref[:, there] = jnp.dot(
                inverse_ref[...], pivot_rows_ref[...], preferred_element_type=F32
            ).astype(BF16)
        fetch(number).wait()

        @pl.when((col_place > 0) | (number * block >= width))
        def _():
            in_order(core, down_ref[:, there], down_got_ref[:, there], right_ref)
            upper = upper_ref[:, there]
            right_ref[width:] = -upper
            right = right_ref[...]
            for start in range(0, count, piece):
                these = slice(start, start + piece)
                change = jnp.dot(left_ref[these], right, preferred_element_type=F32)
                keep = jnp.concatenate([keep_ref[these]] * (block // 128), axis=1)
                kept = rows_ref[these, there].astype(F32) * keep
                rows_ref[these, there] = (kept + change).astype(BF16)
            if first_row < width:
                @pl.when(row_place == 0)
                def _():
                    rows_ref[: width - first_row, there] = upper[first_row:]

        store(number).start()

    for number in range(cols // block):
        store(number).wait()


def update(group, pick_source, place, pivots, matrix, down, down_got, received,
           upper_terms=None, upper=None, out=None):
    first_row, count = group
    rows, cols = matrix.shape
    width = pivots.shape[0]
    make_upper = upper is None
    block = min(UPDATE_BLOCK, cols)
    operands = [place, pivots[None, :], matrix, down, down_got]
    in_specs = [SMEM, VMEM, ANY, VMEM, VMEM]
    terms = list(upper_terms) if make_upper else [upper]
    operands += terms + [matrix] + received
    in_specs += [VMEM] * len(terms) + [ANY] * (1 + len(received))
    hbm = pl.BlockSpec(memory_space=pltpu.HBM)
    aliases = {}
    if out is not None:
        aliases = {len(operands): 0}
        operands.append(out)
        in_specs.append(hbm)
    out_shape = [jax.ShapeDtypeStruct((rows, cols), BF16)]
    if make_upper:
        out_shape.append(jax.ShapeDtypeStruct((width, cols), BF16))
    return pl.pallas_call(
        functools.partial(update_kernel, first_row, len(received), pick_source, make_upper),
        in_specs=in_specs,
        out_specs=[hbm, VMEM][: len(out_shape)],
        out_shape=out_shape,
        scratch_shapes=[
            pltpu.VMEM((count, cols), BF16),
            pltpu.VMEM((count, 2 * width), BF16),
            pltpu.VMEM((2 * width, block), BF16),
            pltpu.VMEM((count, 128), F32),
            pltpu.VMEM((width, block), BF16),
            pltpu.SemaphoreType.DMA((cols // block,)),
            pltpu.SemaphoreType.DMA((cols // block,)),
            pltpu.SemaphoreType.DMA((COPIES,)),
        ],
        input_output_aliases=aliases,
        compiler_params=LARGE,
        cost_estimate=weight_of(0),
        name="update_rows",
    )(*operands)


def swap_kernel(first_row, place_ref, pivots_ref, matrix_ref, down_ref, down_got_ref, out_ref,
                onehot_ref, right_ref, keep_ref, sem):
    count, cols = out_ref.shape
    width = pivots_ref.shape[1]
    row_place, col_place, core, rows = (place_ref[i] for i in range(4))
    block = min(UPDATE_BLOCK, cols)
    piece = min(count, 512)

    def fetch(number):
        there = columns(number, block)
        return pltpu.make_async_copy(
            matrix_ref.at[pl.ds(first_row, count), there], out_ref.at[:, there], sem.at[number]
        )

    for number in range(cols // block):
        fetch(number).start()
    for start in range(0, count, piece):
        these = slice(start, start + piece)
        row = lax.broadcasted_iota(jnp.int32, (piece, width), 0)
        row = row + (row_place * rows + first_row + start)
        onehot = jnp.where(pivots_ref[...] == row, 1.0, 0.0)
        onehot_ref[these] = onehot.astype(BF16)
        has_pivot = jnp.max(onehot, axis=1, keepdims=True)
        keep_ref[these] = jnp.broadcast_to(1.0 - has_pivot, (piece, 128))

    @pl.loop(0, cols // block)
    def _(number):
        there = columns(number, block)
        fetch(number).wait()

        @pl.when((col_place > 0) | (number * block >= width))
        def _():
            in_order(core, down_ref[:, there], down_got_ref[:, there], right_ref)
            right = right_ref[...]
            for start in range(0, count, piece):
                these = slice(start, start + piece)
                moved = jnp.dot(onehot_ref[these], right, preferred_element_type=F32)
                keep = jnp.concatenate([keep_ref[these]] * (block // 128), axis=1)
                kept = out_ref[these, there].astype(F32) * keep
                out_ref[these, there] = (kept + moved).astype(BF16)


def swap(group, place, pivots, matrix, down, down_got):
    first_row, count = group
    cols = matrix.shape[1]
    width = pivots.shape[0]
    block = min(UPDATE_BLOCK, cols)
    return pl.pallas_call(
        functools.partial(swap_kernel, first_row),
        in_specs=[SMEM, VMEM, ANY, VMEM, VMEM],
        out_specs=VMEM,
        out_shape=jax.ShapeDtypeStruct((count, cols), BF16),
        scratch_shapes=[
            pltpu.VMEM((count, width), BF16),
            pltpu.VMEM((width, block), BF16),
            pltpu.VMEM((count, 128), F32),
            pltpu.SemaphoreType.DMA((cols // block,)),
        ],
        compiler_params=LARGE,
        cost_estimate=FREE,
        name="swap_rows",
    )(place, pivots[None, :], matrix, down, down_got)


def finish_kernel(first_row, per_group, pick_source, place_ref, matrix_ref, swapped_ref,
                  upper_ref, *refs):
    sources = [matrix_ref, *refs[:per_group]]
    out_ref, rows_ref, panel_ref, out_sem, sem = refs[-5:]
    count, width = panel_ref.shape
    cols = rows_ref.shape[1]
    row_place, col_place, core = (place_ref[i] for i in range(3))
    block = min(UPDATE_BLOCK, cols)
    piece = min(count, 512)
    here = pl.ds(first_row, count)

    def fetch_panel(action):
        views = [sources[0].at[here, pl.ds(0, width)], *sources[1:]]
        for choice, view in enumerate(views):
            @pl.when(pick_source(col_place, core) == choice)
            def _():
                for copy in row_copies(view, panel_ref, sem):
                    action(copy)

    def store(number):
        there = columns(number, block)
        return pltpu.make_async_copy(
            rows_ref.at[:, there], out_ref.at[here, there], out_sem.at[number]
        )

    fetch_panel(lambda copy: copy.start())
    fetch_panel(lambda copy: copy.wait())

    @pl.loop(0, cols // block)
    def _(number):
        there = columns(number, block)
        updated = (col_place > 0) | (number * block >= width)

        @pl.when(jnp.logical_not(updated))
        def _():
            rows_ref[:, there] = swapped_ref[:, there]

        @pl.when(updated)
        def _():
            upper = upper_ref[:, there]
            for start in range(0, count, piece):
                these = slice(start, start + piece)
                product = jnp.dot(panel_ref[these], upper, preferred_element_type=F32)
                left = swapped_ref[these, there].astype(F32) - product
                rows_ref[these, there] = left.astype(BF16)
            if first_row < width:
                @pl.when(row_place == 0)
                def _():
                    rows_ref[: width - first_row, there] = upper[first_row:]

        store(number).start()

    for number in range(cols // block):
        store(number).wait()


def finish(group, pick_source, place, matrix, swapped, upper, received, out):
    first_row, count = group
    rows, cols = matrix.shape
    width = upper.shape[0]
    block = min(UPDATE_BLOCK, cols)
    hbm = pl.BlockSpec(memory_space=pltpu.HBM)
    return pl.pallas_call(
        functools.partial(finish_kernel, first_row, len(received), pick_source),
        in_specs=[SMEM, ANY, VMEM, VMEM] + [ANY] * len(received) + [hbm],
        out_specs=hbm,
        out_shape=jax.ShapeDtypeStruct((rows, cols), BF16),
        scratch_shapes=[
            pltpu.VMEM((count, cols), BF16),
            pltpu.VMEM((count, width), BF16),
            pltpu.SemaphoreType.DMA((cols // block,)),
            pltpu.SemaphoreType.DMA((COPIES,)),
        ],
        input_output_aliases={4 + len(received): 0},
        compiler_params=LARGE,
        cost_estimate=FREE,
        name="finish_rows",
    )(place, matrix, swapped, upper, *received, out)


def swap_pairs(size, orders, step):
    return [(i, i ^ (1 << orders[i & 1][step])) for i in range(size)]


def grow_pairs(orders, step):
    pairs = []
    for core, order in enumerate(orders):
        places = [core]
        for bit in order[:step]:
            places += [i | (1 << bit) for i in places]
        pairs += [(i, i | (1 << order[step])) for i in places]
    return pairs


def move(value, pairs, core, n_prow, size):
    pairs = [(row * size + a, row * size + b) for row in range(core, n_prow, 2) for a, b in pairs]
    return lax.ppermute(value, ("prow", "pcol"), pairs)


def send(place, matrix, width, groups, core, n_prow, size):
    middle = size // 2
    held = []
    for number, group in enumerate(groups):
        last = held[-1] if held else None
        sent = chunk(place, 1, core, matrix, *group, width, last, CHUNK_WEIGHTS[number])
        if held:
            held[-1] = sent
        pairs = [(0, middle)] + [(middle, middle - 1)] * bool(held[:1])
        held.append(move(sent, pairs, core, n_prow, size))
    return held


def pass_on(place, held, rights, core, n_prow, size):
    middle = size // 2
    last = move(held[-1], [(middle, middle - 1)], core, n_prow, size)
    received = []
    for number, value in enumerate(held):
        left = held[number + 1] if number + 1 < len(held) else last
        right = rights[number] if number < len(rights) else None
        if right is None:
            right = move(value, [(middle, middle + 1)], core, n_prow, size)
        arrays = [value, left, right]
        both = jnp.where(place[1] < middle, left, right) if size > 4 else None
        distance = 1
        while middle - distance > 1 or middle + distance + 1 < size:
            pairs = []
            if middle - distance > 1:
                pairs.append((middle - distance, middle - distance - 1))
            if middle + distance + 1 < size:
                pairs.append((middle + distance, middle + distance + 1))
            both = move(both, pairs, core, n_prow, size)
            arrays.append(both)
            distance += 1
        received.append(arrays)
    return received


def source_of(size, per_core):
    middle = size // 2

    def pick_source(place, core):
        away = jnp.abs(place - middle)
        number = jnp.where(away == 0, 1, jnp.where(place < middle, 2, 3))
        number = jnp.where(away >= 2, away + 2, number)
        return jnp.where(place == 0, 0, number + core * per_core)

    return pick_source


def per_device(n_prow, n_pcol, matrix, pivots, unit_inverse):
    rows, cols = matrix.shape
    width = unit_inverse.shape[0]
    half = width // 2
    row_place = lax.axis_index("prow")
    col_place = lax.axis_index("pcol")
    core = row_place & 1
    place = jnp.stack([row_place, col_place, core, jnp.full_like(core, rows)]).astype(jnp.int32)
    matrix = pltpu.with_memory_space_constraint(matrix, pltpu.HBM)
    bits = list(range(1, n_prow.bit_length() - 1))
    orders = (bits, bits[::-1])
    cores = ([0], [0])
    last = len(bits) - 1

    size = rows // GROUPS
    groups = [(number * size, size) for number in range(GROUPS)]
    held = [send(place, matrix, width, groups, c, n_prow, n_pcol) for c in range(2)]
    arrived = [x for pair in zip(*held) for x in pair]
    middle = n_pcol // 2
    rights = [
        [move(x, [(middle, middle + 1)], c, n_prow, n_pcol) for x in held[c][: GROUPS - c]]
        for c in range(2)
    ]
    arrived_right = [rights[0][0], rights[1][0]] + rights[0][1:]

    order = jnp.where(core == 0, pivots, jnp.roll(pivots, half))
    down_got = lax.ppermute(chunk(place, 0, 0, matrix, half, half, cols), "prow", [(0, 1)])
    down = chunk(place, 0, 0, matrix, 0, half, cols, down_got)
    pieces = pick(place, order, matrix, [])
    up, sent = pieces[: PIECES // 2], pieces[PIECES // 2 :]
    up_got = [lax.ppermute(x, "prow", swap_pairs(n_prow, cores, 0)) for x in sent]
    def pins(a, b):
        return arrived[max(a - 2, 0):a] + arrived_right[max(b - 2, 0):b]
    for step in range(last + 1):
        up = [add(up, up_got, pins(*JOIN_AFTER[min(step, 1)]), JOIN_WEIGHTS[min(step, 1)])]
        down_got = lax.ppermute(down, "prow", grow_pairs(orders, step))
        up_got = [lax.ppermute(up[0], "prow", swap_pairs(n_prow, orders, step))]
        down = add([down], [down_got], [] + pins(*DOWN_AFTER[min(step, 1)]), DOWN_WEIGHTS[min(step, 1)])
    down_got = lax.ppermute(down, "prow", swap_pairs(n_prow, cores, 0))
    up = add(up, up_got, pins(0, 0), 0)
    up_got = lax.ppermute(up, "prow", swap_pairs(n_prow, cores, 0))

    by_core = [pass_on(place, held[c], rights[c], c, n_prow, n_pcol) for c in range(2)]
    received = [first + second for first, second in zip(*by_core)]
    common = (source_of(n_pcol, len(by_core[0][0])), place, pivots, matrix, down, down_got)
    out, upper = update(groups[0], *common, received[0], upper_terms=(unit_inverse, up, up_got))
    for group, arrays in zip(groups[1:-1], received[1:-1]):
        (out,) = update(group, *common, arrays, upper=upper, out=out)
    swapped = swap(groups[-1], *common[1:])
    return finish(
        groups[-1], common[0], place, matrix, swapped, upper, received[-1], out
    )


def solution(mesh):
    return jax.shard_map(
        functools.partial(per_device, mesh.shape["prow"], mesh.shape["pcol"]),
        mesh=mesh,
        in_specs=(P("prow", "pcol"), P(), P()),
        out_specs=P("prow", "pcol"),
        check_vma=False,
    )
```

```python
import functools

import jax
import jax.numpy as jnp
from jax import lax
from jax.experimental import pallas as pl
from jax.experimental.pallas import tpu as pltpu
from jax.sharding import PartitionSpec as P

GROUPS = 2
CHUNK_WEIGHTS = (0, 5)
JOIN_WEIGHTS, JOIN_AFTER = (2, 2), ((1, 0), (3, 1))
DOWN_WEIGHTS, DOWN_AFTER = (0, 20), ((1, 0), (0, 0))
PIECES = 2
PICK_BLOCK, UPDATE_BLOCK = 256, 512
COPIES = 4
F32, BF16 = jnp.float32, jnp.bfloat16
VMEM = pl.BlockSpec(memory_space=pltpu.VMEM)
ANY = pl.BlockSpec(memory_space=pl.ANY)
SMEM = pl.BlockSpec(memory_space=pltpu.SMEM)
SMALL = pltpu.CompilerParams(vmem_limit_bytes=8 * 2**20)
LARGE = pltpu.CompilerParams(vmem_limit_bytes=28 * 2**20)


FREE = pl.CostEstimate(flops=0, bytes_accessed=0, transcendentals=0)
def weight_of(x):
    x = float(x)
    return pl.CostEstimate(flops=int(x*1.15e9), bytes_accessed=int(x*3.69e6), transcendentals=0)


def row_copies(source, target, sem):
    rows = target.shape[0] // COPIES
    return [
        pltpu.make_async_copy(
            source.at[pl.ds(part * rows, rows)], target.at[pl.ds(part * rows, rows)], sem.at[part]
        )
        for part in range(COPIES)
    ]


def chunk_kernel(first_row, axis, core, place_ref, matrix_ref, *refs):
    out_ref, sem = refs[-2:]
    rows, width = out_ref.shape

    @pl.when((place_ref[axis] == 0) & (place_ref[2] == core))
    def _():
        view = matrix_ref.at[pl.ds(first_row, rows), pl.ds(0, width)]
        copies = row_copies(view, out_ref, sem)
        for copy in copies:
            copy.start()
        for copy in copies:
            copy.wait()


def chunk(place, axis, core, matrix, first_row, rows, width, held=None, weight=0, after=()):
    in_specs, operands = [SMEM, ANY], [place, matrix]
    if held is not None:
        in_specs.append(VMEM)
        operands.append(held)
    in_specs += [ANY] * len(after)
    operands += after
    return pl.pallas_call(
        functools.partial(chunk_kernel, first_row, axis, core),
        in_specs=in_specs,
        out_specs=VMEM,
        out_shape=jax.ShapeDtypeStruct((rows, width), BF16),
        scratch_shapes=[pltpu.SemaphoreType.DMA((COPIES,))],
        input_output_aliases={} if held is None else {2: 0},
        compiler_params=SMALL,
        cost_estimate=weight_of(weight),
        name="chunk",
    )(*operands)


def columns(number, block):
    return pl.ds(pl.multiple_of(number * block, block), block)


def pick_kernel(place_ref, pivots_ref, matrix_ref, *refs):
    whole_ref, onehot_ref, sem = refs[-3:]
    outs = refs[-3 - PIECES : -3]
    rows, cols = whole_ref.shape
    width = pivots_ref.shape[0]
    block = min(PICK_BLOCK, cols)
    count = width // PIECES

    def fetch(number):
        here = columns(number, block)
        return pltpu.make_async_copy(
            matrix_ref.at[:, here], whole_ref.at[:, here], sem.at[number]
        )

    for number in range(cols // block):
        fetch(number).start()
    row = lax.broadcasted_iota(jnp.int32, (width, rows), 1) + place_ref[0] * rows
    onehot_ref[...] = jnp.where(pivots_ref[...] == row, 1.0, 0.0).astype(BF16)

    @pl.loop(0, cols // block)
    def _(number):
        fetch(number).wait()
        here = columns(number, block)
        picked = jnp.dot(onehot_ref[...], whole_ref[:, here], preferred_element_type=F32)
        picked = picked.astype(BF16)
        for piece, out_ref in enumerate(outs):
            out_ref[:, here] = picked[piece * count : (piece + 1) * count]


def pick(place, pivots, matrix, after=()):
    rows, cols = matrix.shape
    width = pivots.shape[0]
    block = min(PICK_BLOCK, cols)
    return pl.pallas_call(
        pick_kernel,
        in_specs=[SMEM, VMEM, ANY] + [ANY] * len(after),
        out_specs=[VMEM] * PIECES,
        out_shape=[jax.ShapeDtypeStruct((width // PIECES, cols), BF16)] * PIECES,
        scratch_shapes=[
            pltpu.VMEM((rows, cols), BF16),
            pltpu.VMEM((width, rows), BF16),
            pltpu.SemaphoreType.DMA((cols // block,)),
        ],
        compiler_params=LARGE,
        cost_estimate=weight_of(0),
        name="pick_rows",
    )(place, pivots[:, None], matrix, *after)


def add_kernel(count, *refs):
    start = 0
    out_ref = refs[-1]
    for own_ref, got_ref in zip(refs[:count], refs[count : 2 * count]):
        rows = own_ref.shape[0]
        out_ref[start : start + rows] = own_ref[...] + got_ref[...]
        start += rows


def add(own, got, after=(), weight=0):
    rows, cols = sum(x.shape[0] for x in own), own[0].shape[1]
    return pl.pallas_call(
        functools.partial(add_kernel, len(own)),
        in_specs=[VMEM] * (2 * len(own)) + [ANY] * len(after),
        out_specs=VMEM,
        out_shape=jax.ShapeDtypeStruct((rows, cols), BF16),
        compiler_params=SMALL,
        cost_estimate=weight_of(weight),
        name="add",
    )(*own, *got, *after)


def in_order(core, mine, other, out_ref):
    half = mine.shape[0]
    out_ref[pl.ds(pl.multiple_of(core * half, half), half)] = mine
    out_ref[pl.ds(pl.multiple_of((1 - core) * half, half), half)] = other


def update_kernel(first_row, per_group, pick_source, make_upper, place_ref, pivots_ref,
                  matrix_ref, down_ref, down_got_ref, *refs):
    if make_upper:
        inverse_ref, up_ref, up_got_ref = refs[:3]
        sources = refs[3 : 4 + per_group]
        out_ref, upper_ref = refs[-10:-8]
    else:
        upper_ref = refs[0]
        sources = refs[1 : 2 + per_group]
        out_ref = refs[-9]
    rows_ref, left_ref, right_ref, keep_ref, pivot_rows_ref, in_sem, out_sem, sem = refs[-8:]
    count, cols = rows_ref.shape
    width = left_ref.shape[1] // 2
    row_place, col_place, core, rows = (place_ref[i] for i in range(4))
    block = min(UPDATE_BLOCK, cols)
    piece = min(count, 512)
    here = pl.ds(first_row, count)

    def fetch_panel(action):
        views = [sources[0].at[here, pl.ds(0, width)], *sources[1:]]
        panel_ref = left_ref.at[pl.ds(0, count), pl.ds(width, width)]
        for choice, view in enumerate(views):
            @pl.when(pick_source(col_place, core) == choice)
            def _():
                for copy in row_copies(view, panel_ref, sem):
                    action(copy)

    def fetch(number):
        there = columns(number, block)
        return pltpu.make_async_copy(
            matrix_ref.at[here, there], rows_ref.at[:, there], in_sem.at[number]
        )

    def store(number):
        there = columns(number, block)
        return pltpu.make_async_copy(
            rows_ref.at[:, there], out_ref.at[here, there], out_sem.at[number]
        )

    fetch_panel(lambda copy: copy.start())
    for number in range(cols // block):
        fetch(number).start()
    for start in range(0, count, piece):
        these = slice(start, start + piece)
        row = lax.broadcasted_iota(jnp.int32, (piece, width), 0)
        row = row + (row_place * rows + first_row + start)
        onehot = jnp.where(pivots_ref[...] == row, 1.0, 0.0)
        left_ref[these, :width] = onehot.astype(BF16)
        has_pivot = jnp.max(onehot, axis=1, keepdims=True)
        keep_ref[these] = jnp.broadcast_to(1.0 - has_pivot, (piece, 128))
    fetch_panel(lambda copy: copy.wait())

    @pl.loop(0, cols // block)
    def _(number):
        there = columns(number, block)
        if make_upper:
            in_order(core, up_ref[:, there], up_got_ref[:, there], pivot_rows_ref)
            upper_ref[:, there] = jnp.dot(
                inverse_ref[...], pivot_rows_ref[...], preferred_element_type=F32
            ).astype(BF16)
        fetch(number).wait()

        @pl.when((col_place > 0) | (number * block >= width))
        def _():
            in_order(core, down_ref[:, there], down_got_ref[:, there], right_ref)
            upper = upper_ref[:, there]
            right_ref[width:] = -upper
            right = right_ref[...]
            for start in range(0, count, piece):
                these = slice(start, start + piece)
                change = jnp.dot(left_ref[these], right, preferred_element_type=F32)
                keep = jnp.concatenate([keep_ref[these]] * (block // 128), axis=1)
                kept = rows_ref[these, there].astype(F32) * keep
                rows_ref[these, there] = (kept + change).astype(BF16)
            if first_row < width:
                @pl.when(row_place == 0)
                def _():
                    rows_ref[: width - first_row, there] = upper[first_row:]

        store(number).start()

    for number in range(cols // block):
        store(number).wait()


def update(group, pick_source, place, pivots, matrix, down, down_got, received,
           upper_terms=None, upper=None, out=None):
    first_row, count = group
    rows, cols = matrix.shape
    width = pivots.shape[0]
    make_upper = upper is None
    block = min(UPDATE_BLOCK, cols)
    operands = [place, pivots[None, :], matrix, down, down_got]
    in_specs = [SMEM, VMEM, ANY, VMEM, VMEM]
    terms = list(upper_terms) if make_upper else [upper]
    operands += terms + [matrix] + received
    in_specs += [VMEM] * len(terms) + [ANY] * (1 + len(received))
    hbm = pl.BlockSpec(memory_space=pltpu.HBM)
    aliases = {}
    if out is not None:
        aliases = {len(operands): 0}
        operands.append(out)
        in_specs.append(hbm)
    out_shape = [jax.ShapeDtypeStruct((rows, cols), BF16)]
    if make_upper:
        out_shape.append(jax.ShapeDtypeStruct((width, cols), BF16))
    return pl.pallas_call(
        functools.partial(update_kernel, first_row, len(received), pick_source, make_upper),
        in_specs=in_specs,
        out_specs=[hbm, VMEM][: len(out_shape)],
        out_shape=out_shape,
        scratch_shapes=[
            pltpu.VMEM((count, cols), BF16),
            pltpu.VMEM((count, 2 * width), BF16),
            pltpu.VMEM((2 * width, block), BF16),
            pltpu.VMEM((count, 128), F32),
            pltpu.VMEM((width, block), BF16),
            pltpu.SemaphoreType.DMA((cols // block,)),
            pltpu.SemaphoreType.DMA((cols // block,)),
            pltpu.SemaphoreType.DMA((COPIES,)),
        ],
        input_output_aliases=aliases,
        compiler_params=LARGE,
        cost_estimate=weight_of(0),
        name="update_rows",
    )(*operands)


def swap_kernel(first_row, place_ref, pivots_ref, matrix_ref, down_ref, down_got_ref, out_ref,
                onehot_ref, right_ref, keep_ref, sem):
    count, cols = out_ref.shape
    width = pivots_ref.shape[1]
    row_place, col_place, core, rows = (place_ref[i] for i in range(4))
    block = min(UPDATE_BLOCK, cols)
    piece = min(count, 512)

    def fetch(number):
        there = columns(number, block)
        return pltpu.make_async_copy(
            matrix_ref.at[pl.ds(first_row, count), there], out_ref.at[:, there], sem.at[number]
        )

    for number in range(cols // block):
        fetch(number).start()
    for start in range(0, count, piece):
        these = slice(start, start + piece)
        row = lax.broadcasted_iota(jnp.int32, (piece, width), 0)
        row = row + (row_place * rows + first_row + start)
        onehot = jnp.where(pivots_ref[...] == row, 1.0, 0.0)
        onehot_ref[these] = onehot.astype(BF16)
        has_pivot = jnp.max(onehot, axis=1, keepdims=True)
        keep_ref[these] = jnp.broadcast_to(1.0 - has_pivot, (piece, 128))

    @pl.loop(0, cols // block)
    def _(number):
        there = columns(number, block)
        fetch(number).wait()

        @pl.when((col_place > 0) | (number * block >= width))
        def _():
            in_order(core, down_ref[:, there], down_got_ref[:, there], right_ref)
            right = right_ref[...]
            for start in range(0, count, piece):
                these = slice(start, start + piece)
                moved = jnp.dot(onehot_ref[these], right, preferred_element_type=F32)
                keep = jnp.concatenate([keep_ref[these]] * (block // 128), axis=1)
                kept = out_ref[these, there].astype(F32) * keep
                out_ref[these, there] = (kept + moved).astype(BF16)


def swap(group, place, pivots, matrix, down, down_got):
    first_row, count = group
    cols = matrix.shape[1]
    width = pivots.shape[0]
    block = min(UPDATE_BLOCK, cols)
    return pl.pallas_call(
        functools.partial(swap_kernel, first_row),
        in_specs=[SMEM, VMEM, ANY, VMEM, VMEM],
        out_specs=VMEM,
        out_shape=jax.ShapeDtypeStruct((count, cols), BF16),
        scratch_shapes=[
            pltpu.VMEM((count, width), BF16),
            pltpu.VMEM((width, block), BF16),
            pltpu.VMEM((count, 128), F32),
            pltpu.SemaphoreType.DMA((cols // block,)),
        ],
        compiler_params=LARGE,
        cost_estimate=FREE,
        name="swap_rows",
    )(place, pivots[None, :], matrix, down, down_got)


def finish_kernel(first_row, per_group, pick_source, place_ref, matrix_ref, swapped_ref,
                  upper_ref, *refs):
    sources = [matrix_ref, *refs[:per_group]]
    out_ref, rows_ref, panel_ref, out_sem, sem = refs[-5:]
    count, width = panel_ref.shape
    cols = rows_ref.shape[1]
    row_place, col_place, core = (place_ref[i] for i in range(3))
    block = min(UPDATE_BLOCK, cols)
    piece = min(count, 512)
    here = pl.ds(first_row, count)

    def fetch_panel(action):
        views = [sources[0].at[here, pl.ds(0, width)], *sources[1:]]
        for choice, view in enumerate(views):
            @pl.when(pick_source(col_place, core) == choice)
            def _():
                for copy in row_copies(view, panel_ref, sem):
                    action(copy)

    def store(number):
        there = columns(number, block)
        return pltpu.make_async_copy(
            rows_ref.at[:, there], out_ref.at[here, there], out_sem.at[number]
        )

    fetch_panel(lambda copy: copy.start())
    fetch_panel(lambda copy: copy.wait())

    @pl.loop(0, cols // block)
    def _(number):
        there = columns(number, block)
        updated = (col_place > 0) | (number * block >= width)

        @pl.when(jnp.logical_not(updated))
        def _():
            rows_ref[:, there] = swapped_ref[:, there]

        @pl.when(updated)
        def _():
            upper = upper_ref[:, there]
            for start in range(0, count, piece):
                these = slice(start, start + piece)
                product = jnp.dot(panel_ref[these], upper, preferred_element_type=F32)
                left = swapped_ref[these, there].astype(F32) - product
                rows_ref[these, there] = left.astype(BF16)
            if first_row < width:
                @pl.when(row_place == 0)
                def _():
                    rows_ref[: width - first_row, there] = upper[first_row:]

        store(number).start()

    for number in range(cols // block):
        store(number).wait()


def finish(group, pick_source, place, matrix, swapped, upper, received, out):
    first_row, count = group
    rows, cols = matrix.shape
    width = upper.shape[0]
    block = min(UPDATE_BLOCK, cols)
    hbm = pl.BlockSpec(memory_space=pltpu.HBM)
    return pl.pallas_call(
        functools.partial(finish_kernel, first_row, len(received), pick_source),
        in_specs=[SMEM, ANY, VMEM, VMEM] + [ANY] * len(received) + [hbm],
        out_specs=hbm,
        out_shape=jax.ShapeDtypeStruct((rows, cols), BF16),
        scratch_shapes=[
            pltpu.VMEM((count, cols), BF16),
            pltpu.VMEM((count, width), BF16),
            pltpu.SemaphoreType.DMA((cols // block,)),
            pltpu.SemaphoreType.DMA((COPIES,)),
        ],
        input_output_aliases={4 + len(received): 0},
        compiler_params=LARGE,
        cost_estimate=FREE,
        name="finish_rows",
    )(place, matrix, swapped, upper, *received, out)


def swap_pairs(size, orders, step):
    return [(i, i ^ (1 << orders[i & 1][step])) for i in range(size)]


def grow_pairs(orders, step):
    pairs = []
    for core, order in enumerate(orders):
        places = [core]
        for bit in order[:step]:
            places += [i | (1 << bit) for i in places]
        pairs += [(i, i | (1 << order[step])) for i in places]
    return pairs


def move(value, pairs, core, n_prow, size):
    pairs = [(row * size + a, row * size + b) for row in range(core, n_prow, 2) for a, b in pairs]
    return lax.ppermute(value, ("prow", "pcol"), pairs)


def send(place, matrix, width, groups, core, n_prow, size):
    middle = size // 2
    held = []
    for number, group in enumerate(groups):
        last = held[-1] if held else None
        sent = chunk(place, 1, core, matrix, *group, width, last, CHUNK_WEIGHTS[number])
        if held:
            held[-1] = sent
        pairs = [(0, middle)] + [(middle, middle - 1)] * bool(held[:1])
        held.append(move(sent, pairs, core, n_prow, size))
    return held


def pass_on(place, held, rights, core, n_prow, size):
    middle = size // 2
    last = move(held[-1], [(middle, middle - 1)], core, n_prow, size)
    received = []
    for number, value in enumerate(held):
        left = held[number + 1] if number + 1 < len(held) else last
        right = rights[number] if number < len(rights) else None
        if right is None:
            right = move(value, [(middle, middle + 1)], core, n_prow, size)
        arrays = [value, right, left]
        both = jnp.where(place[1] < middle, left, right) if size > 4 else None
        distance = 1
        while middle - distance > 1 or middle + distance + 1 < size:
            pairs = []
            if middle - distance > 1:
                pairs.append((middle - distance, middle - distance - 1))
            if middle + distance + 1 < size:
                pairs.append((middle + distance, middle + distance + 1))
            both = move(both, pairs, core, n_prow, size)
            arrays.append(both)
            distance += 1
        received.append(arrays)
    return received


def source_of(size, per_core):
    middle = size // 2

    def pick_source(place, core):
        away = jnp.abs(place - middle)
        number = jnp.where(away == 0, 1, jnp.where(place < middle, 3, 2))
        number = jnp.where(away >= 2, away + 2, number)
        return jnp.where(place == 0, 0, number + core * per_core)

    return pick_source


def per_device(n_prow, n_pcol, matrix, pivots, unit_inverse):
    rows, cols = matrix.shape
    width = unit_inverse.shape[0]
    half = width // 2
    row_place = lax.axis_index("prow")
    col_place = lax.axis_index("pcol")
    core = row_place & 1
    place = jnp.stack([row_place, col_place, core, jnp.full_like(core, rows)]).astype(jnp.int32)
    matrix = pltpu.with_memory_space_constraint(matrix, pltpu.HBM)
    bits = list(range(1, n_prow.bit_length() - 1))
    orders = (bits, bits[::-1])
    cores = ([0], [0])
    last = len(bits) - 1

    size = rows // GROUPS
    groups = [(number * size, size) for number in range(GROUPS)]
    held = [send(place, matrix, width, groups, c, n_prow, n_pcol) for c in range(2)]
    arrived = [x for pair in zip(*held) for x in pair]
    middle = n_pcol // 2
    rights = [
        [move(x, [(middle, middle + 1)], c, n_prow, n_pcol) for x in held[c][: GROUPS - c]]
        for c in range(2)
    ]
    arrived_right = [rights[0][0], rights[1][0]] + rights[0][1:]

    order = jnp.where(core == 0, pivots, jnp.roll(pivots, half))
    down_got = lax.ppermute(chunk(place, 0, 0, matrix, half, half, cols), "prow", [(0, 1)])
    down = chunk(place, 0, 0, matrix, 0, half, cols, down_got)
    pieces = pick(place, order, matrix, [])
    up, sent = pieces[: PIECES // 2], pieces[PIECES // 2 :]
    up_got = [lax.ppermute(x, "prow", swap_pairs(n_prow, cores, 0)) for x in sent]
    def pins(a, b):
        return arrived[max(a - 2, 0):a] + arrived_right[max(b - 2, 0):b]
    for step in range(last + 1):
        up = [add(up, up_got, pins(*JOIN_AFTER[min(step, 1)]), JOIN_WEIGHTS[min(step, 1)])]
        down_got = lax.ppermute(down, "prow", grow_pairs(orders, step))
        up_got = [lax.ppermute(up[0], "prow", swap_pairs(n_prow, orders, step))]
        down = add([down], [down_got], [] + pins(*DOWN_AFTER[min(step, 1)]), DOWN_WEIGHTS[min(step, 1)])
    down_got = lax.ppermute(down, "prow", swap_pairs(n_prow, cores, 0))
    up = add(up, up_got, pins(0, 0), 0)
    up_got = lax.ppermute(up, "prow", swap_pairs(n_prow, cores, 0))

    by_core = [pass_on(place, held[c], rights[c], c, n_prow, n_pcol) for c in range(2)]
    received = [first + second for first, second in zip(*by_core)]
    common = (source_of(n_pcol, len(by_core[0][0])), place, pivots, matrix, down, down_got)
    out, upper = update(groups[0], *common, received[0], upper_terms=(unit_inverse, up, up_got))
    for group, arrays in zip(groups[1:-1], received[1:-1]):
        (out,) = update(group, *common, arrays, upper=upper, out=out)
    swapped = swap(groups[-1], *common[1:])
    return finish(
        groups[-1], common[0], place, matrix, swapped, upper, received[-1], out
    )


def solution(mesh):
    return jax.shard_map(
        functools.partial(per_device, mesh.shape["prow"], mesh.shape["pcol"]),
        mesh=mesh,
        in_specs=(P("prow", "pcol"), P(), P()),
        out_specs=P("prow", "pcol"),
        check_vma=False,
    )
```

```python
import functools

import jax
import jax.numpy as jnp
from jax import lax
from jax.experimental import pallas as pl
from jax.experimental.pallas import tpu as pltpu
from jax.sharding import PartitionSpec as P

GROUPS = 2
CHUNK_WEIGHTS = (0, 5)
JOIN_WEIGHTS, JOIN_AFTER = (2, 2), ((1, 0), (3, 1))
DOWN_WEIGHTS, DOWN_AFTER = (0, 20), ((1, 0), (0, 0))
PIECES = 2
PICK_BLOCK, UPDATE_BLOCK = 256, 512
COPIES = 4
F32, BF16 = jnp.float32, jnp.bfloat16
VMEM = pl.BlockSpec(memory_space=pltpu.VMEM)
ANY = pl.BlockSpec(memory_space=pl.ANY)
SMEM = pl.BlockSpec(memory_space=pltpu.SMEM)
SMALL = pltpu.CompilerParams(vmem_limit_bytes=8 * 2**20)
LARGE = pltpu.CompilerParams(vmem_limit_bytes=28 * 2**20)


FREE = pl.CostEstimate(flops=0, bytes_accessed=0, transcendentals=0)
def weight_of(x):
    x = float(x)
    return pl.CostEstimate(flops=int(x*1.15e9), bytes_accessed=int(x*3.69e6), transcendentals=0)


def row_copies(source, target, sem):
    rows = target.shape[0] // COPIES
    return [
        pltpu.make_async_copy(
            source.at[pl.ds(part * rows, rows)], target.at[pl.ds(part * rows, rows)], sem.at[part]
        )
        for part in range(COPIES)
    ]


def chunk_kernel(first_row, axis, core, place_ref, matrix_ref, *refs):
    out_ref, sem = refs[-2:]
    rows, width = out_ref.shape

    @pl.when((place_ref[axis] == 0) & (place_ref[2] == core))
    def _():
        view = matrix_ref.at[pl.ds(first_row, rows), pl.ds(0, width)]
        copies = row_copies(view, out_ref, sem)
        for copy in copies:
            copy.start()
        for copy in copies:
            copy.wait()


def chunk(place, axis, core, matrix, first_row, rows, width, held=None, weight=0, after=()):
    in_specs, operands = [SMEM, ANY], [place, matrix]
    if held is not None:
        in_specs.append(VMEM)
        operands.append(held)
    in_specs += [ANY] * len(after)
    operands += after
    return pl.pallas_call(
        functools.partial(chunk_kernel, first_row, axis, core),
        in_specs=in_specs,
        out_specs=VMEM,
        out_shape=jax.ShapeDtypeStruct((rows, width), BF16),
        scratch_shapes=[pltpu.SemaphoreType.DMA((COPIES,))],
        input_output_aliases={} if held is None else {2: 0},
        compiler_params=SMALL,
        cost_estimate=weight_of(weight),
        name="chunk",
    )(*operands)


def columns(number, block):
    return pl.ds(pl.multiple_of(number * block, block), block)


def pick_kernel(place_ref, pivots_ref, matrix_ref, *refs):
    whole_ref, onehot_ref, sem = refs[-3:]
    outs = refs[-3 - PIECES : -3]
    rows, cols = whole_ref.shape
    width = pivots_ref.shape[0]
    block = min(PICK_BLOCK, cols)
    count = width // PIECES

    def fetch(number):
        here = columns(number, block)
        return pltpu.make_async_copy(
            matrix_ref.at[:, here], whole_ref.at[:, here], sem.at[number]
        )

    for number in range(cols // block):
        fetch(number).start()
    row = lax.broadcasted_iota(jnp.int32, (width, rows), 1) + place_ref[0] * rows
    onehot_ref[...] = jnp.where(pivots_ref[...] == row, 1.0, 0.0).astype(BF16)

    @pl.loop(0, cols // block)
    def _(number):
        fetch(number).wait()
        here = columns(number, block)
        picked = jnp.dot(onehot_ref[...], whole_ref[:, here], preferred_element_type=F32)
        picked = picked.astype(BF16)
        for piece, out_ref in enumerate(outs):
            out_ref[:, here] = picked[piece * count : (piece + 1) * count]


def pick(place, pivots, matrix, after=()):
    rows, cols = matrix.shape
    width = pivots.shape[0]
    block = min(PICK_BLOCK, cols)
    return pl.pallas_call(
        pick_kernel,
        in_specs=[SMEM, VMEM, ANY] + [ANY] * len(after),
        out_specs=[VMEM] * PIECES,
        out_shape=[jax.ShapeDtypeStruct((width // PIECES, cols), BF16)] * PIECES,
        scratch_shapes=[
            pltpu.VMEM((rows, cols), BF16),
            pltpu.VMEM((width, rows), BF16),
            pltpu.SemaphoreType.DMA((cols // block,)),
        ],
        compiler_params=LARGE,
        cost_estimate=weight_of(0),
        name="pick_rows",
    )(place, pivots[:, None], matrix, *after)


def add_kernel(count, *refs):
    start = 0
    out_ref = refs[-1]
    for own_ref, got_ref in zip(refs[:count], refs[count : 2 * count]):
        rows = own_ref.shape[0]
        out_ref[start : start + rows] = own_ref[...] + got_ref[...]
        start += rows


def add(own, got, after=(), weight=0):
    rows, cols = sum(x.shape[0] for x in own), own[0].shape[1]
    return pl.pallas_call(
        functools.partial(add_kernel, len(own)),
        in_specs=[VMEM] * (2 * len(own)) + [ANY] * len(after),
        out_specs=VMEM,
        out_shape=jax.ShapeDtypeStruct((rows, cols), BF16),
        compiler_params=SMALL,
        cost_estimate=weight_of(weight),
        name="add",
    )(*own, *got, *after)


def in_order(core, mine, other, out_ref):
    half = mine.shape[0]
    out_ref[pl.ds(pl.multiple_of(core * half, half), half)] = mine
    out_ref[pl.ds(pl.multiple_of((1 - core) * half, half), half)] = other


def update_kernel(first_row, per_group, pick_source, make_upper, place_ref, pivots_ref,
                  matrix_ref, down_ref, down_got_ref, *refs):
    if make_upper:
        inverse_ref, up_ref, up_got_ref = refs[:3]
        sources = refs[3 : 4 + per_group]
        out_ref, upper_ref = refs[-10:-8]
    else:
        upper_ref = refs[0]
        sources = refs[1 : 2 + per_group]
        out_ref = refs[-9]
    rows_ref, left_ref, right_ref, keep_ref, pivot_rows_ref, in_sem, out_sem, sem = refs[-8:]
    count, cols = rows_ref.shape
    width = left_ref.shape[1] // 2
    row_place, col_place, core, rows = (place_ref[i] for i in range(4))
    block = min(UPDATE_BLOCK, cols)
    piece = min(count, 512)
    here = pl.ds(first_row, count)

    def fetch_panel(action):
        views = [sources[0].at[here, pl.ds(0, width)], *sources[1:]]
        panel_ref = left_ref.at[pl.ds(0, count), pl.ds(width, width)]
        for choice, view in enumerate(views):
            @pl.when(pick_source(col_place, core) == choice)
            def _():
                for copy in row_copies(view, panel_ref, sem):
                    action(copy)

    def fetch(number):
        there = columns(number, block)
        return pltpu.make_async_copy(
            matrix_ref.at[here, there], rows_ref.at[:, there], in_sem.at[number]
        )

    def store(number):
        there = columns(number, block)
        return pltpu.make_async_copy(
            rows_ref.at[:, there], out_ref.at[here, there], out_sem.at[number]
        )

    fetch_panel(lambda copy: copy.start())
    for number in range(cols // block):
        fetch(number).start()
    for start in range(0, count, piece):
        these = slice(start, start + piece)
        row = lax.broadcasted_iota(jnp.int32, (piece, width), 0)
        row = row + (row_place * rows + first_row + start)
        onehot = jnp.where(pivots_ref[...] == row, 1.0, 0.0)
        left_ref[these, :width] = onehot.astype(BF16)
        has_pivot = jnp.max(onehot, axis=1, keepdims=True)
        keep_ref[these] = jnp.broadcast_to(1.0 - has_pivot, (piece, 128))
    fetch_panel(lambda copy: copy.wait())

    @pl.loop(0, cols // block)
    def _(number):
        there = columns(number, block)
        if make_upper:
            in_order(core, up_ref[:, there], up_got_ref[:, there], pivot_rows_ref)
            upper_ref[:, there] = jnp.dot(
                inverse_ref[...], pivot_rows_ref[...], preferred_element_type=F32
            ).astype(BF16)
        fetch(number).wait()

        @pl.when((col_place > 0) | (number * block >= width))
        def _():
            in_order(core, down_ref[:, there], down_got_ref[:, there], right_ref)
            upper = upper_ref[:, there]
            right_ref[width:] = -upper
            right = right_ref[...]
            for start in range(0, count, piece):
                these = slice(start, start + piece)
                change = jnp.dot(left_ref[these], right, preferred_element_type=F32)
                keep = jnp.concatenate([keep_ref[these]] * (block // 128), axis=1)
                kept = rows_ref[these, there].astype(F32) * keep
                rows_ref[these, there] = (kept + change).astype(BF16)
            if first_row < width:
                @pl.when(row_place == 0)
                def _():
                    rows_ref[: width - first_row, there] = upper[first_row:]

        store(number).start()

    for number in range(cols // block):
        store(number).wait()


def update(group, pick_source, place, pivots, matrix, down, down_got, received,
           upper_terms=None, upper=None, out=None):
    first_row, count = group
    rows, cols = matrix.shape
    width = pivots.shape[0]
    make_upper = upper is None
    block = min(UPDATE_BLOCK, cols)
    operands = [place, pivots[None, :], matrix, down, down_got]
    in_specs = [SMEM, VMEM, ANY, VMEM, VMEM]
    terms = list(upper_terms) if make_upper else [upper]
    operands += terms + [matrix] + received
    in_specs += [VMEM] * len(terms) + [ANY] * (1 + len(received))
    hbm = pl.BlockSpec(memory_space=pltpu.HBM)
    aliases = {}
    if out is not None:
        aliases = {len(operands): 0}
        operands.append(out)
        in_specs.append(hbm)
    out_shape = [jax.ShapeDtypeStruct((rows, cols), BF16)]
    if make_upper:
        out_shape.append(jax.ShapeDtypeStruct((width, cols), BF16))
    return pl.pallas_call(
        functools.partial(update_kernel, first_row, len(received), pick_source, make_upper),
        in_specs=in_specs,
        out_specs=[hbm, VMEM][: len(out_shape)],
        out_shape=out_shape,
        scratch_shapes=[
            pltpu.VMEM((count, cols), BF16),
            pltpu.VMEM((count, 2 * width), BF16),
            pltpu.VMEM((2 * width, block), BF16),
            pltpu.VMEM((count, 128), F32),
            pltpu.VMEM((width, block), BF16),
            pltpu.SemaphoreType.DMA((cols // block,)),
            pltpu.SemaphoreType.DMA((cols // block,)),
            pltpu.SemaphoreType.DMA((COPIES,)),
        ],
        input_output_aliases=aliases,
        compiler_params=LARGE,
        cost_estimate=weight_of(0),
        name="update_rows",
    )(*operands)


def swap_kernel(first_row, place_ref, pivots_ref, matrix_ref, down_ref, down_got_ref, out_ref,
                onehot_ref, right_ref, keep_ref, sem):
    count, cols = out_ref.shape
    width = pivots_ref.shape[1]
    row_place, col_place, core, rows = (place_ref[i] for i in range(4))
    block = min(UPDATE_BLOCK, cols)
    piece = min(count, 512)

    def fetch(number):
        there = columns(number, block)
        return pltpu.make_async_copy(
            matrix_ref.at[pl.ds(first_row, count), there], out_ref.at[:, there], sem.at[number]
        )

    for number in range(cols // block):
        fetch(number).start()
    for start in range(0, count, piece):
        these = slice(start, start + piece)
        row = lax.broadcasted_iota(jnp.int32, (piece, width), 0)
        row = row + (row_place * rows + first_row + start)
        onehot = jnp.where(pivots_ref[...] == row, 1.0, 0.0)
        onehot_ref[these] = onehot.astype(BF16)
        has_pivot = jnp.max(onehot, axis=1, keepdims=True)
        keep_ref[these] = jnp.broadcast_to(1.0 - has_pivot, (piece, 128))

    @pl.loop(0, cols // block)
    def _(number):
        there = columns(number, block)
        fetch(number).wait()

        @pl.when((col_place > 0) | (number * block >= width))
        def _():
            in_order(core, down_ref[:, there], down_got_ref[:, there], right_ref)
            right = right_ref[...]
            for start in range(0, count, piece):
                these = slice(start, start + piece)
                moved = jnp.dot(onehot_ref[these], right, preferred_element_type=F32)
                keep = jnp.concatenate([keep_ref[these]] * (block // 128), axis=1)
                kept = out_ref[these, there].astype(F32) * keep
                out_ref[these, there] = (kept + moved).astype(BF16)


def swap(group, place, pivots, matrix, down, down_got):
    first_row, count = group
    cols = matrix.shape[1]
    width = pivots.shape[0]
    block = min(UPDATE_BLOCK, cols)
    return pl.pallas_call(
        functools.partial(swap_kernel, first_row),
        in_specs=[SMEM, VMEM, ANY, VMEM, VMEM],
        out_specs=VMEM,
        out_shape=jax.ShapeDtypeStruct((count, cols), BF16),
        scratch_shapes=[
            pltpu.VMEM((count, width), BF16),
            pltpu.VMEM((width, block), BF16),
            pltpu.VMEM((count, 128), F32),
            pltpu.SemaphoreType.DMA((cols // block,)),
        ],
        compiler_params=LARGE,
        cost_estimate=FREE,
        name="swap_rows",
    )(place, pivots[None, :], matrix, down, down_got)


def finish_kernel(first_row, per_group, pick_source, place_ref, matrix_ref, swapped_ref,
                  upper_ref, *refs):
    sources = [matrix_ref, *refs[:per_group]]
    out_ref, rows_ref, panel_ref, out_sem, sem = refs[-5:]
    count, width = panel_ref.shape
    cols = rows_ref.shape[1]
    row_place, col_place, core = (place_ref[i] for i in range(3))
    block = min(UPDATE_BLOCK, cols)
    piece = min(count, 512)
    here = pl.ds(first_row, count)

    def fetch_panel(action, first=0, last=COPIES):
        views = [sources[0].at[here, pl.ds(0, width)], *sources[1:]]
        for choice, view in enumerate(views):
            @pl.when(pick_source(col_place, core) == choice)
            def _():
                for copy in row_copies(view, panel_ref, sem)[first:last]:
                    action(copy)

    def store(number):
        there = columns(number, block)
        return pltpu.make_async_copy(
            rows_ref.at[:, there], out_ref.at[here, there], out_sem.at[number]
        )

    fetch_panel(lambda copy: copy.start())

    @pl.loop(0, cols // block)
    def _(number):
        there = columns(number, block)
        updated = (col_place > 0) | (number * block >= width)

        @pl.when(jnp.logical_not(updated))
        def _():
            rows_ref[:, there] = swapped_ref[:, there]

        for start in range(0, count, piece):
            these = slice(start, start + piece)

            @pl.when(number == 0)
            def _():
                parts = [COPIES * row // count for row in (start, start + piece)]
                fetch_panel(lambda copy: copy.wait(), *parts)

            @pl.when(updated)
            def _():
                product = jnp.dot(panel_ref[these], upper_ref[:, there], preferred_element_type=F32)
                left = swapped_ref[these, there].astype(F32) - product
                rows_ref[these, there] = left.astype(BF16)

        if first_row < width:
            @pl.when(updated & (row_place == 0))
            def _():
                rows_ref[: width - first_row, there] = upper_ref[first_row:, there]

        store(number).start()

    for number in range(cols // block):
        store(number).wait()


def finish(group, pick_source, place, matrix, swapped, upper, received, out):
    first_row, count = group
    rows, cols = matrix.shape
    width = upper.shape[0]
    block = min(UPDATE_BLOCK, cols)
    hbm = pl.BlockSpec(memory_space=pltpu.HBM)
    return pl.pallas_call(
        functools.partial(finish_kernel, first_row, len(received), pick_source),
        in_specs=[SMEM, ANY, VMEM, VMEM] + [ANY] * len(received) + [hbm],
        out_specs=hbm,
        out_shape=jax.ShapeDtypeStruct((rows, cols), BF16),
        scratch_shapes=[
            pltpu.VMEM((count, cols), BF16),
            pltpu.VMEM((count, width), BF16),
            pltpu.SemaphoreType.DMA((cols // block,)),
            pltpu.SemaphoreType.DMA((COPIES,)),
        ],
        input_output_aliases={4 + len(received): 0},
        compiler_params=LARGE,
        cost_estimate=FREE,
        name="finish_rows",
    )(place, matrix, swapped, upper, *received, out)


def swap_pairs(size, orders, step):
    return [(i, i ^ (1 << orders[i & 1][step])) for i in range(size)]


def grow_pairs(orders, step):
    pairs = []
    for core, order in enumerate(orders):
        places = [core]
        for bit in order[:step]:
            places += [i | (1 << bit) for i in places]
        pairs += [(i, i | (1 << order[step])) for i in places]
    return pairs


def move(value, pairs, core, n_prow, size):
    pairs = [(row * size + a, row * size + b) for row in range(core, n_prow, 2) for a, b in pairs]
    return lax.ppermute(value, ("prow", "pcol"), pairs)


def send(place, matrix, width, groups, core, n_prow, size):
    middle = size // 2
    held = []
    for number, group in enumerate(groups):
        last = held[-1] if held else None
        sent = chunk(place, 1, core, matrix, *group, width, last, CHUNK_WEIGHTS[number])
        if held:
            held[-1] = sent
        pairs = [(0, middle)] + [(middle, middle - 1)] * bool(held[:1])
        held.append(move(sent, pairs, core, n_prow, size))
    return held


def pass_on(place, held, rights, core, n_prow, size):
    middle = size // 2
    last = move(held[-1], [(middle, middle - 1)], core, n_prow, size)
    received = []
    for number, value in enumerate(held):
        left = held[number + 1] if number + 1 < len(held) else last
        right = rights[number] if number < len(rights) else None
        if right is None:
            right = move(value, [(middle, middle + 1)], core, n_prow, size)
        arrays = [value, right, left]
        both = jnp.where(place[1] < middle, left, right) if size > 4 else None
        distance = 1
        while middle - distance > 1 or middle + distance + 1 < size:
            pairs = []
            if middle - distance > 1:
                pairs.append((middle - distance, middle - distance - 1))
            if middle + distance + 1 < size:
                pairs.append((middle + distance, middle + distance + 1))
            both = move(both, pairs, core, n_prow, size)
            arrays.append(both)
            distance += 1
        received.append(arrays)
    return received


def source_of(size, per_core):
    middle = size // 2

    def pick_source(place, core):
        away = jnp.abs(place - middle)
        number = jnp.where(away == 0, 1, jnp.where(place < middle, 3, 2))
        number = jnp.where(away >= 2, away + 2, number)
        return jnp.where(place == 0, 0, number + core * per_core)

    return pick_source


def per_device(n_prow, n_pcol, matrix, pivots, unit_inverse):
    rows, cols = matrix.shape
    width = unit_inverse.shape[0]
    half = width // 2
    row_place = lax.axis_index("prow")
    col_place = lax.axis_index("pcol")
    core = row_place & 1
    place = jnp.stack([row_place, col_place, core, jnp.full_like(core, rows)]).astype(jnp.int32)
    matrix = pltpu.with_memory_space_constraint(matrix, pltpu.HBM)
    bits = list(range(1, n_prow.bit_length() - 1))
    orders = (bits, bits[::-1])
    cores = ([0], [0])
    last = len(bits) - 1

    size = rows // GROUPS
    groups = [(number * size, size) for number in range(GROUPS)]
    held = [send(place, matrix, width, groups, c, n_prow, n_pcol) for c in range(2)]
    arrived = [x for pair in zip(*held) for x in pair]
    middle = n_pcol // 2
    rights = [
        [move(x, [(middle, middle + 1)], c, n_prow, n_pcol) for x in held[c][: GROUPS - c]]
        for c in range(2)
    ]
    arrived_right = [rights[0][0], rights[1][0]] + rights[0][1:]

    order = jnp.where(core == 0, pivots, jnp.roll(pivots, half))
    down_got = lax.ppermute(chunk(place, 0, 0, matrix, half, half, cols), "prow", [(0, 1)])
    down = chunk(place, 0, 0, matrix, 0, half, cols, down_got)
    pieces = pick(place, order, matrix, [])
    up, sent = pieces[: PIECES // 2], pieces[PIECES // 2 :]
    up_got = [lax.ppermute(x, "prow", swap_pairs(n_prow, cores, 0)) for x in sent]
    def pins(a, b):
        return arrived[max(a - 2, 0):a] + arrived_right[max(b - 2, 0):b]
    for step in range(last + 1):
        up = [add(up, up_got, pins(*JOIN_AFTER[min(step, 1)]), JOIN_WEIGHTS[min(step, 1)])]
        down_got = lax.ppermute(down, "prow", grow_pairs(orders, step))
        up_got = [lax.ppermute(up[0], "prow", swap_pairs(n_prow, orders, step))]
        down = add([down], [down_got], [] + pins(*DOWN_AFTER[min(step, 1)]), DOWN_WEIGHTS[min(step, 1)])
    down_got = lax.ppermute(down, "prow", swap_pairs(n_prow, cores, 0))
    up = add(up, up_got, pins(0, 0), 0)
    up_got = lax.ppermute(up, "prow", swap_pairs(n_prow, cores, 0))

    by_core = [pass_on(place, held[c], rights[c], c, n_prow, n_pcol) for c in range(2)]
    received = [first + second for first, second in zip(*by_core)]
    common = (source_of(n_pcol, len(by_core[0][0])), place, pivots, matrix, down, down_got)
    out, upper = update(groups[0], *common, received[0], upper_terms=(unit_inverse, up, up_got))
    for group, arrays in zip(groups[1:-1], received[1:-1]):
        (out,) = update(group, *common, arrays, upper=upper, out=out)
    swapped = swap(groups[-1], *common[1:])
    return finish(
        groups[-1], common[0], place, matrix, swapped, upper, received[-1], out
    )


def solution(mesh):
    return jax.shard_map(
        functools.partial(per_device, mesh.shape["prow"], mesh.shape["pcol"]),
        mesh=mesh,
        in_specs=(P("prow", "pcol"), P(), P()),
        out_specs=P("prow", "pcol"),
        check_vma=False,
    )
```

```python
import functools

import jax
import jax.numpy as jnp
from jax import lax
from jax.experimental import pallas as pl
from jax.experimental.pallas import tpu as pltpu
from jax.sharding import PartitionSpec as P

GROUPS = 2
CHUNK_WEIGHTS = (0, 5)
JOIN_WEIGHTS, JOIN_AFTER = (2, 2), ((1, 0), (3, 1))
DOWN_WEIGHTS, DOWN_AFTER = (0, 20), ((1, 0), (0, 0))
PIECES = 2
PICK_BLOCK, UPDATE_BLOCK = 256, 512
COPIES = 8
F32, BF16 = jnp.float32, jnp.bfloat16
VMEM = pl.BlockSpec(memory_space=pltpu.VMEM)
ANY = pl.BlockSpec(memory_space=pl.ANY)
SMEM = pl.BlockSpec(memory_space=pltpu.SMEM)
SMALL = pltpu.CompilerParams(vmem_limit_bytes=8 * 2**20)
LARGE = pltpu.CompilerParams(vmem_limit_bytes=28 * 2**20)


FREE = pl.CostEstimate(flops=0, bytes_accessed=0, transcendentals=0)
def weight_of(x):
    x = float(x)
    return pl.CostEstimate(flops=int(x*1.15e9), bytes_accessed=int(x*3.69e6), transcendentals=0)


def row_copies(source, target, sem):
    rows = target.shape[0] // COPIES
    return [
        pltpu.make_async_copy(
            source.at[pl.ds(part * rows, rows)], target.at[pl.ds(part * rows, rows)], sem.at[part]
        )
        for part in range(COPIES)
    ]


def chunk_kernel(first_row, axis, core, place_ref, matrix_ref, *refs):
    out_ref, sem = refs[-2:]
    rows, width = out_ref.shape

    @pl.when((place_ref[axis] == 0) & (place_ref[2] == core))
    def _():
        view = matrix_ref.at[pl.ds(first_row, rows), pl.ds(0, width)]
        copies = row_copies(view, out_ref, sem)
        for copy in copies:
            copy.start()
        for copy in copies:
            copy.wait()


def chunk(place, axis, core, matrix, first_row, rows, width, held=None, weight=0, after=()):
    in_specs, operands = [SMEM, ANY], [place, matrix]
    if held is not None:
        in_specs.append(VMEM)
        operands.append(held)
    in_specs += [ANY] * len(after)
    operands += after
    return pl.pallas_call(
        functools.partial(chunk_kernel, first_row, axis, core),
        in_specs=in_specs,
        out_specs=VMEM,
        out_shape=jax.ShapeDtypeStruct((rows, width), BF16),
        scratch_shapes=[pltpu.SemaphoreType.DMA((COPIES,))],
        input_output_aliases={} if held is None else {2: 0},
        compiler_params=SMALL,
        cost_estimate=weight_of(weight),
        name="chunk",
    )(*operands)


def columns(number, block):
    return pl.ds(pl.multiple_of(number * block, block), block)


def pick_kernel(place_ref, pivots_ref, matrix_ref, *refs):
    whole_ref, onehot_ref, sem = refs[-3:]
    outs = refs[-3 - PIECES : -3]
    rows, cols = whole_ref.shape
    width = pivots_ref.shape[0]
    block = min(PICK_BLOCK, cols)
    count = width // PIECES

    def fetch(number):
        here = columns(number, block)
        return pltpu.make_async_copy(
            matrix_ref.at[:, here], whole_ref.at[:, here], sem.at[number]
        )

    for number in range(cols // block):
        fetch(number).start()
    row = lax.broadcasted_iota(jnp.int32, (width, rows), 1) + place_ref[0] * rows
    onehot_ref[...] = jnp.where(pivots_ref[...] == row, 1.0, 0.0).astype(BF16)

    @pl.loop(0, cols // block)
    def _(number):
        fetch(number).wait()
        here = columns(number, block)
        picked = jnp.dot(onehot_ref[...], whole_ref[:, here], preferred_element_type=F32)
        picked = picked.astype(BF16)
        for piece, out_ref in enumerate(outs):
            out_ref[:, here] = picked[piece * count : (piece + 1) * count]


def pick(place, pivots, matrix, after=()):
    rows, cols = matrix.shape
    width = pivots.shape[0]
    block = min(PICK_BLOCK, cols)
    return pl.pallas_call(
        pick_kernel,
        in_specs=[SMEM, VMEM, ANY] + [ANY] * len(after),
        out_specs=[VMEM] * PIECES,
        out_shape=[jax.ShapeDtypeStruct((width // PIECES, cols), BF16)] * PIECES,
        scratch_shapes=[
            pltpu.VMEM((rows, cols), BF16),
            pltpu.VMEM((width, rows), BF16),
            pltpu.SemaphoreType.DMA((cols // block,)),
        ],
        compiler_params=LARGE,
        cost_estimate=weight_of(0),
        name="pick_rows",
    )(place, pivots[:, None], matrix, *after)


def add_kernel(count, *refs):
    start = 0
    out_ref = refs[-1]
    for own_ref, got_ref in zip(refs[:count], refs[count : 2 * count]):
        rows = own_ref.shape[0]
        out_ref[start : start + rows] = own_ref[...] + got_ref[...]
        start += rows


def add(own, got, after=(), weight=0):
    rows, cols = sum(x.shape[0] for x in own), own[0].shape[1]
    return pl.pallas_call(
        functools.partial(add_kernel, len(own)),
        in_specs=[VMEM] * (2 * len(own)) + [ANY] * len(after),
        out_specs=VMEM,
        out_shape=jax.ShapeDtypeStruct((rows, cols), BF16),
        compiler_params=SMALL,
        cost_estimate=weight_of(weight),
        name="add",
    )(*own, *got, *after)


def in_order(core, mine, other, out_ref):
    half = mine.shape[0]
    out_ref[pl.ds(pl.multiple_of(core * half, half), half)] = mine
    out_ref[pl.ds(pl.multiple_of((1 - core) * half, half), half)] = other


def update_kernel(first_row, per_group, pick_source, make_upper, place_ref, pivots_ref,
                  matrix_ref, down_ref, down_got_ref, *refs):
    if make_upper:
        inverse_ref, up_ref, up_got_ref = refs[:3]
        sources = refs[3 : 4 + per_group]
        out_ref, upper_ref = refs[-10:-8]
    else:
        upper_ref = refs[0]
        sources = refs[1 : 2 + per_group]
        out_ref = refs[-9]
    rows_ref, left_ref, right_ref, keep_ref, pivot_rows_ref, in_sem, out_sem, sem = refs[-8:]
    count, cols = rows_ref.shape
    width = left_ref.shape[1] // 2
    row_place, col_place, core, rows = (place_ref[i] for i in range(4))
    block = min(UPDATE_BLOCK, cols)
    piece = min(count, 512)
    here = pl.ds(first_row, count)

    def fetch_panel(action):
        views = [sources[0].at[here, pl.ds(0, width)], *sources[1:]]
        panel_ref = left_ref.at[pl.ds(0, count), pl.ds(width, width)]
        for choice, view in enumerate(views):
            @pl.when(pick_source(col_place, core) == choice)
            def _():
                for copy in row_copies(view, panel_ref, sem):
                    action(copy)

    def fetch(number):
        there = columns(number, block)
        return pltpu.make_async_copy(
            matrix_ref.at[here, there], rows_ref.at[:, there], in_sem.at[number]
        )

    def store(number):
        there = columns(number, block)
        return pltpu.make_async_copy(
            rows_ref.at[:, there], out_ref.at[here, there], out_sem.at[number]
        )

    fetch_panel(lambda copy: copy.start())
    for number in range(cols // block):
        fetch(number).start()
    for start in range(0, count, piece):
        these = slice(start, start + piece)
        row = lax.broadcasted_iota(jnp.int32, (piece, width), 0)
        row = row + (row_place * rows + first_row + start)
        onehot = jnp.where(pivots_ref[...] == row, 1.0, 0.0)
        left_ref[these, :width] = onehot.astype(BF16)
        has_pivot = jnp.max(onehot, axis=1, keepdims=True)
        keep_ref[these] = jnp.broadcast_to(1.0 - has_pivot, (piece, 128))
    fetch_panel(lambda copy: copy.wait())

    @pl.loop(0, cols // block)
    def _(number):
        there = columns(number, block)
        if make_upper:
            in_order(core, up_ref[:, there], up_got_ref[:, there], pivot_rows_ref)
            upper_ref[:, there] = jnp.dot(
                inverse_ref[...], pivot_rows_ref[...], preferred_element_type=F32
            ).astype(BF16)
        fetch(number).wait()

        @pl.when((col_place > 0) | (number * block >= width))
        def _():
            in_order(core, down_ref[:, there], down_got_ref[:, there], right_ref)
            upper = upper_ref[:, there]
            right_ref[width:] = -upper
            right = right_ref[...]
            for start in range(0, count, piece):
                these = slice(start, start + piece)
                change = jnp.dot(left_ref[these], right, preferred_element_type=F32)
                keep = jnp.concatenate([keep_ref[these]] * (block // 128), axis=1)
                kept = rows_ref[these, there].astype(F32) * keep
                rows_ref[these, there] = (kept + change).astype(BF16)
            if first_row < width:
                @pl.when(row_place == 0)
                def _():
                    rows_ref[: width - first_row, there] = upper[first_row:]

        store(number).start()

    for number in range(cols // block):
        store(number).wait()


def update(group, pick_source, place, pivots, matrix, down, down_got, received,
           upper_terms=None, upper=None, out=None):
    first_row, count = group
    rows, cols = matrix.shape
    width = pivots.shape[0]
    make_upper = upper is None
    block = min(UPDATE_BLOCK, cols)
    operands = [place, pivots[None, :], matrix, down, down_got]
    in_specs = [SMEM, VMEM, ANY, VMEM, VMEM]
    terms = list(upper_terms) if make_upper else [upper]
    operands += terms + [matrix] + received
    in_specs += [VMEM] * len(terms) + [ANY] * (1 + len(received))
    hbm = pl.BlockSpec(memory_space=pltpu.HBM)
    aliases = {}
    if out is not None:
        aliases = {len(operands): 0}
        operands.append(out)
        in_specs.append(hbm)
    out_shape = [jax.ShapeDtypeStruct((rows, cols), BF16)]
    if make_upper:
        out_shape.append(jax.ShapeDtypeStruct((width, cols), BF16))
    return pl.pallas_call(
        functools.partial(update_kernel, first_row, len(received), pick_source, make_upper),
        in_specs=in_specs,
        out_specs=[hbm, VMEM][: len(out_shape)],
        out_shape=out_shape,
        scratch_shapes=[
            pltpu.VMEM((count, cols), BF16),
            pltpu.VMEM((count, 2 * width), BF16),
            pltpu.VMEM((2 * width, block), BF16),
            pltpu.VMEM((count, 128), F32),
            pltpu.VMEM((width, block), BF16),
            pltpu.SemaphoreType.DMA((cols // block,)),
            pltpu.SemaphoreType.DMA((cols // block,)),
            pltpu.SemaphoreType.DMA((COPIES,)),
        ],
        input_output_aliases=aliases,
        compiler_params=LARGE,
        cost_estimate=weight_of(0),
        name="update_rows",
    )(*operands)


def swap_kernel(first_row, place_ref, pivots_ref, matrix_ref, down_ref, down_got_ref, out_ref,
                onehot_ref, right_ref, keep_ref, sem):
    count, cols = out_ref.shape
    width = pivots_ref.shape[1]
    row_place, col_place, core, rows = (place_ref[i] for i in range(4))
    block = min(UPDATE_BLOCK, cols)
    piece = min(count, 512)

    def fetch(number):
        there = columns(number, block)
        return pltpu.make_async_copy(
            matrix_ref.at[pl.ds(first_row, count), there], out_ref.at[:, there], sem.at[number]
        )

    for number in range(cols // block):
        fetch(number).start()
    for start in range(0, count, piece):
        these = slice(start, start + piece)
        row = lax.broadcasted_iota(jnp.int32, (piece, width), 0)
        row = row + (row_place * rows + first_row + start)
        onehot = jnp.where(pivots_ref[...] == row, 1.0, 0.0)
        onehot_ref[these] = onehot.astype(BF16)
        has_pivot = jnp.max(onehot, axis=1, keepdims=True)
        keep_ref[these] = jnp.broadcast_to(1.0 - has_pivot, (piece, 128))

    @pl.loop(0, cols // block)
    def _(number):
        there = columns(number, block)
        fetch(number).wait()

        @pl.when((col_place > 0) | (number * block >= width))
        def _():
            in_order(core, down_ref[:, there], down_got_ref[:, there], right_ref)
            right = right_ref[...]
            for start in range(0, count, piece):
                these = slice(start, start + piece)
                moved = jnp.dot(onehot_ref[these], right, preferred_element_type=F32)
                keep = jnp.concatenate([keep_ref[these]] * (block // 128), axis=1)
                kept = out_ref[these, there].astype(F32) * keep
                out_ref[these, there] = (kept + moved).astype(BF16)


def swap(group, place, pivots, matrix, down, down_got):
    first_row, count = group
    cols = matrix.shape[1]
    width = pivots.shape[0]
    block = min(UPDATE_BLOCK, cols)
    return pl.pallas_call(
        functools.partial(swap_kernel, first_row),
        in_specs=[SMEM, VMEM, ANY, VMEM, VMEM],
        out_specs=VMEM,
        out_shape=jax.ShapeDtypeStruct((count, cols), BF16),
        scratch_shapes=[
            pltpu.VMEM((count, width), BF16),
            pltpu.VMEM((width, block), BF16),
            pltpu.VMEM((count, 128), F32),
            pltpu.SemaphoreType.DMA((cols // block,)),
        ],
        compiler_params=LARGE,
        cost_estimate=FREE,
        name="swap_rows",
    )(place, pivots[None, :], matrix, down, down_got)


def finish_kernel(first_row, per_group, pick_source, place_ref, matrix_ref, swapped_ref,
                  upper_ref, *refs):
    sources = [matrix_ref, *refs[:per_group]]
    out_ref, rows_ref, panel_ref, out_sem, sem = refs[-5:]
    count, width = panel_ref.shape
    cols = rows_ref.shape[1]
    row_place, col_place, core = (place_ref[i] for i in range(3))
    block = min(UPDATE_BLOCK, cols)
    piece = min(count, 512)
    here = pl.ds(first_row, count)

    def fetch_panel(action):
        views = [sources[0].at[here, pl.ds(0, width)], *sources[1:]]
        for choice, view in enumerate(views):
            @pl.when(pick_source(col_place, core) == choice)
            def _():
                for copy in row_copies(view, panel_ref, sem):
                    action(copy)

    def store(number):
        there = columns(number, block)
        return pltpu.make_async_copy(
            rows_ref.at[:, there], out_ref.at[here, there], out_sem.at[number]
        )

    fetch_panel(lambda copy: copy.start())
    fetch_panel(lambda copy: copy.wait())

    @pl.loop(0, cols // block)
    def _(number):
        there = columns(number, block)
        updated = (col_place > 0) | (number * block >= width)

        @pl.when(jnp.logical_not(updated))
        def _():
            rows_ref[:, there] = swapped_ref[:, there]

        @pl.when(updated)
        def _():
            upper = upper_ref[:, there]
            for start in range(0, count, piece):
                these = slice(start, start + piece)
                product = jnp.dot(panel_ref[these], upper, preferred_element_type=F32)
                left = swapped_ref[these, there].astype(F32) - product
                rows_ref[these, there] = left.astype(BF16)
            if first_row < width:
                @pl.when(row_place == 0)
                def _():
                    rows_ref[: width - first_row, there] = upper[first_row:]

        store(number).start()

    for number in range(cols // block):
        store(number).wait()


def finish(group, pick_source, place, matrix, swapped, upper, received, out):
    first_row, count = group
    rows, cols = matrix.shape
    width = upper.shape[0]
    block = min(UPDATE_BLOCK, cols)
    hbm = pl.BlockSpec(memory_space=pltpu.HBM)
    return pl.pallas_call(
        functools.partial(finish_kernel, first_row, len(received), pick_source),
        in_specs=[SMEM, ANY, VMEM, VMEM] + [ANY] * len(received) + [hbm],
        out_specs=hbm,
        out_shape=jax.ShapeDtypeStruct((rows, cols), BF16),
        scratch_shapes=[
            pltpu.VMEM((count, cols), BF16),
            pltpu.VMEM((count, width), BF16),
            pltpu.SemaphoreType.DMA((cols // block,)),
            pltpu.SemaphoreType.DMA((COPIES,)),
        ],
        input_output_aliases={4 + len(received): 0},
        compiler_params=LARGE,
        cost_estimate=FREE,
        name="finish_rows",
    )(place, matrix, swapped, upper, *received, out)


def swap_pairs(size, orders, step):
    return [(i, i ^ (1 << orders[i & 1][step])) for i in range(size)]


def grow_pairs(orders, step):
    pairs = []
    for core, order in enumerate(orders):
        places = [core]
        for bit in order[:step]:
            places += [i | (1 << bit) for i in places]
        pairs += [(i, i | (1 << order[step])) for i in places]
    return pairs


def move(value, pairs, core, n_prow, size):
    pairs = [(row * size + a, row * size + b) for row in range(core, n_prow, 2) for a, b in pairs]
    return lax.ppermute(value, ("prow", "pcol"), pairs)


def send(place, matrix, width, groups, core, n_prow, size):
    middle = size // 2
    held = []
    for number, group in enumerate(groups):
        last = held[-1] if held else None
        sent = chunk(place, 1, core, matrix, *group, width, last, CHUNK_WEIGHTS[number])
        if held:
            held[-1] = sent
        pairs = [(0, middle)] + [(middle, middle - 1)] * bool(held[:1])
        held.append(move(sent, pairs, core, n_prow, size))
    return held


def pass_on(place, held, rights, core, n_prow, size):
    middle = size // 2
    last = move(held[-1], [(middle, middle - 1)], core, n_prow, size)
    received = []
    for number, value in enumerate(held):
        left = held[number + 1] if number + 1 < len(held) else last
        right = rights[number] if number < len(rights) else None
        if right is None:
            right = move(value, [(middle, middle + 1)], core, n_prow, size)
        arrays = [value, right, left]
        both = jnp.where(place[1] < middle, left, right) if size > 4 else None
        distance = 1
        while middle - distance > 1 or middle + distance + 1 < size:
            pairs = []
            if middle - distance > 1:
                pairs.append((middle - distance, middle - distance - 1))
            if middle + distance + 1 < size:
                pairs.append((middle + distance, middle + distance + 1))
            both = move(both, pairs, core, n_prow, size)
            arrays.append(both)
            distance += 1
        received.append(arrays)
    return received


def source_of(size, per_core):
    middle = size // 2

    def pick_source(place, core):
        away = jnp.abs(place - middle)
        number = jnp.where(away == 0, 1, jnp.where(place < middle, 3, 2))
        number = jnp.where(away >= 2, away + 2, number)
        return jnp.where(place == 0, 0, number + core * per_core)

    return pick_source


def per_device(n_prow, n_pcol, matrix, pivots, unit_inverse):
    rows, cols = matrix.shape
    width = unit_inverse.shape[0]
    half = width // 2
    row_place = lax.axis_index("prow")
    col_place = lax.axis_index("pcol")
    core = row_place & 1
    place = jnp.stack([row_place, col_place, core, jnp.full_like(core, rows)]).astype(jnp.int32)
    matrix = pltpu.with_memory_space_constraint(matrix, pltpu.HBM)
    bits = list(range(1, n_prow.bit_length() - 1))
    orders = (bits, bits[::-1])
    cores = ([0], [0])
    last = len(bits) - 1

    size = rows // GROUPS
    groups = [(number * size, size) for number in range(GROUPS)]
    held = [send(place, matrix, width, groups, c, n_prow, n_pcol) for c in range(2)]
    arrived = [x for pair in zip(*held) for x in pair]
    middle = n_pcol // 2
    rights = [
        [move(x, [(middle, middle + 1)], c, n_prow, n_pcol) for x in held[c][: GROUPS - c]]
        for c in range(2)
    ]
    arrived_right = [rights[0][0], rights[1][0]] + rights[0][1:]

    order = jnp.where(core == 0, pivots, jnp.roll(pivots, half))
    down_got = lax.ppermute(chunk(place, 0, 0, matrix, half, half, cols), "prow", [(0, 1)])
    down = chunk(place, 0, 0, matrix, 0, half, cols, down_got)
    pieces = pick(place, order, matrix, [])
    up, sent = pieces[: PIECES // 2], pieces[PIECES // 2 :]
    up_got = [lax.ppermute(x, "prow", swap_pairs(n_prow, cores, 0)) for x in sent]
    def pins(a, b):
        return arrived[max(a - 2, 0):a] + arrived_right[max(b - 2, 0):b]
    for step in range(last + 1):
        up = [add(up, up_got, pins(*JOIN_AFTER[min(step, 1)]), JOIN_WEIGHTS[min(step, 1)])]
        down_got = lax.ppermute(down, "prow", grow_pairs(orders, step))
        up_got = [lax.ppermute(up[0], "prow", swap_pairs(n_prow, orders, step))]
        down = add([down], [down_got], [] + pins(*DOWN_AFTER[min(step, 1)]), DOWN_WEIGHTS[min(step, 1)])
    down_got = lax.ppermute(down, "prow", swap_pairs(n_prow, cores, 0))
    up = add(up, up_got, pins(0, 0), 0)
    up_got = lax.ppermute(up, "prow", swap_pairs(n_prow, cores, 0))

    by_core = [pass_on(place, held[c], rights[c], c, n_prow, n_pcol) for c in range(2)]
    received = [first + second for first, second in zip(*by_core)]
    common = (source_of(n_pcol, len(by_core[0][0])), place, pivots, matrix, down, down_got)
    out, upper = update(groups[0], *common, received[0], upper_terms=(unit_inverse, up, up_got))
    for group, arrays in zip(groups[1:-1], received[1:-1]):
        (out,) = update(group, *common, arrays, upper=upper, out=out)
    swapped = swap(groups[-1], *common[1:])
    return finish(
        groups[-1], common[0], place, matrix, swapped, upper, received[-1], out
    )


def solution(mesh):
    return jax.shard_map(
        functools.partial(per_device, mesh.shape["prow"], mesh.shape["pcol"]),
        mesh=mesh,
        in_specs=(P("prow", "pcol"), P(), P()),
        out_specs=P("prow", "pcol"),
        check_vma=False,
    )
```
